256 devices in a mesh: lon: 32 (over z_lo, y, core), lat: 8 (over x, z_hi).
Axes of the slice: x: 4, y: 4, z: 8 (z_hi: 2, z_lo: 4; z = z_hi * 4 + z_lo), core: 2. Of those that a mesh axis runs over, the one named last changes fastest.
Arguments:
- field: float32 [2, 1536, 768, 128], P(None, 'lon', 'lat'), may hold values from -6 to 6
- lat_factor: float32 [768, 96], P('lat'), may hold values from -0.21875 to 0.21875
- lev_factor: float32 [128, 32], replicated, may hold values from -0.5 to 0.5
- old_factor: float32 [1536, 96], P('lon'), may hold values from -0.15625 to 0.15625
Outputs:
- new_factor: float32 [1536, 96], P('lon')
The draws below stay inside these ranges and needn't reach their ends.
All inputs are finite; a program needn't handle non-finite values.
Results may differ from the reference program's by a relative error of at most 0.0003.
Values sent between devices are 32-bit elements; how exact they have to be, the bound alone decides.
A program may use at most 64 MiB of HBM per device.

```python
import jax
import jax.numpy as jnp
from jax import lax

R_LAT = 96
R_LEV = 32
R_LON = 96
LEV = 128
TIMES = 2
NLON = 1536
NLAT = 768


def block_levels(rng, shape, split, smallest, largest):
    def one(dim, shards_of):
        heights = jax.random.uniform(jax.random.fold_in(jax.random.fold_in(rng, 6), dim), (shards_of,), jnp.float32, smallest / len(split), largest / len(split))
        return jnp.repeat(jnp.exp(heights), shape[dim] // shards_of).reshape((-1,) + (1,) * (len(shape) - dim - 1))

    gain = one(*split[0])
    for cut in split[1:]:
        gain = gain * one(*cut)
    return gain


def scatter_about(rng, dims, width, bound, shards=(), kind=jnp.bfloat16):
    factor_of = block_levels(rng, dims, shards, -0.22, 0.18) if shards else 1.0
    entries = jax.random.normal(rng, dims, jnp.float32) * width * factor_of
    return jnp.minimum(jnp.maximum(entries, -bound), bound).astype(kind)


def setup_inputs(seed: int = 0) -> dict:
    key_list = jax.random.split(jax.random.key(seed), 5)
    return {
        "field": scatter_about(key_list[0], (TIMES, NLON, NLAT, LEV), 1.0, 6.0, ((1, 32), (2, 8)), jnp.float32),
        "lat_factor": scatter_about(key_list[1], (NLAT, R_LAT), NLAT ** -0.5, 0.21875, ((0, 8),), jnp.float32),
        "lev_factor": scatter_about(key_list[2], (LEV, R_LEV), LEV ** -0.5, 0.5, (), jnp.float32),
        "old_factor": scatter_about(key_list[3], (NLON, R_LON), NLON ** -0.5, 0.15625, ((0, 32),), jnp.float32),
    }


HIGH = lax.Precision.HIGHEST

def project_one(snap, lat_factor, lev_factor):
    levels = jnp.einsum('ijg,gs->ijs', snap, lev_factor, precision=HIGH)
    both = jnp.einsum('ijs,ja->ias', levels, lat_factor, precision=HIGH)
    return both.reshape(snap.shape[0], -1)

def reference(field, lat_factor, lev_factor, old_factor):
    projected = lax.map(lambda snap: project_one(snap, lat_factor, lev_factor), field)
    weights = jnp.einsum('tik,ir->tkr', projected, old_factor, precision=HIGH)
    image = jnp.einsum('tik,tkr->ir', projected, weights, precision=HIGH)
    gram = jnp.dot(image.T, image, precision=HIGH)
    chol = jnp.linalg.cholesky(gram)
    solved = jax.scipy.linalg.solve_triangular(chol, image.T, lower=True)
    return solved.T * jnp.sqrt(jnp.float32(NLON))
```

```python
import functools

import jax
import jax.numpy as jnp
from jax import lax
from jax.experimental import pallas as pl
from jax.experimental.pallas import tpu as pltpu
from jax.sharding import PartitionSpec as P

MESH = pl.DeviceIdType.MESH
HIGHEST = lax.Precision.HIGHEST
F32, BF16 = jnp.float32, jnp.bfloat16
TIMES, ROWS, LATS, LEVS = 2, 48, 96, 128
RLAT, RLEV, RLON = 96, 32, 96
SLABS = 3
OWNERS = 12
GROUP = 32


def split(v):
    hi = v.astype(BF16)
    return hi, (v - hi.astype(F32)).astype(BF16)


def place():
    lon, lat = lax.axis_index("lon"), lax.axis_index("lat")
    return lat // 2, (lat % 2) * 4 + lon // 8, (lon // 2) % 4, lon % 2


def device(x, z, y, core):
    return (z % 4) * 8 + y * 2 + core, x * 2 + z // 4


def contract_lanes(a, b):
    return lax.dot_general(a, b, (((1,), (1,)), ((), ())), precision=HIGHEST, preferred_element_type=F32)


def gather_kernel(
    field, lat, lev, old, gram_out, image_out,
    fv, lats, lvl, proj, xr, zsrc, zr, pz, oldr, wt, wr, ws, wf, img, ir, gp, gr, gs, gf,
    fsem, xsend, xrecv, zsend, zrecv, osem, wsend, wrecv, asend, arecv, isem, gsem,
):
    x, z, y, core = place()
    slice_ = ((z + 6) % 8) // 4
    gz = (z + 6) % 4
    member = gz * 8 + y * 2 + core
    own = y * 4 + gz

    def in_group(m):
        return device(x, (2 + 4 * slice_ + m // 8) % 8, (m // 2) % 4, m % 2)

    def owner_member(o, kind):
        return (o % 4) * 8 + (o // 4) * 2 + kind

    def send(src, dst, ssem, rsem, to):
        return pltpu.make_async_remote_copy(
            src_ref=src, dst_ref=dst, send_sem=ssem, recv_sem=rsem, device_id=to, device_id_type=MESH
        )

    def arrived(ref, sem):
        pltpu.make_async_copy(ref, ref, sem).wait()

    barrier = pltpu.get_barrier_semaphore()
    for dx in (1, 2, 3):
        pl.semaphore_signal(barrier, inc=1, device_id=device((x + dx) % 4, z, y, core), device_id_type=MESH)
    for dx in range(4):
        for dz in (2, 6):
            pl.semaphore_signal(
                barrier, inc=1, device_id=device((x + dx) % 4, (z + dz) % 8, y, core), device_id_type=MESH
            )

    def greet(j, c):
        pl.semaphore_signal(barrier, inc=1, device_id=in_group((member + j) % GROUP), device_id_type=MESH)
        return c

    lax.fori_loop(1, GROUP, greet, 0)

    chunk = 16 * LATS
    loads = [
        pltpu.make_async_copy(field.at[pl.ds(k * chunk, chunk)], fv.at[pl.ds(k * chunk, chunk)], fsem.at[k])
        for k in range(6)
    ]
    for load in loads:
        load.start()

    levh, levl = split(lev[...].T)
    lev2 = jnp.concatenate(
        [jnp.concatenate([levh, levh], 1), jnp.concatenate([levl, jnp.zeros_like(levl)], 1)], 0
    )
    lats[...] = jnp.zeros_like(lats)
    lats[0:LATS, 0:RLAT] = lat[...]
    lat_pad = lats[...]
    lane = lax.broadcasted_iota(jnp.int32, (128, 128), 1)
    lat_hi, lat_lo = [], []
    for u in range(SLABS):
        tail = jnp.where(lane >= RLAT, pltpu.roll(lat_pad, 96 - 32 * u, 1), 0.0)
        hi, lo = split(jnp.concatenate([lat_pad, tail], 0))
        lat_hi.append(hi)
        lat_lo.append(lo)

    xcopies = []
    for t in range(TIMES):
        for c in range(3):
            loads[3 * t + c].wait()

            def levels(i, carry, t=t):
                f = fv[pl.ds(pl.multiple_of((t * ROWS + i) * LATS, LATS), LATS), :]
                fh, fl = split(f)
                both = jnp.concatenate([fh, fl], 1)
                both = jnp.concatenate([both, jnp.zeros((128 - LATS, 256), BF16)], 0)
                r = lax.dot_general(lev2, both, (((1,), (1,)), ((), ())), preferred_element_type=F32)
                lvl[pl.ds(i, RLEV, stride=ROWS), :] = r[:RLEV] + r[RLEV:]
                return carry

            lax.fori_loop(16 * c, 16 * c + 16, levels, 0, unroll=4)
        for u in range(SLABS):
            parts = [
                jnp.concatenate([lvl[pl.ds((4 * d + v) * ROWS, ROWS), :] for d in range(8)], 0) for v in (u, 3)
            ]
            hi, lo = split(jnp.concatenate(parts, 1))
            r = (
                jnp.dot(hi, lat_hi[u], preferred_element_type=F32)
                + jnp.dot(lo, lat_hi[u], preferred_element_type=F32)
                + jnp.dot(hi, lat_lo[u], preferred_element_type=F32)
            )
            for d in range(8):
                proj[t, d, u] = r[d * ROWS : (d + 1) * ROWS]
        if t == 0:
            pl.semaphore_wait(barrier, 3 + 8 + GROUP - 1)
            oldcopy = send(old, oldr, osem.at[0], osem.at[1], device(x, (z + 2) % 8, y, core))
            oldcopy.start()
        row = []
        for dx in (1, 2, 3):
            to = (x + dx) % 4
            copy = send(
                proj.at[t, pl.ds(2 * to, 2)], xr.at[t, dx - 1], xsend.at[t, dx - 1], xrecv.at[t, dx - 1],
                device(to, z, y, core),
            )
            copy.start()
            row.append(copy)
        xcopies.append(row)

    up = z // 4
    zcopies = []
    for t in range(TIMES):
        for copy in xcopies[t]:
            copy.wait_recv()
        total = proj[t, pl.ds(2 * x, 2)] + xr[t, 0] + xr[t, 1] + xr[t, 2]
        zsrc[t] = total
        row = [
            send(zsrc.at[t, up], zr.at[t, 0], zsend.at[t, 0], zrecv.at[t, 0], device(x, (z + 2) % 8, y, core)),
            send(zsrc.at[t, 1 - up], zr.at[t, 1], zsend.at[t, 1], zrecv.at[t, 1], device(x, (z + 6) % 8, y, core)),
        ]
        for copy in row:
            copy.start()
        zcopies.append(row)

    def reduce_start(src, slots, kind, ssem, rsem):
        mine = jnp.logical_and(core == kind, y < 3)

        def one(j, c):
            o = (own + j) % OWNERS
            m = owner_member(o, kind)
            part = src.at[:, pl.ds(pl.multiple_of(8 * o, 8), 8), :]

            @pl.when(m != member)
            def _():
                send(part, slots.at[member], ssem, rsem, in_group(m)).start()

            @pl.when(m == member)
            def _():
                pltpu.make_async_copy(part, slots.at[member], rsem).start()

            return c

        lax.fori_loop(0, OWNERS, one, 0)
        return mine

    def reduce_finish(slots, summed, full, mine, rsem, ssem2, rsem2):
        @pl.when(mine)
        def _():
            arrived(slots, rsem)
            acc = slots[0]
            for k in range(1, GROUP):
                acc = acc + slots[k]
            summed[...] = acc
            here = full.at[:, pl.ds(pl.multiple_of(8 * own, 8), 8), :]
            pltpu.make_async_copy(summed, here, rsem2).start()

            def one(j, c):
                send(summed, here, ssem2, rsem2, in_group((member + j) % GROUP)).start()
                return c

            lax.fori_loop(1, GROUP, one, 0)

    def drain(src, slots, mine, ssem, ssem2):
        @pl.when(mine)
        def _():
            arrived(src.at[:, pl.ds(0, 88), :], ssem)
            arrived(slots.at[pl.ds(0, GROUP - 1)], ssem2)

        @pl.when(jnp.logical_not(mine))
        def _():
            arrived(src, ssem)

    oldcopy.wait_recv()
    old_t = oldr[...].T
    mines = []
    for t in range(TIMES):
        for copy in zcopies[t]:
            copy.wait_recv()
        pz[t] = zr[t, 0] + zr[t, 1]
        for u in range(SLABS):
            wt[t, u] = jnp.dot(old_t, pz[t, u], precision=HIGHEST, preferred_element_type=F32)
        mines.append(reduce_start(wt.at[t], wr.at[t], t, wsend.at[t], wrecv.at[t]))
    for t in range(TIMES):
        reduce_finish(wr.at[t], ws.at[t], wf.at[t], mines[t], wrecv.at[t], asend.at[t], arecv.at[t])
    acc = jnp.zeros((ROWS, RLON), F32)
    for t in range(TIMES):
        arrived(wf.at[t], arecv.at[t])
        for u in range(SLABS):
            acc = acc + contract_lanes(pz[t, u], wf[t, u])
    img[:, 0:RLON] = acc
    img[:, RLON:] = jnp.zeros((ROWS, 128 - RLON), F32)

    for dx in range(4):
        for k, dz in enumerate((2, 6)):
            send(
                img, ir.at[2 * dx + k], isem.at[0], isem.at[1], device((x + dx) % 4, (z + dz) % 8, y, core)
            ).start()
    arrived(ir, isem.at[1])
    image = ir[0]
    for k in range(1, 8):
        image = image + ir[k]
    image_out[...] = image
    gp[0] = lax.dot_general(
        image, image, (((0,), (0,)), ((), ())), precision=HIGHEST, preferred_element_type=F32
    )[0:RLON]
    mine = reduce_start(gp, gr, 0, gsem.at[0], gsem.at[1])
    reduce_finish(gr, gs, gf, mine, gsem.at[1], gsem.at[2], gsem.at[3])
    arrived(gf, gsem.at[3])
    gram_out[...] = gf[0]

    oldcopy.wait_send()
    for row in xcopies + zcopies:
        for copy in row:
            copy.wait_send()
    for t in range(TIMES):
        drain(wt.at[t], wr.at[t], mines[t], wsend.at[t], asend.at[t])
    drain(gp, gr, mine, gsem.at[0], gsem.at[2])
    arrived(ir, isem.at[0])


BLOCK = 8


def solve_kernel(total_rows, gram, image, out, uref):
    image_t = image[...].T[0:RLON]
    right = jnp.concatenate([image_t, jnp.zeros((RLON, 128 - ROWS), F32)], 1)
    uref[...] = jnp.zeros_like(uref)
    sub = lax.broadcasted_iota(jnp.int32, (BLOCK, 256), 0)
    for j in range(RLON // BLOCK):
        at = BLOCK * j
        panel = jnp.concatenate([gram[at : at + BLOCK, :], right[at : at + BLOCK, :]], 1)
        if j:
            above = uref[0:at, :]
            panel = panel - lax.dot_general(
                above[:, at : at + BLOCK], above, (((0,), (0,)), ((), ())), precision=HIGHEST,
                preferred_element_type=F32,
            )
        col = [jnp.broadcast_to(panel[:, at + q : at + q + 1], (BLOCK, 128)) for q in range(BLOCK)]
        d = [[None] * BLOCK for _ in range(BLOCK)]
        for q in range(BLOCK):
            for p in range(q + 1):
                d[q][p] = jnp.broadcast_to(col[p][q : q + 1, :], (BLOCK, 128))
        inv = []
        for p in range(BLOCK):
            inv.append(lax.rsqrt(d[p][p]))
            for q in range(p + 1, BLOCK):
                d[q][p] = d[q][p] * inv[p]
            for q in range(p + 1, BLOCK):
                for r in range(p + 1, q + 1):
                    d[q][r] = d[q][r] - d[q][p] * d[r][p]
        wide = lambda v: jnp.concatenate([v, v], 1)
        rows = []
        for p in range(BLOCK):
            v = jnp.broadcast_to(panel[p : p + 1, :], (BLOCK, 256))
            for q in range(p):
                v = v - wide(d[p][q]) * rows[q]
            rows.append(v * wide(inv[p]))
        block = rows[0]
        for p in range(1, BLOCK):
            block = jnp.where(sub == p, rows[p], block)
        uref[at : at + BLOCK, :] = block
    y = uref[:, 128:256].T
    out[...] = y[0:ROWS, :] * jnp.sqrt(F32(total_rows))


def body(field, lat_factor, lev_factor, old_factor):
    vmem = pl.BlockSpec(memory_space=pltpu.VMEM)
    dma = pltpu.SemaphoreType.DMA
    field = field.reshape(TIMES * ROWS * LATS, LEVS)
    total_rows = ROWS * lax.axis_size("lon")
    gram, image = pl.pallas_call(
        gather_kernel,
        out_shape=(jax.ShapeDtypeStruct((RLON, 128), F32), jax.ShapeDtypeStruct((ROWS, 128), F32)),
        in_specs=[pl.BlockSpec(memory_space=pl.ANY), vmem, vmem, vmem],
        out_specs=(vmem, vmem),
        scratch_shapes=[
            pltpu.VMEM((TIMES * ROWS * LATS, LEVS), F32),
            pltpu.VMEM((128, 128), F32),
            pltpu.VMEM((RLEV * ROWS, 128), F32),
            pltpu.VMEM((TIMES, 8, SLABS, ROWS, 128), F32),
            pltpu.VMEM((TIMES, 3, 2, SLABS, ROWS, 128), F32),
            pltpu.VMEM((TIMES, 2, SLABS, ROWS, 128), F32),
            pltpu.VMEM((TIMES, 2, SLABS, ROWS, 128), F32),
            pltpu.VMEM((TIMES, SLABS, ROWS, 128), F32),
            pltpu.VMEM((ROWS, RLON), F32),
            pltpu.VMEM((TIMES, SLABS, RLON, 128), F32),
            pltpu.VMEM((TIMES, GROUP, SLABS, 8, 128), F32),
            pltpu.VMEM((TIMES, SLABS, 8, 128), F32),
            pltpu.VMEM((TIMES, SLABS, RLON, 128), F32),
            pltpu.VMEM((ROWS, 128), F32),
            pltpu.VMEM((8, ROWS, 128), F32),
            pltpu.VMEM((1, RLON, 128), F32),
            pltpu.VMEM((GROUP, 1, 8, 128), F32),
            pltpu.VMEM((1, 8, 128), F32),
            pltpu.VMEM((1, RLON, 128), F32),
            dma((6,)),
            dma((TIMES, 3)),
            dma((TIMES, 3)),
            dma((TIMES, 2)),
            dma((TIMES, 2)),
            dma((2,)),
            dma((TIMES,)),
            dma((TIMES,)),
            dma((TIMES,)),
            dma((TIMES,)),
            dma((2,)),
            dma((4,)),
        ],
        compiler_params=pltpu.CompilerParams(
            collective_id=0, has_side_effects=True, vmem_limit_bytes=32 * 1024 * 1024
        ),
    )(field, lat_factor, lev_factor, old_factor)
    return pl.pallas_call(
        functools.partial(solve_kernel, total_rows),
        out_shape=jax.ShapeDtypeStruct((ROWS, RLON), F32),
        in_specs=[vmem, vmem],
        out_specs=vmem,
        scratch_shapes=[pltpu.VMEM((RLON, 256), F32)],
    )(gram, image)


def solution(mesh):
    placed = (P(None, "lon", "lat", None), P("lat", None), P(), P("lon", None))
    return jax.shard_map(
        body, mesh=mesh, in_specs=placed, out_specs=P("lon", None), check_vma=False
    )
```

```python
import functools

import jax
import jax.numpy as jnp
from jax import lax
from jax.experimental import pallas as pl
from jax.experimental.pallas import tpu as pltpu
from jax.sharding import PartitionSpec as P

MESH = pl.DeviceIdType.MESH
HIGHEST = lax.Precision.HIGHEST
F32, BF16 = jnp.float32, jnp.bfloat16
TIMES, ROWS, LATS, LEVS = 2, 48, 96, 128
RLAT, RLEV, RLON = 96, 32, 96
SLABS = 3
BLOCKS = TIMES * SLABS
PART = 2 * RLON // 8
SCHEDULE = sorted((b + lag, kind, b) for b in range(BLOCKS) for kind, lag in enumerate((0, 2.6, 6.2, 8.8)))


def split(v):
    hi = v.astype(BF16)
    return hi, (v - hi.astype(F32)).astype(BF16)


def place():
    lon, lat = lax.axis_index("lon"), lax.axis_index("lat")
    return lat // 2, (lat % 2) * 4 + lon // 8, (lon // 2) % 4, lon % 2


def device(x, z, y, core):
    return (z % 4) * 8 + y * 2 + core, x * 2 + z // 4


def contract_lanes(a, b):
    return lax.dot_general(a, b, (((1,), (1,)), ((), ())), precision=HIGHEST, preferred_element_type=F32)


BLOCK = 8


def solve(total_rows, gram, image, out, uref):
    image_t = image[...].T[0:RLON]
    right = jnp.concatenate([image_t, jnp.zeros((RLON, 128 - ROWS), F32)], 1)
    uref[...] = jnp.zeros_like(uref)
    sub = lax.broadcasted_iota(jnp.int32, (BLOCK, 256), 0)
    for j in range(RLON // BLOCK):
        at = BLOCK * j
        panel = jnp.concatenate([gram[at : at + BLOCK, :], right[at : at + BLOCK, :]], 1)
        if j:
            above = uref[0:at, :]
            panel = panel - lax.dot_general(
                above[:, at : at + BLOCK], above, (((0,), (0,)), ((), ())), precision=HIGHEST,
                preferred_element_type=F32,
            )
        col = [jnp.broadcast_to(panel[:, at + q : at + q + 1], (BLOCK, 128)) for q in range(BLOCK)]
        d = [[None] * BLOCK for _ in range(BLOCK)]
        for q in range(BLOCK):
            for p in range(q + 1):
                d[q][p] = jnp.broadcast_to(col[p][q : q + 1, :], (BLOCK, 128))
        inv = []
        for p in range(BLOCK):
            inv.append(lax.rsqrt(d[p][p]))
            for q in range(p + 1, BLOCK):
                d[q][p] = d[q][p] * inv[p]
            for q in range(p + 1, BLOCK):
                for r in range(p + 1, q + 1):
                    d[q][r] = d[q][r] - d[q][p] * d[r][p]
        wide = lambda v: jnp.concatenate([v, v], 1)
        rows = []
        for p in range(BLOCK):
            v = jnp.broadcast_to(panel[p : p + 1, :], (BLOCK, 256))
            for q in range(p):
                v = v - wide(d[p][q]) * rows[q]
            rows.append(v * wide(inv[p]))
        block = rows[0]
        for p in range(1, BLOCK):
            block = jnp.where(sub == p, rows[p], block)
        uref[at : at + BLOCK, :] = block
    y = uref[:, 128:256].T
    out[...] = y[0:ROWS, :] * jnp.sqrt(F32(total_rows))


def hooi_kernel(
    total_rows, field, lat, lev_t, old, out,
    fv, lat_in, lev_in, old_in, lats, lvl, proj, xr, pz, wt, wr, ws, wz, wf, img, ir, summed, home, gp, gr, gh, go, gf,
    uref, fsem, csem, xsem, rsem, zsem, asem, isem, hsem, gsem,
):
    x, z, y, core = place()
    me = y * 2 + core

    def send(src, dst, sems, to):
        copy = pltpu.make_async_remote_copy(
            src_ref=src, dst_ref=dst, send_sem=sems.at[0], recv_sem=sems.at[1], device_id=to, device_id_type=MESH
        )
        copy.start()
        return copy

    def arrived(ref, sem):
        pltpu.make_async_copy(ref, ref, sem).wait()

    chunk = 16 * LATS
    loads = [
        pltpu.make_async_copy(field.at[pl.ds(k * chunk, chunk)], fv.at[pl.ds(k * chunk, chunk)], fsem.at[k])
        for k in range(6)
    ]
    small = [
        pltpu.make_async_copy(src, dst, csem.at[k])
        for k, (src, dst) in enumerate(((lev_t, lev_in), (lat, lat_in), (old, old_in)))
    ]
    for load in small + loads:
        load.start()

    x_peers = [device((x + dx) % 4, z, y, core) for dx in (1, 2, 3)]
    z_peers = [device(x, (z + dz) % 8, y, core) for dz in range(1, 8)]
    yc_peers = [device(x, z, ((me + j) % 8) // 2, (me + j) % 2) for j in range(1, 8)]
    i_peers = [device((x + dx) % 4, (z + dz) % 8, y, core) for dx in range(4) for dz in (2, 6)]
    g_steps = [(dy, dz) for dy in range(4) for dz in (0, 1, 7, 2 if dy < 2 else 6)][1:]
    g_peers = [device(x, (z + dz) % 8, (y + dy) % 4, core) for dy, dz in g_steps]
    also = [device(x, (z + 2) % 8, (y + 2) % 4, core)]
    greeted = x_peers + z_peers + yc_peers + i_peers[2:] + [
        peer for (dy, dz), peer in zip(g_steps, g_peers) if dy and dz
    ] + also
    barrier = pltpu.get_barrier_semaphore()
    for peer in greeted:
        pl.semaphore_signal(barrier, inc=1, device_id=peer, device_id_type=MESH)

    small[0].wait()
    small[1].wait()
    levh, levl = split(lev_in[...])
    lev2 = jnp.concatenate(
        [jnp.concatenate([levh, levh], 1), jnp.concatenate([levl, jnp.zeros_like(levl)], 1)], 0
    )
    lats[...] = jnp.zeros_like(lats)
    lats[0:LATS, 0:RLAT] = lat_in[...]
    lat_pad = lats[...]
    lane = lax.broadcasted_iota(jnp.int32, (128, 128), 1)
    lat_hi, lat_lo = [], []
    for u in range(SLABS):
        tail = jnp.where(lane >= RLAT, pltpu.roll(lat_pad, 96 - 32 * u, 1), 0.0)
        hi, lo = split(jnp.concatenate([lat_pad, tail], 0))
        lat_hi.append(hi)
        lat_lo.append(lo)

    xcopies = []
    for t in range(TIMES):
        for c in range(3):
            loads[3 * t + c].wait()

            def levels(i, carry, t=t):
                f = fv[pl.ds(pl.multiple_of((t * ROWS + i) * LATS, LATS), LATS), :]
                fh, fl = split(f)
                both = jnp.concatenate([fh, fl], 1)
                both = jnp.concatenate([both, jnp.zeros((128 - LATS, 256), BF16)], 0)
                r = lax.dot_general(lev2, both, (((1,), (1,)), ((), ())), preferred_element_type=F32)
                lvl[pl.ds(i, RLEV, stride=ROWS), :] = r[:RLEV] + r[RLEV:]
                return carry

            lax.fori_loop(16 * c, 16 * c + 16, levels, 0, unroll=4)
        for u in range(SLABS):
            parts = [
                jnp.concatenate([lvl[pl.ds((4 * d + v) * ROWS, ROWS), :] for d in range(8)], 0) for v in (u, 3)
            ]
            hi, lo = split(jnp.concatenate(parts, 1))
            r = (
                jnp.dot(hi, lat_hi[u], preferred_element_type=F32)
                + jnp.dot(lo, lat_hi[u], preferred_element_type=F32)
                + jnp.dot(hi, lat_lo[u], preferred_element_type=F32)
            )
            b = t * SLABS + u
            for d in range(8):
                proj[b, d // 2, d % 2] = r[d * ROWS : (d + 1) * ROWS]
            if b == 0:
                pl.semaphore_wait(barrier, len(greeted))
            xcopies.append(
                [send(proj.at[b, (x + k + 1) % 4], xr.at[b, k], xsem.at[b, k], x_peers[k]) for k in range(3)]
            )

    small[2].wait()
    old_t = old_in[...].T
    acc = jnp.zeros((ROWS, RLON), F32)

    for at, kind, b in SCHEDULE:
        if kind == 0:
            for copy in xcopies[b]:
                copy.wait_recv()
            pz[b] = proj[b, x] + xr[b, 0] + xr[b, 1] + xr[b, 2]
            for s in range(2):
                wt[b, s * RLON : (s + 1) * RLON] = jnp.dot(
                    old_t, pz[b, s], precision=HIGHEST, preferred_element_type=F32
                )
            for k in range(7):
                part = wt.at[b, pl.ds(pl.multiple_of(PART * ((me + k + 1) % 8), 8), PART)]
                send(part, wr.at[b, k], rsem.at[b], yc_peers[k])
        elif kind == 1:
            arrived(wr.at[b], rsem.at[b, 1])
            part = wt[b, pl.ds(pl.multiple_of(PART * me, 8), PART)]
            for k in range(7):
                part = part + wr[b, k]
            ws[b, 0] = part
            for k in range(7):
                send(ws.at[b, 0], wz.at[b, k], zsem.at[b], z_peers[k])
        elif kind == 2:
            arrived(wz.at[b], zsem.at[b, 1])
            part = ws[b, 0]
            for k in range(7):
                part = part + wz[b, k]
            mine = pl.ds(pl.multiple_of(PART * me, 8), PART)
            wf[b, mine] = part
            for k in range(7):
                send(wf.at[b, mine], wf.at[b, mine], asem.at[b], yc_peers[k])
        else:
            arrived(wr.at[b], asem.at[b, 1])
            for s in range(2):
                acc = acc + contract_lanes(pz[b, s], wf[b, s * RLON : (s + 1) * RLON])
    img[:, 0:RLON] = acc
    img[:, RLON:] = jnp.zeros((ROWS, 128 - RLON), F32)
    for k in range(8):
        send(img, ir.at[k], isem, i_peers[k])
    arrived(ir, isem.at[1])
    image = ir[0]
    for k in range(1, 8):
        image = image + ir[k]
    summed[...] = image
    back = send(summed, home, hsem, z_peers[1])
    gp[...] = lax.dot_general(
        image, image, (((0,), (0,)), ((), ())), precision=HIGHEST, preferred_element_type=F32
    )[0:RLON]
    half = RLON // 2
    sibling = device(x, z, y, 1 - core)
    mine, other = (pl.ds(pl.multiple_of(half * c, 8), half) for c in (core, 1 - core))
    first = send(gp.at[other], gr, gsem.at[0], sibling)
    first.wait_recv()
    gh[...] = gp[mine] + gr[...]
    for k in range(15):
        send(gh, go.at[k], gsem.at[1], g_peers[k])
    arrived(go, gsem.at[1, 1])
    total = gh[...]
    for k in range(15):
        total = total + go[k]
    gf[mine] = total
    last = send(gf.at[mine], gf.at[mine], gsem.at[2], sibling)
    last.wait_recv()
    back.wait_recv()
    solve(total_rows, gf, home, out, uref)

    for row in xcopies:
        for copy in row:
            copy.wait_send()
    for b in range(BLOCKS):
        arrived(wr.at[b], rsem.at[b, 0])
        arrived(wz.at[b], zsem.at[b, 0])
        arrived(wr.at[b], asem.at[b, 0])
    arrived(ir, isem.at[0])
    back.wait_send()
    first.wait_send()
    arrived(go, gsem.at[1, 0])
    last.wait_send()


def body(field, lat_factor, lev_factor, old_factor):
    vmem = pl.BlockSpec(memory_space=pltpu.VMEM)
    dma = pltpu.SemaphoreType.DMA
    field = field.reshape(TIMES * ROWS * LATS, LEVS)
    total_rows = ROWS * lax.axis_size("lon")
    return pl.pallas_call(
        functools.partial(hooi_kernel, total_rows),
        out_shape=jax.ShapeDtypeStruct((ROWS, RLON), F32),
        in_specs=[pl.BlockSpec(memory_space=pltpu.HBM)] * 4,
        out_specs=vmem,
        scratch_shapes=[
            pltpu.VMEM((TIMES * ROWS * LATS, LEVS), F32),
            pltpu.VMEM((LATS, RLAT), F32),
            pltpu.VMEM((RLEV, LEVS), F32),
            pltpu.VMEM((ROWS, RLON), F32),
            pltpu.VMEM((128, 128), F32),
            pltpu.VMEM((RLEV * ROWS, 128), F32),
            pltpu.VMEM((BLOCKS, 4, 2, ROWS, 128), F32),
            pltpu.VMEM((BLOCKS, 3, 2, ROWS, 128), F32),
            pltpu.VMEM((BLOCKS, 2, ROWS, 128), F32),
            pltpu.VMEM((BLOCKS, 2 * RLON, 128), F32),
            pltpu.VMEM((BLOCKS, 7, PART, 128), F32),
            pltpu.VMEM((BLOCKS, 1, PART, 128), F32),
            pltpu.VMEM((BLOCKS, 7, PART, 128), F32),
            pltpu.VMEM((BLOCKS, 2 * RLON, 128), F32),
            pltpu.VMEM((ROWS, 128), F32),
            pltpu.VMEM((8, ROWS, 128), F32),
            pltpu.VMEM((ROWS, 128), F32),
            pltpu.VMEM((ROWS, 128), F32),
            pltpu.VMEM((RLON, 128), F32),
            pltpu.VMEM((RLON // 2, 128), F32),
            pltpu.VMEM((RLON // 2, 128), F32),
            pltpu.VMEM((15, RLON // 2, 128), F32),
            pltpu.VMEM((RLON, 128), F32),
            pltpu.VMEM((RLON, 256), F32),
            dma((6,)),
            dma((3,)),
            dma((BLOCKS, 3, 2)),
            dma((BLOCKS, 2)),
            dma((BLOCKS, 2)),
            dma((BLOCKS, 2)),
            dma((2,)),
            dma((2,)),
            dma((3, 2)),
        ],
        compiler_params=pltpu.CompilerParams(
            collective_id=0, has_side_effects=True, vmem_limit_bytes=56 * 1024 * 1024
        ),
    )(field, lat_factor, lev_factor.T, old_factor)


def solution(mesh):
    placed = (P(None, "lon", "lat", None), P("lat", None), P(), P("lon", None))
    return jax.shard_map(
        body, mesh=mesh, in_specs=placed, out_specs=P("lon", None), check_vma=False
    )
```

```python
import functools

import jax
import jax.numpy as jnp
from jax import lax
from jax.experimental import pallas as pl
from jax.experimental.pallas import tpu as pltpu
from jax.sharding import PartitionSpec as P

MESH = pl.DeviceIdType.MESH
HIGHEST = lax.Precision.HIGHEST
F32, BF16 = jnp.float32, jnp.bfloat16
TIMES, ROWS, LATS, LEVS = 2, 48, 96, 128
RLAT, RLEV, RLON = 96, 32, 96
SLABS = 3
BLOCKS = TIMES * SLABS
PART = 2 * RLON // 8
SCHEDULE = sorted((b + lag, kind, b) for b in range(BLOCKS) for kind, lag in enumerate((0, 2.6, 6.2, 8.8)))


def split(v):
    hi = v.astype(BF16)
    return hi, (v - hi.astype(F32)).astype(BF16)


def place():
    lon, lat = lax.axis_index("lon"), lax.axis_index("lat")
    return lat // 2, (lat % 2) * 4 + lon // 8, (lon // 2) % 4, lon % 2


def device(x, z, y, core):
    return (z % 4) * 8 + y * 2 + core, x * 2 + z // 4


def contract_lanes(a, b):
    return lax.dot_general(a, b, (((1,), (1,)), ((), ())), precision=HIGHEST, preferred_element_type=F32)


PANEL = 16


def solve(total_rows, top, image_t, out, yt):
    tiles = RLON // 8
    left = [top[8 * r : 8 * r + 8] for r in range(tiles)]
    right = [image_t[8 * r : 8 * r + 8] for r in range(tiles)]
    sub = lax.broadcasted_iota(jnp.int32, (8, 128), 0)
    diagonal = lax.broadcasted_iota(jnp.int32, (8, 128), 1) - sub
    spread = lambda v: jnp.broadcast_to(v, (8, 128))
    for j in range(RLON // PANEL):
        at, first = PANEL * j, PANEL // 8 * j
        col = [
            [spread(left[first + s][:, at + q : at + q + 1]) if q >= 8 * s else None for q in range(PANEL)]
            for s in range(PANEL // 8)
        ]
        d = [[spread(col[p // 8][q][p % 8 : p % 8 + 1]) for p in range(q + 1)] for q in range(PANEL)]
        vl = [spread(left[first + p // 8][p % 8 : p % 8 + 1]) for p in range(PANEL)]
        vr = [spread(right[first + p // 8][p % 8 : p % 8 + 1]) for p in range(PANEL)]
        for p in range(PANEL):
            inv = lax.rsqrt(d[p][p])
            for q in range(p + 1, PANEL):
                d[q][p] = d[q][p] * inv
            for q in range(p + 1, PANEL):
                for r in range(p + 1, q + 1):
                    d[q][r] = d[q][r] - d[q][p] * d[r][p]
            vl[p], vr[p] = vl[p] * inv, vr[p] * inv
            for q in range(p + 1, PANEL):
                vl[q] = vl[q] - d[q][p] * vl[p]
                vr[q] = vr[q] - d[q][p] * vr[p]
        for s in range(PANEL // 8):
            rows = vr[8 * s]
            for p in range(1, 8):
                rows = jnp.where(sub == p, vr[8 * s + p], rows)
            yt[at + 8 * s : at + 8 * s + 8] = rows
        for r in range(first + PANEL // 8, tiles):
            ml, mr = [], []
            for p in range(PANEL):
                c = jnp.sum(jnp.where(diagonal == 8 * r, vl[p], 0.0), axis=1, keepdims=True)
                ml.append(c * vl[p])
                mr.append(c * vr[p])
            while len(ml) > 1:
                ml = [a + b for a, b in zip(ml[::2], ml[1::2])]
                mr = [a + b for a, b in zip(mr[::2], mr[1::2])]
            left[r], right[r] = left[r] - ml[0], right[r] - mr[0]
    out[...] = yt[...].T[0:ROWS] * jnp.sqrt(F32(total_rows))


def hooi_kernel(
    total_rows, field, lat, lev_t, old, out,
    fv, lat_in, lev_in, old_in, lats, lvl, proj, xr, pz, wt, wr, ws, wz, wf, img, ir, summed, home, gp, gr, gh, go, gf,
    yt, fsem, csem, xsem, rsem, zsem, asem, isem, hsem, gsem,
):
    x, z, y, core = place()
    me = y * 2 + core

    def send(src, dst, sems, to):
        copy = pltpu.make_async_remote_copy(
            src_ref=src, dst_ref=dst, send_sem=sems.at[0], recv_sem=sems.at[1], device_id=to, device_id_type=MESH
        )
        copy.start()
        return copy

    def arrived(ref, sem):
        pltpu.make_async_copy(ref, ref, sem).wait()

    chunk = 16 * LATS
    loads = [
        pltpu.make_async_copy(field.at[pl.ds(k * chunk, chunk)], fv.at[pl.ds(k * chunk, chunk)], fsem.at[k])
        for k in range(6)
    ]
    small = [
        pltpu.make_async_copy(src, dst, csem.at[k])
        for k, (src, dst) in enumerate(((lev_t, lev_in), (lat, lat_in), (old, old_in)))
    ]
    for load in small + loads:
        load.start()

    x_peers = [device((x + dx) % 4, z, y, core) for dx in (1, 2, 3)]
    z_peers = [device(x, (z + dz) % 8, y, core) for dz in range(1, 8)]
    yc_peers = [device(x, z, ((me + j) % 8) // 2, (me + j) % 2) for j in range(1, 8)]
    i_peers = [device((x + dx) % 4, (z + dz) % 8, y, core) for dx in range(4) for dz in (2, 6)]
    g_steps = [(dy, dz) for dy in range(4) for dz in (0, 1, 7, 2 if dy < 2 else 6)][1:]
    g_peers = [device(x, (z + dz) % 8, (y + dy) % 4, core) for dy, dz in g_steps]
    also = [device(x, (z + 2) % 8, (y + 2) % 4, core)]
    greeted = x_peers + z_peers + yc_peers + i_peers[2:] + [
        peer for (dy, dz), peer in zip(g_steps, g_peers) if dy and dz
    ] + also
    barrier = pltpu.get_barrier_semaphore()
    for peer in greeted:
        pl.semaphore_signal(barrier, inc=1, device_id=peer, device_id_type=MESH)

    small[0].wait()
    small[1].wait()
    levh, levl = split(lev_in[...])
    lev2 = jnp.concatenate(
        [jnp.concatenate([levh, levh], 1), jnp.concatenate([levl, jnp.zeros_like(levl)], 1)], 0
    )
    lats[...] = jnp.zeros_like(lats)
    lats[0:LATS, 0:RLAT] = lat_in[...]
    lat_pad = lats[...]
    lane = lax.broadcasted_iota(jnp.int32, (128, 128), 1)
    lat_hi, lat_lo = [], []
    for u in range(SLABS):
        tail = jnp.where(lane >= RLAT, pltpu.roll(lat_pad, 96 - 32 * u, 1), 0.0)
        hi, lo = split(jnp.concatenate([lat_pad, tail], 0))
        lat_hi.append(hi)
        lat_lo.append(lo)

    xcopies = []
    for t in range(TIMES):
        for c in range(3):
            loads[3 * t + c].wait()

            def levels(i, carry, t=t):
                f = fv[pl.ds(pl.multiple_of((t * ROWS + i) * LATS, LATS), LATS), :]
                fh, fl = split(f)
                both = jnp.concatenate([fh, fl], 1)
                both = jnp.concatenate([both, jnp.zeros((128 - LATS, 256), BF16)], 0)
                r = lax.dot_general(lev2, both, (((1,), (1,)), ((), ())), preferred_element_type=F32)
                lvl[pl.ds(i, RLEV, stride=ROWS), :] = r[:RLEV] + r[RLEV:]
                return carry

            lax.fori_loop(16 * c, 16 * c + 16, levels, 0, unroll=4)
        for u in range(SLABS):
            parts = [
                jnp.concatenate([lvl[pl.ds((4 * d + v) * ROWS, ROWS), :] for d in range(8)], 0) for v in (u, 3)
            ]
            hi, lo = split(jnp.concatenate(parts, 1))
            r = (
                jnp.dot(hi, lat_hi[u], preferred_element_type=F32)
                + jnp.dot(lo, lat_hi[u], preferred_element_type=F32)
                + jnp.dot(hi, lat_lo[u], preferred_element_type=F32)
            )
            b = t * SLABS + u
            for d in range(8):
                proj[b, d // 2, d % 2] = r[d * ROWS : (d + 1) * ROWS]
            if b == 0:
                pl.semaphore_wait(barrier, len(greeted))
            xcopies.append(
                [send(proj.at[b, (x + k + 1) % 4], xr.at[b, k], xsem.at[b, k], x_peers[k]) for k in range(3)]
            )

    small[2].wait()
    old_t = old_in[...].T
    acc = jnp.zeros((ROWS, RLON), F32)

    for at, kind, b in SCHEDULE:
        if kind == 0:
            for copy in xcopies[b]:
                copy.wait_recv()
            pz[b] = proj[b, x] + xr[b, 0] + xr[b, 1] + xr[b, 2]
            for s in range(2):
                wt[b, s * RLON : (s + 1) * RLON] = jnp.dot(
                    old_t, pz[b, s], precision=HIGHEST, preferred_element_type=F32
                )
            for k in range(7):
                part = wt.at[b, pl.ds(pl.multiple_of(PART * ((me + k + 1) % 8), 8), PART)]
                send(part, wr.at[b, k], rsem.at[b], yc_peers[k])
        elif kind == 1:
            arrived(wr.at[b], rsem.at[b, 1])
            part = wt[b, pl.ds(pl.multiple_of(PART * me, 8), PART)]
            for k in range(7):
                part = part + wr[b, k]
            ws[b, 0] = part
            for k in range(7):
                send(ws.at[b, 0], wz.at[b, k], zsem.at[b], z_peers[k])
        elif kind == 2:
            arrived(wz.at[b], zsem.at[b, 1])
            part = ws[b, 0]
            for k in range(7):
                part = part + wz[b, k]
            mine = pl.ds(pl.multiple_of(PART * me, 8), PART)
            wf[b, mine] = part
            for k in range(7):
                send(wf.at[b, mine], wf.at[b, mine], asem.at[b], yc_peers[k])
        else:
            arrived(wr.at[b], asem.at[b, 1])
            for s in range(2):
                acc = acc + contract_lanes(pz[b, s], wf[b, s * RLON : (s + 1) * RLON])
    img[:, 0:RLON] = acc
    img[:, RLON:] = jnp.zeros((ROWS, 128 - RLON), F32)
    for k in range(8):
        send(img, ir.at[k], isem, i_peers[k])
    arrived(ir, isem.at[1])
    image = ir[0]
    for k in range(1, 8):
        image = image + ir[k]
    summed[...] = image
    back = send(summed, home, hsem, z_peers[1])
    gp[...] = lax.dot_general(
        image, image, (((0,), (0,)), ((), ())), precision=HIGHEST, preferred_element_type=F32
    )[0:RLON]
    half = RLON // 2
    sibling = device(x, z, y, 1 - core)
    mine, other = (pl.ds(pl.multiple_of(half * c, 8), half) for c in (core, 1 - core))
    first = send(gp.at[other], gr, gsem.at[0], sibling)
    first.wait_recv()
    gh[...] = gp[mine] + gr[...]
    for k in range(15):
        send(gh, go.at[k], gsem.at[1], g_peers[k])
    arrived(go, gsem.at[1, 1])
    total = gh[...]
    for k in range(15):
        total = total + go[k]
    gf[mine] = total
    last = send(gf.at[mine], gf.at[mine], gsem.at[2], sibling)
    last.wait_recv()
    back.wait_recv()
    image_t = jnp.concatenate([home[...].T[0:RLON], jnp.zeros((RLON, 128 - ROWS), F32)], 1)
    solve(total_rows, gf[...], image_t, out, yt)

    for row in xcopies:
        for copy in row:
            copy.wait_send()
    for b in range(BLOCKS):
        arrived(wr.at[b], rsem.at[b, 0])
        arrived(wz.at[b], zsem.at[b, 0])
        arrived(wr.at[b], asem.at[b, 0])
    arrived(ir, isem.at[0])
    back.wait_send()
    first.wait_send()
    arrived(go, gsem.at[1, 0])
    last.wait_send()


def body(field, lat_factor, lev_factor, old_factor):
    vmem = pl.BlockSpec(memory_space=pltpu.VMEM)
    dma = pltpu.SemaphoreType.DMA
    field = field.reshape(TIMES * ROWS * LATS, LEVS)
    total_rows = ROWS * lax.axis_size("lon")
    return pl.pallas_call(
        functools.partial(hooi_kernel, total_rows),
        out_shape=pltpu.VMEM((ROWS, RLON), F32),
        in_specs=[pl.BlockSpec(memory_space=pltpu.HBM)] * 4,
        out_specs=vmem,
        scratch_shapes=[
            pltpu.VMEM((TIMES * ROWS * LATS, LEVS), F32),
            pltpu.VMEM((LATS, RLAT), F32),
            pltpu.VMEM((RLEV, LEVS), F32),
            pltpu.VMEM((ROWS, RLON), F32),
            pltpu.VMEM((128, 128), F32),
            pltpu.VMEM((RLEV * ROWS, 128), F32),
            pltpu.VMEM((BLOCKS, 4, 2, ROWS, 128), F32),
            pltpu.VMEM((BLOCKS, 3, 2, ROWS, 128), F32),
            pltpu.VMEM((BLOCKS, 2, ROWS, 128), F32),
            pltpu.VMEM((BLOCKS, 2 * RLON, 128), F32),
            pltpu.VMEM((BLOCKS, 7, PART, 128), F32),
            pltpu.VMEM((BLOCKS, 1, PART, 128), F32),
            pltpu.VMEM((BLOCKS, 7, PART, 128), F32),
            pltpu.VMEM((BLOCKS, 2 * RLON, 128), F32),
            pltpu.VMEM((ROWS, 128), F32),
            pltpu.VMEM((8, ROWS, 128), F32),
            pltpu.VMEM((ROWS, 128), F32),
            pltpu.VMEM((ROWS, 128), F32),
            pltpu.VMEM((RLON, 128), F32),
            pltpu.VMEM((RLON // 2, 128), F32),
            pltpu.VMEM((RLON // 2, 128), F32),
            pltpu.VMEM((15, RLON // 2, 128), F32),
            pltpu.VMEM((RLON, 128), F32),
            pltpu.VMEM((RLON, 128), F32),
            dma((6,)),
            dma((3,)),
            dma((BLOCKS, 3, 2)),
            dma((BLOCKS, 2)),
            dma((BLOCKS, 2)),
            dma((BLOCKS, 2)),
            dma((2,)),
            dma((2,)),
            dma((3, 2)),
        ],
        compiler_params=pltpu.CompilerParams(
            collective_id=0, has_side_effects=True, vmem_limit_bytes=48 * 1024 * 1024
        ),
    )(*(pltpu.with_memory_space_constraint(v, pltpu.HBM) for v in (field, lat_factor, lev_factor.T, old_factor)))


def solution(mesh):
    placed = (P(None, "lon", "lat", None), P("lat", None), P(), P("lon", None))
    return jax.shard_map(
        body, mesh=mesh, in_specs=placed, out_specs=P("lon", None), check_vma=False
    )
```

```python
import functools

import jax
import jax.numpy as jnp
from jax import lax
from jax.experimental import pallas as pl
from jax.experimental.pallas import tpu as pltpu
from jax.sharding import PartitionSpec as P

MESH = pl.DeviceIdType.MESH
HIGHEST = lax.Precision.HIGHEST
F32, BF16 = jnp.float32, jnp.bfloat16
TIMES, ROWS, LATS, LEVS = 2, 48, 96, 128
RLAT, RLEV, RLON = 96, 32, 96
SLABS = 3
BLOCKS = TIMES * SLABS
CHUNK = 16
PART = 2 * RLON // 8
SCHEDULE = sorted((b + lag, kind, b) for b in range(BLOCKS) for kind, lag in enumerate((0, 2.6, 6.2, 8.8)))


def split(v):
    hi = v.astype(BF16)
    return hi, (v - hi.astype(F32)).astype(BF16)


def place():
    lon, lat = lax.axis_index("lon"), lax.axis_index("lat")
    return lat // 2, (lat % 2) * 4 + lon // 8, (lon // 2) % 4, lon % 2


def device(x, z, y, core):
    return (z % 4) * 8 + y * 2 + core, x * 2 + z // 4


def contract_lanes(a, b):
    return lax.dot_general(a, b, (((1,), (1,)), ((), ())), precision=HIGHEST, preferred_element_type=F32)


IMAGE_ROWS = 40


def lanes_of(v):
    return lax.broadcasted_iota(jnp.int32, v.shape, 1)


def pack_image(v):
    last = v[IMAGE_ROWS:]
    tail = [pltpu.roll(last, 96 - 32 * k, 1) for k in range(3)]
    tail = jnp.concatenate(tail + [jnp.zeros((IMAGE_ROWS - 24, 128), F32)], 0)
    return jnp.where(lanes_of(tail) < RLON, v[:IMAGE_ROWS], tail)


def unpack_image(v):
    last = jnp.zeros((8, 128), F32)
    for k in range(3):
        piece = pltpu.roll(v[8 * k : 8 * k + 8], 32 + 32 * k, 1)
        last = jnp.where(lanes_of(last) // 32 == k, piece, last)
    return jnp.concatenate([jnp.where(lanes_of(v) < RLON, v, 0.0), last], 0)


def pack_gram(g):
    half = RLON // 2
    top, low = g[:half], g[half:RLON]
    lane, row = lanes_of(top), lax.broadcasted_iota(jnp.int32, top.shape, 0)
    rest = jnp.where(lane <= half, pltpu.roll(top, 1, 1), pltpu.roll(top, 16, 1))
    return jnp.where(lane <= row, pltpu.roll(low, 128 - half, 1), rest)


def unpack_gram(v):
    half = RLON // 2
    top = jnp.where(lanes_of(v) < half, pltpu.roll(v, 127, 1), pltpu.roll(v, 112, 1))
    square = jnp.concatenate([v, jnp.zeros((128 - half, 128), F32)], 0).T
    return jnp.concatenate([top, pltpu.roll(square[:half], half, 1)], 0)


PANEL = 16


def solve(total_rows, top, image_t, out, yt):
    tiles = RLON // 8
    left = [top[8 * r : 8 * r + 8] for r in range(tiles)]
    right = [image_t[8 * r : 8 * r + 8] for r in range(tiles)]
    sub = lax.broadcasted_iota(jnp.int32, (8, 128), 0)
    diagonal = lax.broadcasted_iota(jnp.int32, (8, 128), 1) - sub
    spread = lambda v: jnp.broadcast_to(v, (8, 128))
    for j in range(RLON // PANEL):
        at, first = PANEL * j, PANEL // 8 * j
        col = [
            [spread(left[first + s][:, at + q : at + q + 1]) if q >= 8 * s else None for q in range(PANEL)]
            for s in range(PANEL // 8)
        ]
        d = [[spread(col[p // 8][q][p % 8 : p % 8 + 1]) for p in range(q + 1)] for q in range(PANEL)]
        vl = [spread(left[first + p // 8][p % 8 : p % 8 + 1]) for p in range(PANEL)]
        vr = [spread(right[first + p // 8][p % 8 : p % 8 + 1]) for p in range(PANEL)]
        for p in range(PANEL):
            inv = lax.rsqrt(d[p][p])
            for q in range(p + 1, PANEL):
                d[q][p] = d[q][p] * inv
            for q in range(p + 1, PANEL):
                for r in range(p + 1, q + 1):
                    d[q][r] = d[q][r] - d[q][p] * d[r][p]
            vl[p], vr[p] = vl[p] * inv, vr[p] * inv
            for q in range(p + 1, PANEL):
                vl[q] = vl[q] - d[q][p] * vl[p]
                vr[q] = vr[q] - d[q][p] * vr[p]
        for s in range(PANEL // 8):
            rows = vr[8 * s]
            for p in range(1, 8):
                rows = jnp.where(sub == p, vr[8 * s + p], rows)
            yt[at + 8 * s : at + 8 * s + 8] = rows
        for r in range(first + PANEL // 8, tiles):
            ml, mr = [], []
            for p in range(PANEL):
                c = jnp.sum(jnp.where(diagonal == 8 * r, vl[p], 0.0), axis=1, keepdims=True)
                ml.append(c * vl[p])
                mr.append(c * vr[p])
            while len(ml) > 1:
                ml = [a + b for a, b in zip(ml[::2], ml[1::2])]
                mr = [a + b for a, b in zip(mr[::2], mr[1::2])]
            left[r], right[r] = left[r] - ml[0], right[r] - mr[0]
    out[...] = yt[...].T[0:ROWS] * jnp.sqrt(F32(total_rows))


def hooi_kernel(
    total_rows, field, lat, lev_t, old, out,
    fv, lat_in, lev_in, old_in, lats, lvl, proj, xr, pz, wt, wr, ws, wz, wf, img, ir, summed, home, gp, gr, gh, go, gf,
    yt, fsem, csem, xsem, rsem, zsem, asem, isem, hsem, gsem,
):
    x, z, y, core = place()
    me = y * 2 + core

    def send(src, dst, sems, to):
        copy = pltpu.make_async_remote_copy(
            src_ref=src, dst_ref=dst, send_sem=sems.at[0], recv_sem=sems.at[1], device_id=to, device_id_type=MESH
        )
        copy.start()
        return copy

    def arrived(ref, sem):
        pltpu.make_async_copy(ref, ref, sem).wait()

    chunk = CHUNK * LATS
    loads = [
        pltpu.make_async_copy(field.at[pl.ds(k * chunk, chunk)], fv.at[pl.ds(k * chunk, chunk)], fsem.at[k])
        for k in range(6)
    ]
    small = [
        pltpu.make_async_copy(src, dst, csem.at[k])
        for k, (src, dst) in enumerate(((lev_t, lev_in), (lat, lat_in), (old, old_in)))
    ]
    for load in small + loads:
        load.start()

    x_peers = [device((x + dx) % 4, z, y, core) for dx in (1, 2, 3)]
    z_peers = [device(x, (z + dz) % 8, y, core) for dz in range(1, 8)]
    yc_peers = [device(x, z, ((me + j) % 8) // 2, (me + j) % 2) for j in range(1, 8)]
    i_peers = [device((x + dx) % 4, (z + dz) % 8, y, core) for dx in range(4) for dz in (2, 6)]
    g_steps = [(dy, dz) for dy in range(4) for dz in (0, 1, 7, 2 if dy < 2 else 6)][1:]
    g_peers = [device(x, (z + dz) % 8, (y + dy) % 4, core) for dy, dz in g_steps]
    also = [device(x, (z + 2) % 8, (y + 2) % 4, core)]
    far = [peer for (dy, dz), peer in zip(g_steps, g_peers) if dy and dz] + also
    greeted = far + i_peers[2:] + z_peers + yc_peers + x_peers
    barrier = pltpu.get_barrier_semaphore()
    for peer in greeted:
        pl.semaphore_signal(barrier, inc=1, device_id=peer, device_id_type=MESH)

    small[0].wait()
    small[1].wait()
    levh, levl = split(lev_in[...])
    lev2 = jnp.concatenate(
        [jnp.concatenate([levh, levh], 1), jnp.concatenate([levl, jnp.zeros_like(levl)], 1)], 0
    )
    lats[...] = jnp.zeros_like(lats)
    lats[0:LATS, 0:RLAT] = lat_in[...]
    lat_pad = lats[...]
    lane = lax.broadcasted_iota(jnp.int32, (128, 128), 1)
    lat_hi, lat_lo = [], []
    for u in range(SLABS):
        tail = jnp.where(lane >= RLAT, pltpu.roll(lat_pad, 96 - 32 * u, 1), 0.0)
        hi, lo = split(jnp.concatenate([lat_pad, tail], 0))
        lat_hi.append(hi)
        lat_lo.append(lo)

    def levels(t, c):
        def one(i, carry):
            f = fv[pl.ds(pl.multiple_of((t * ROWS + i) * LATS, LATS), LATS), :]
            fh, fl = split(f)
            both = jnp.concatenate([fh, fl], 1)
            both = jnp.concatenate([both, jnp.zeros((128 - LATS, 256), BF16)], 0)
            r = lax.dot_general(lev2, both, (((1,), (1,)), ((), ())), preferred_element_type=F32)
            lvl[pl.ds(i, RLEV, stride=ROWS), :] = r[:RLEV] + r[RLEV:]
            return carry

        loads[3 * t + c].wait()
        lax.fori_loop(CHUNK * c, CHUNK * c + CHUNK, one, 0, unroll=4)

    def latitudes(t, u):
        parts = [
            jnp.concatenate([lvl[pl.ds((4 * d + v) * ROWS, ROWS), :] for d in range(8)], 0) for v in (u, 3)
        ]
        hi, lo = split(jnp.concatenate(parts, 1))
        r = (
            jnp.dot(hi, lat_hi[u], preferred_element_type=F32)
            + jnp.dot(lo, lat_hi[u], preferred_element_type=F32)
            + jnp.dot(hi, lat_lo[u], preferred_element_type=F32)
        )
        for d in range(8):
            proj[t * SLABS + u, d // 2, d % 2] = r[d * ROWS : (d + 1) * ROWS]

    xcopies = []
    for t in range(TIMES):
        for c in range(3):
            levels(t, c)
        for u in range(SLABS):
            latitudes(t, u)
            b = t * SLABS + u
            if b == 0:
                pl.semaphore_wait(barrier, len(greeted))
            xcopies.append(
                [send(proj.at[b, (x + k + 1) % 4], xr.at[b, k], xsem.at[b, k], x_peers[k]) for k in range(3)]
            )

    small[2].wait()
    old_t = old_in[...].T
    acc = jnp.zeros((ROWS, RLON), F32)

    for at, kind, b in SCHEDULE:
        if kind == 0:
            for copy in xcopies[b]:
                copy.wait_recv()
            pz[b] = proj[b, x] + xr[b, 0] + xr[b, 1] + xr[b, 2]
            for s in range(2):
                wt[b, s * RLON : (s + 1) * RLON] = jnp.dot(
                    old_t, pz[b, s], precision=HIGHEST, preferred_element_type=F32
                )
            for k in range(7):
                part = wt.at[b, pl.ds(pl.multiple_of(PART * ((me + k + 1) % 8), 8), PART)]
                send(part, wr.at[b, k], rsem.at[b], yc_peers[k])
        elif kind == 1:
            arrived(wr.at[b], rsem.at[b, 1])
            part = wt[b, pl.ds(pl.multiple_of(PART * me, 8), PART)]
            for k in range(7):
                part = part + wr[b, k]
            ws[b] = part
            for k in range(7):
                send(ws.at[b], wz.at[b, k], zsem.at[b], z_peers[k])
        elif kind == 2:
            arrived(wz.at[b], zsem.at[b, 1])
            part = ws[b]
            for k in range(7):
                part = part + wz[b, k]
            mine = pl.ds(pl.multiple_of(PART * me, 8), PART)
            wf[b, mine] = part
            for k in range(7):
                send(wf.at[b, mine], wf.at[b, mine], asem.at[b], yc_peers[k])
        else:
            arrived(wr.at[b], asem.at[b, 1])
            for s in range(2):
                acc = acc + contract_lanes(pz[b, s], wf[b, s * RLON : (s + 1) * RLON])
    img[...] = pack_image(jnp.concatenate([acc, jnp.zeros((ROWS, 128 - RLON), F32)], 1))
    for k in range(8):
        send(img, ir.at[k], isem, i_peers[k])
    arrived(ir, isem.at[1])
    image = ir[0]
    for k in range(1, 8):
        image = image + ir[k]
    image = unpack_image(image)
    summed[...] = image
    back = send(summed, home, hsem, z_peers[1])
    gp[...] = pack_gram(
        lax.dot_general(image, image, (((0,), (0,)), ((), ())), precision=HIGHEST, preferred_element_type=F32)
    )
    half = RLON // 4
    sibling = device(x, z, y, 1 - core)
    mine, other = (pl.ds(pl.multiple_of(half * c, 8), half) for c in (core, 1 - core))
    first = send(gp.at[other], gr, gsem.at[0], sibling)
    first.wait_recv()
    gh[...] = gp[mine] + gr[...]
    for k in range(15):
        send(gh, go.at[k], gsem.at[1], g_peers[k])
    arrived(go, gsem.at[1, 1])
    total = gh[...]
    for k in range(15):
        total = total + go[k]
    gf[mine] = total
    last = send(gf.at[mine], gf.at[mine], gsem.at[2], sibling)
    last.wait_recv()
    back.wait_recv()
    image_t = jnp.concatenate([home[...].T[0:RLON], jnp.zeros((RLON, 128 - ROWS), F32)], 1)
    solve(total_rows, unpack_gram(gf[...]), image_t, out, yt)

    for row in xcopies:
        for copy in row:
            copy.wait_send()
    for b in range(BLOCKS):
        arrived(wr.at[b], rsem.at[b, 0])
        arrived(wz.at[b], zsem.at[b, 0])
        arrived(wr.at[b], asem.at[b, 0])
    arrived(ir, isem.at[0])
    back.wait_send()
    first.wait_send()
    arrived(go, gsem.at[1, 0])
    last.wait_send()


def body(field, lat_factor, lev_factor, old_factor):
    vmem = pl.BlockSpec(memory_space=pltpu.VMEM)
    dma = pltpu.SemaphoreType.DMA
    field = field.reshape(TIMES * ROWS * LATS, LEVS)
    total_rows = ROWS * lax.axis_size("lon")
    return pl.pallas_call(
        functools.partial(hooi_kernel, total_rows),
        out_shape=pltpu.VMEM((ROWS, RLON), F32),
        in_specs=[pl.BlockSpec(memory_space=pltpu.HBM)] * 4,
        out_specs=vmem,
        scratch_shapes=[
            pltpu.VMEM((TIMES * ROWS * LATS, LEVS), F32),
            pltpu.VMEM((LATS, RLAT), F32),
            pltpu.VMEM((RLEV, LEVS), F32),
            pltpu.VMEM((ROWS, RLON), F32),
            pltpu.VMEM((128, 128), F32),
            pltpu.VMEM((RLEV * ROWS, 128), F32),
            pltpu.VMEM((BLOCKS, 4, 2, ROWS, 128), F32),
            pltpu.VMEM((BLOCKS, 3, 2, ROWS, 128), F32),
            pltpu.VMEM((BLOCKS, 2, ROWS, 128), F32),
            pltpu.VMEM((BLOCKS, 2 * RLON, 128), F32),
            pltpu.VMEM((BLOCKS, 7, PART, 128), F32),
            pltpu.VMEM((BLOCKS, PART, 128), F32),
            pltpu.VMEM((BLOCKS, 7, PART, 128), F32),
            pltpu.VMEM((BLOCKS, 2 * RLON, 128), F32),
            pltpu.VMEM((IMAGE_ROWS, 128), F32),
            pltpu.VMEM((8, IMAGE_ROWS, 128), F32),
            pltpu.VMEM((ROWS, 128), F32),
            pltpu.VMEM((ROWS, 128), F32),
            pltpu.VMEM((RLON // 2, 128), F32),
            pltpu.VMEM((RLON // 4, 128), F32),
            pltpu.VMEM((RLON // 4, 128), F32),
            pltpu.VMEM((15, RLON // 4, 128), F32),
            pltpu.VMEM((RLON // 2, 128), F32),
            pltpu.VMEM((RLON, 128), F32),
            dma((6,)),
            dma((3,)),
            dma((BLOCKS, 3, 2)),
            dma((BLOCKS, 2)),
            dma((BLOCKS, 2)),
            dma((BLOCKS, 2)),
            dma((2,)),
            dma((2,)),
            dma((3, 2)),
        ],
        compiler_params=pltpu.CompilerParams(
            collective_id=0, has_side_effects=True, vmem_limit_bytes=48 * 1024 * 1024
        ),
    )(*(pltpu.with_memory_space_constraint(v, pltpu.HBM) for v in (field, lat_factor, lev_factor.T, old_factor)))


def solution(mesh):
    placed = (P(None, "lon", "lat", None), P("lat", None), P(), P("lon", None))
    return jax.shard_map(
        body, mesh=mesh, in_specs=placed, out_specs=P("lon", None), check_vma=False
    )
```

```python
import functools

import jax
import jax.numpy as jnp
from jax import lax
from jax.experimental import pallas as pl
from jax.experimental.pallas import tpu as pltpu
from jax.sharding import PartitionSpec as P

MESH = pl.DeviceIdType.MESH
HIGHEST = lax.Precision.HIGHEST
F32, BF16 = jnp.float32, jnp.bfloat16
TIMES, ROWS, LATS, LEVS = 2, 48, 96, 128
RLAT, RLEV, RLON = 96, 32, 96
SLABS = 3
BLOCKS = TIMES * SLABS * 2
PART = RLON // 8
SCHEDULE = sorted((b + lag, kind, b) for b in range(BLOCKS) for kind, lag in enumerate((0, 4.6, 11, 16)))


def split(v):
    hi = v.astype(BF16)
    return hi, (v - hi.astype(F32)).astype(BF16)


def place():
    lon, lat = lax.axis_index("lon"), lax.axis_index("lat")
    return lat // 2, (lat % 2) * 4 + lon // 8, (lon // 2) % 4, lon % 2


def device(x, z, y, core):
    return (z % 4) * 8 + y * 2 + core, x * 2 + z // 4


def contract_lanes(a, b):
    return lax.dot_general(a, b, (((1,), (1,)), ((), ())), precision=HIGHEST, preferred_element_type=F32)


IMAGE_ROWS = 40


def lanes_of(v):
    return lax.broadcasted_iota(jnp.int32, v.shape, 1)


def pack_image(v):
    last = v[IMAGE_ROWS:]
    tail = [pltpu.roll(last, 96 - 32 * k, 1) for k in range(3)]
    tail = jnp.concatenate(tail + [jnp.zeros((IMAGE_ROWS - 24, 128), F32)], 0)
    return jnp.where(lanes_of(tail) < RLON, v[:IMAGE_ROWS], tail)


def unpack_image(v):
    last = jnp.zeros((8, 128), F32)
    for k in range(3):
        piece = pltpu.roll(v[8 * k : 8 * k + 8], 32 + 32 * k, 1)
        last = jnp.where(lanes_of(last) // 32 == k, piece, last)
    return jnp.concatenate([jnp.where(lanes_of(v) < RLON, v, 0.0), last], 0)


def pack_gram(g):
    half = RLON // 2
    top, low = g[:half], g[half:RLON]
    lane, row = lanes_of(top), lax.broadcasted_iota(jnp.int32, top.shape, 0)
    rest = jnp.where(lane <= half, pltpu.roll(top, 1, 1), pltpu.roll(top, 16, 1))
    return jnp.where(lane <= row, pltpu.roll(low, 128 - half, 1), rest)


def unpack_gram(v):
    half = RLON // 2
    top = jnp.where(lanes_of(v) < half, pltpu.roll(v, 127, 1), pltpu.roll(v, 112, 1))
    square = jnp.concatenate([v, jnp.zeros((128 - half, 128), F32)], 0).T
    return jnp.concatenate([top, pltpu.roll(square[:half], half, 1)], 0)


PANEL = 16


def solve(total_rows, top, image_t, out, yt):
    tiles = RLON // 8
    left = [top[8 * r : 8 * r + 8] for r in range(tiles)]
    right = [image_t[8 * r : 8 * r + 8] for r in range(tiles)]
    sub = lax.broadcasted_iota(jnp.int32, (8, 128), 0)
    diagonal = lax.broadcasted_iota(jnp.int32, (8, 128), 1) - sub
    spread = lambda v: jnp.broadcast_to(v, (8, 128))
    for j in range(RLON // PANEL):
        at, first = PANEL * j, PANEL // 8 * j
        col = [
            [spread(left[first + s][:, at + q : at + q + 1]) if q >= 8 * s else None for q in range(PANEL)]
            for s in range(PANEL // 8)
        ]
        d = [[spread(col[p // 8][q][p % 8 : p % 8 + 1]) for p in range(q + 1)] for q in range(PANEL)]
        vl = [spread(left[first + p // 8][p % 8 : p % 8 + 1]) for p in range(PANEL)]
        vr = [spread(right[first + p // 8][p % 8 : p % 8 + 1]) for p in range(PANEL)]
        for p in range(PANEL):
            inv = lax.rsqrt(d[p][p])
            for q in range(p + 1, PANEL):
                d[q][p] = d[q][p] * inv
            for q in range(p + 1, PANEL):
                for r in range(p + 1, q + 1):
                    d[q][r] = d[q][r] - d[q][p] * d[r][p]
            vl[p], vr[p] = vl[p] * inv, vr[p] * inv
            for q in range(p + 1, PANEL):
                vl[q] = vl[q] - d[q][p] * vl[p]
                vr[q] = vr[q] - d[q][p] * vr[p]
        for s in range(PANEL // 8):
            rows = vr[8 * s]
            for p in range(1, 8):
                rows = jnp.where(sub == p, vr[8 * s + p], rows)
            yt[at + 8 * s : at + 8 * s + 8] = rows
        for r in range(first + PANEL // 8, tiles):
            ml, mr = [], []
            for p in range(PANEL):
                c = jnp.sum(jnp.where(diagonal == 8 * r, vl[p], 0.0), axis=1, keepdims=True)
                ml.append(c * vl[p])
                mr.append(c * vr[p])
            while len(ml) > 1:
                ml = [a + b for a, b in zip(ml[::2], ml[1::2])]
                mr = [a + b for a, b in zip(mr[::2], mr[1::2])]
            left[r], right[r] = left[r] - ml[0], right[r] - mr[0]
    out[...] = yt[...].T[0:ROWS] * jnp.sqrt(F32(total_rows))


def hooi_kernel(
    total_rows, field, lat, lev_t, old, out,
    fv, lat_in, lev_in, old_in, lats, lvl, proj, xr, pz, wt, wr, ws, wz, wf, img, ir, summed, home, gp, gr, gh, go, gf,
    yt, fsem, csem, sent, xsem, rsem, zsem, asem, isem, hsem, gsem,
):
    x, z, y, core = place()
    me = y * 2 + core

    def send(src, dst, sent, landed, to):
        copy = pltpu.make_async_remote_copy(
            src_ref=src, dst_ref=dst, send_sem=sent, recv_sem=landed, device_id=to, device_id_type=MESH
        )
        copy.start()
        return copy

    def arrived(ref, sem):
        pltpu.make_async_copy(ref, ref, sem).wait()

    chunk = ROWS * LATS
    loads = [
        pltpu.make_async_copy(field.at[pl.ds(k * chunk, chunk)], fv.at[pl.ds(k * chunk, chunk)], fsem.at[k])
        for k in range(TIMES)
    ]
    small = [
        pltpu.make_async_copy(src, dst, csem.at[k])
        for k, (src, dst) in enumerate(((lev_t, lev_in), (lat, lat_in), (old, old_in)))
    ]
    for load in small + loads:
        load.start()

    x_peers = [device((x + dx) % 4, z, y, core) for dx in (1, 2, 3)]
    z_peers = [device(x, (z + dz) % 8, y, core) for dz in range(1, 8)]
    yc_peers = [device(x, z, ((me + j) % 8) // 2, (me + j) % 2) for j in range(1, 8)]
    i_peers = [device((x + dx) % 4, (z + dz) % 8, y, core) for dx in range(4) for dz in (2, 6)]
    g_steps = [(dy, dz) for dy in range(4) for dz in (0, 1, 7, 2 if dy < 2 else 6)][1:]
    g_peers = [device(x, (z + dz) % 8, (y + dy) % 4, core) for dy, dz in g_steps]
    also = [device(x, (z + 2) % 8, (y + 2) % 4, core)]
    far = [peer for (dy, dz), peer in zip(g_steps, g_peers) if dy and dz] + also
    greeted = far + i_peers[2:] + z_peers + yc_peers + x_peers
    barrier = pltpu.get_barrier_semaphore()
    for peer in greeted:
        pl.semaphore_signal(barrier, inc=1, device_id=peer, device_id_type=MESH)

    small[0].wait()
    small[1].wait()
    levh, levl = split(lev_in[...])
    lev2 = jnp.concatenate(
        [jnp.concatenate([levh, levh], 1), jnp.concatenate([levl, jnp.zeros_like(levl)], 1)], 0
    )
    lats[...] = jnp.zeros_like(lats)
    lats[0:LATS, 0:RLAT] = lat_in[...]
    lat_pad = lats[...]
    lane = lax.broadcasted_iota(jnp.int32, (128, 128), 1)
    lat_hi, lat_lo = [], []
    for u in range(SLABS):
        tail = jnp.where(lane >= RLAT, pltpu.roll(lat_pad, 96 - 32 * u, 1), 0.0)
        hi, lo = split(jnp.concatenate([lat_pad, tail], 0))
        lat_hi.append(hi)
        lat_lo.append(lo)

    def levels(t):
        def one(i, carry):
            f = fv[pl.ds(pl.multiple_of((t * ROWS + i) * LATS, LATS), LATS), :]
            fh, fl = split(f)
            both = jnp.concatenate([fh, fl], 1)
            both = jnp.concatenate([both, jnp.zeros((128 - LATS, 256), BF16)], 0)
            r = lax.dot_general(lev2, both, (((1,), (1,)), ((), ())), preferred_element_type=F32)
            lvl[pl.ds(i, RLEV, stride=ROWS), :] = r[:RLEV] + r[RLEV:]
            return carry

        loads[t].wait()
        lax.fori_loop(0, ROWS, one, 0, unroll=16)

    def latitudes(t, u):
        parts = [
            jnp.concatenate([lvl[pl.ds((4 * d + v) * ROWS, ROWS), :] for d in range(8)], 0) for v in (u, 3)
        ]
        hi, lo = split(jnp.concatenate(parts, 1))
        r = (
            jnp.dot(hi, lat_hi[u], preferred_element_type=F32)
            + jnp.dot(lo, lat_hi[u], preferred_element_type=F32)
            + jnp.dot(hi, lat_lo[u], preferred_element_type=F32)
        )
        for d in range(8):
            proj[2 * (t * SLABS + u) + d % 2, d // 2] = r[d * ROWS : (d + 1) * ROWS]

    for t in range(TIMES):
        levels(t)
        for u in range(SLABS):
            latitudes(t, u)
            if t + u == 0:
                pl.semaphore_wait(barrier, len(greeted))
            for b in range(2 * (t * SLABS + u), 2 * (t * SLABS + u) + 2):
                for k in range(3):
                    send(proj.at[b, (x + k + 1) % 4], xr.at[b, k], sent.at[0], xsem.at[b], x_peers[k])

    small[2].wait()
    place_of = lambda r: 16 * (r // PART) + r % PART
    to_slots = (
        place_of(lax.broadcasted_iota(jnp.int32, (128, 128), 0)) == lax.broadcasted_iota(jnp.int32, (128, 128), 1)
    ).astype(F32)
    to_slots = jnp.where(lax.broadcasted_iota(jnp.int32, (128, 128), 0) < RLON, to_slots, 0.0)
    old_t = jnp.dot(old_in[...], to_slots[:RLON], precision=HIGHEST, preferred_element_type=F32).T
    wf[...] = jnp.zeros_like(wf)
    acc = jnp.zeros((ROWS, 128), F32)

    for at, kind, b in SCHEDULE:
        if kind == 0:
            arrived(xr.at[b], xsem.at[b])
            pz[b] = proj[b, x] + xr[b, 0] + xr[b, 1] + xr[b, 2]
            part = jnp.dot(old_t, pz[b], precision=HIGHEST, preferred_element_type=F32)
            for k in range(8):
                wt[b, k] = part[16 * k : 16 * k + PART]
            for k in range(7):
                send(wt.at[b, (me + k + 1) % 8], wr.at[b, k], sent.at[1], rsem.at[b], yc_peers[k])
        elif kind == 1:
            arrived(wr.at[b], rsem.at[b])
            part = wt[b, me]
            for k in range(7):
                part = part + wr[b, k]
            ws[b] = part
            for k in range(7):
                send(ws.at[b], wz.at[b, k], sent.at[2], zsem.at[b], z_peers[k])
        elif kind == 2:
            arrived(wz.at[b], zsem.at[b])
            part = ws[b]
            for k in range(7):
                part = part + wz[b, k]
            wf[b, me, 0:PART] = part
            mine = wf.at[b, me, pl.ds(0, PART)]
            for k in range(7):
                send(mine, mine, sent.at[3], asem.at[b], yc_peers[k])
        else:
            arrived(wr.at[b], asem.at[b])
            acc = acc + contract_lanes(pz[b], wf[b].reshape(128, 128))
    img[...] = pack_image(contract_lanes(acc, to_slots))
    for k in range(8):
        send(img, ir.at[k], sent.at[4], isem, i_peers[k])
    arrived(ir, isem)
    image = ir[0]
    for k in range(1, 8):
        image = image + ir[k]
    image = unpack_image(image)
    summed[...] = image
    back = send(summed, home, sent.at[5], hsem, z_peers[1])
    gp[...] = pack_gram(
        lax.dot_general(image, image, (((0,), (0,)), ((), ())), precision=HIGHEST, preferred_element_type=F32)
    )
    half = RLON // 4
    sibling = device(x, z, y, 1 - core)
    mine, other = (pl.ds(pl.multiple_of(half * c, 8), half) for c in (core, 1 - core))
    first = send(gp.at[other], gr, sent.at[6], gsem.at[0], sibling)
    first.wait_recv()
    gh[...] = gp[mine] + gr[...]
    for k in range(15):
        send(gh, go.at[k], sent.at[7], gsem.at[1], g_peers[k])
    arrived(go, gsem.at[1])
    total = gh[...]
    for k in range(15):
        total = total + go[k]
    gf[mine] = total
    last = send(gf.at[mine], gf.at[mine], sent.at[8], gsem.at[2], sibling)
    last.wait_recv()
    back.wait_recv()
    image_t = jnp.concatenate([home[...].T[0:RLON], jnp.zeros((RLON, 128 - ROWS), F32)], 1)
    solve(total_rows, unpack_gram(gf[...]), image_t, out, yt)

    for k, ref in enumerate((xr, wr, wz, wr, ir)):
        arrived(ref, sent.at[k])
    back.wait_send()
    first.wait_send()
    arrived(go, sent.at[7])
    last.wait_send()


def body(field, lat_factor, lev_factor, old_factor):
    vmem = pl.BlockSpec(memory_space=pltpu.VMEM)
    dma = pltpu.SemaphoreType.DMA
    field = field.reshape(TIMES * ROWS * LATS, LEVS)
    total_rows = ROWS * lax.axis_size("lon")
    return pl.pallas_call(
        functools.partial(hooi_kernel, total_rows),
        out_shape=pltpu.VMEM((ROWS, RLON), F32),
        in_specs=[pl.BlockSpec(memory_space=pltpu.HBM)] * 4,
        out_specs=vmem,
        scratch_shapes=[
            pltpu.VMEM((TIMES * ROWS * LATS, LEVS), F32),
            pltpu.VMEM((LATS, RLAT), F32),
            pltpu.VMEM((RLEV, LEVS), F32),
            pltpu.VMEM((ROWS, RLON), F32),
            pltpu.VMEM((128, 128), F32),
            pltpu.VMEM((RLEV * ROWS, 128), F32),
            pltpu.VMEM((BLOCKS, 4, ROWS, 128), F32),
            pltpu.VMEM((BLOCKS, 3, ROWS, 128), F32),
            pltpu.VMEM((BLOCKS, ROWS, 128), F32),
            pltpu.VMEM((BLOCKS, 8, PART, 128), F32),
            pltpu.VMEM((BLOCKS, 7, PART, 128), F32),
            pltpu.VMEM((BLOCKS, PART, 128), F32),
            pltpu.VMEM((BLOCKS, 7, PART, 128), F32),
            pltpu.VMEM((BLOCKS, 8, 16, 128), F32),
            pltpu.VMEM((IMAGE_ROWS, 128), F32),
            pltpu.VMEM((8, IMAGE_ROWS, 128), F32),
            pltpu.VMEM((ROWS, 128), F32),
            pltpu.VMEM((ROWS, 128), F32),
            pltpu.VMEM((RLON // 2, 128), F32),
            pltpu.VMEM((RLON // 4, 128), F32),
            pltpu.VMEM((RLON // 4, 128), F32),
            pltpu.VMEM((15, RLON // 4, 128), F32),
            pltpu.VMEM((RLON // 2, 128), F32),
            pltpu.VMEM((RLON, 128), F32),
            dma((TIMES,)),
            dma((3,)),
            dma((9,)),
            dma((BLOCKS,)),
            dma((BLOCKS,)),
            dma((BLOCKS,)),
            dma((BLOCKS,)),
            dma,
            dma,
            dma((3,)),
        ],
        compiler_params=pltpu.CompilerParams(
            collective_id=0, has_side_effects=True, vmem_limit_bytes=48 * 1024 * 1024
        ),
    )(*(pltpu.with_memory_space_constraint(v, pltpu.HBM) for v in (field, lat_factor, lev_factor.T, old_factor)))


def solution(mesh):
    placed = (P(None, "lon", "lat", None), P("lat", None), P(), P("lon", None))
    return jax.shard_map(
        body, mesh=mesh, in_specs=placed, out_specs=P("lon", None), check_vma=False
    )
```

```python
import functools
import math

import jax
import jax.numpy as jnp
from jax import lax
from jax.experimental import pallas as pl
from jax.experimental.pallas import tpu as pltpu
from jax.sharding import PartitionSpec as P

MESH = pl.DeviceIdType.MESH
HIGHEST = lax.Precision.HIGHEST
F32, BF16 = jnp.float32, jnp.bfloat16
TIMES, ROWS, LATS, LEVS = 2, 48, 96, 128
RLAT, RLEV, RLON = 96, 32, 96
SLABS = 3
BLOCKS = TIMES * SLABS * 2
LOADS = (0, 16), (16, 32), (48, 48)
PART = RLON // 8
SCHEDULE = sorted((b + lag, kind, b) for b in range(BLOCKS) for kind, lag in enumerate((0, 4.6, 11, 16)))


def split(v):
    hi = v.astype(BF16)
    return hi, (v - hi.astype(F32)).astype(BF16)


def place():
    lon, lat = lax.axis_index("lon"), lax.axis_index("lat")
    return lat // 2, (lat % 2) * 4 + lon // 8, (lon // 2) % 4, lon % 2


def device(x, z, y, core):
    return (z % 4) * 8 + y * 2 + core, x * 2 + z // 4


def contract_lanes(a, b):
    return lax.dot_general(a, b, (((1,), (1,)), ((), ())), precision=HIGHEST, preferred_element_type=F32)


IMAGE_ROWS = 40


def lanes_of(v):
    return lax.broadcasted_iota(jnp.int32, v.shape, 1)


def pack_image(v):
    last = v[IMAGE_ROWS:]
    tail = [pltpu.roll(last, 96 - 32 * k, 1) for k in range(3)]
    tail = jnp.concatenate(tail + [jnp.zeros((IMAGE_ROWS - 24, 128), F32)], 0)
    return jnp.where(lanes_of(tail) < RLON, v[:IMAGE_ROWS], tail)


def unpack_image(v):
    last = jnp.zeros((8, 128), F32)
    for k in range(3):
        piece = pltpu.roll(v[8 * k : 8 * k + 8], 32 + 32 * k, 1)
        last = jnp.where(lanes_of(last) // 32 == k, piece, last)
    return jnp.concatenate([jnp.where(lanes_of(v) < RLON, v, 0.0), last], 0)


def pack_gram(g):
    half = RLON // 2
    top, low = g[:half], g[half:RLON]
    lane, row = lanes_of(top), lax.broadcasted_iota(jnp.int32, top.shape, 0)
    rest = jnp.where(lane <= half, pltpu.roll(top, 1, 1), pltpu.roll(top, 16, 1))
    return jnp.where(lane <= row, pltpu.roll(low, 128 - half, 1), rest)


def unpack_gram(v):
    half = RLON // 2
    top = jnp.where(lanes_of(v) < half, pltpu.roll(v, 127, 1), pltpu.roll(v, 112, 1))
    square = jnp.concatenate([v, jnp.zeros((128 - half, 128), F32)], 0).T
    return jnp.concatenate([top, pltpu.roll(square[:half], half, 1)], 0)


PANEL = 16


def solve(total_rows, top, image_t, out, yt):
    tiles = RLON // 8
    left = [top[8 * r : 8 * r + 8] for r in range(tiles)]
    right = [image_t[8 * r : 8 * r + 8] for r in range(tiles)]
    sub = lax.broadcasted_iota(jnp.int32, (8, 128), 0)
    diagonal = lax.broadcasted_iota(jnp.int32, (8, 128), 1) - sub
    spread = lambda v: jnp.broadcast_to(v, (8, 128))
    for j in range(RLON // PANEL):
        at, first = PANEL * j, PANEL // 8 * j
        col = [
            [spread(left[first + s][:, at + q : at + q + 1]) if q >= 8 * s else None for q in range(PANEL)]
            for s in range(PANEL // 8)
        ]
        d = [[spread(col[p // 8][q][p % 8 : p % 8 + 1]) for p in range(q + 1)] for q in range(PANEL)]
        vl = [spread(left[first + p // 8][p % 8 : p % 8 + 1]) for p in range(PANEL)]
        vr = [spread(right[first + p // 8][p % 8 : p % 8 + 1]) for p in range(PANEL)]
        for p in range(PANEL):
            inv = lax.rsqrt(d[p][p])
            for q in range(p + 1, PANEL):
                d[q][p] = d[q][p] * inv
            for q in range(p + 1, PANEL):
                for r in range(p + 1, q + 1):
                    d[q][r] = d[q][r] - d[q][p] * d[r][p]
            vl[p], vr[p] = vl[p] * inv, vr[p] * inv
            for q in range(p + 1, PANEL):
                vl[q] = vl[q] - d[q][p] * vl[p]
                vr[q] = vr[q] - d[q][p] * vr[p]
        for s in range(PANEL // 8):
            rows = vr[8 * s]
            for p in range(1, 8):
                rows = jnp.where(sub == p, vr[8 * s + p], rows)
            yt[at + 8 * s : at + 8 * s + 8] = rows
        for r in range(first + PANEL // 8, tiles):
            ml, mr = [], []
            for p in range(PANEL):
                c = jnp.sum(jnp.where(diagonal == 8 * r, vl[p], 0.0), axis=1, keepdims=True)
                ml.append(c * vl[p])
                mr.append(c * vr[p])
            while len(ml) > 1:
                ml = [a + b for a, b in zip(ml[::2], ml[1::2])]
                mr = [a + b for a, b in zip(mr[::2], mr[1::2])]
            left[r], right[r] = left[r] - ml[0], right[r] - mr[0]
    out[...] = yt[...].T[0:ROWS] * jnp.sqrt(F32(total_rows))


def hooi_kernel(
    total_rows, field, lat, lev_t, old, out,
    fv, lat_in, lev_in, old_in, lats, lvl, proj, xr, pz, wt, wr, ws, wz, wf, img, ir, summed, home, gp, gr, gh, go, gf,
    yt, fsem, csem, passed, sent, xsem, rsem, zsem, asem, isem, hsem, gsem,
):
    x, z, y, core = place()
    me = y * 2 + core

    def send(src, dst, sent, landed, to):
        copy = pltpu.make_async_remote_copy(
            src_ref=src, dst_ref=dst, send_sem=sent, recv_sem=landed, device_id=to, device_id_type=MESH
        )
        copy.start()
        return copy

    def arrived(ref, sem):
        pltpu.make_async_copy(ref, ref, sem).wait()

    loads = [
        pltpu.make_async_copy(
            field.at[pl.ds(at * LATS, rows * LATS)], fv.at[pl.ds(at * LATS, rows * LATS)], fsem.at[k]
        )
        for k, (at, rows) in enumerate(LOADS)
    ]
    small = [
        pltpu.make_async_copy(src, dst, csem.at[k])
        for k, (src, dst) in enumerate(((lev_t, lev_in), (lat, lat_in), (old, old_in)))
    ]
    for load in small + loads:
        load.start()

    x_peers = [device((x + dx) % 4, z, y, core) for dx in (1, 2, 3)]
    y_peers = [device(x, z, (y + dy) % 4, core) for dy in (1, 2, 3)]
    z_peers = [device(x, (z + dz) % 8, y, core) for dz in range(1, 8)]
    yc_peers = [device(x, z, ((me + j) % 8) // 2, (me + j) % 2) for j in range(1, 8)]
    i_peers = [device((x + dx) % 4, (z + dz) % 8, y, core) for dx in range(4) for dz in (2, 6)]
    g_steps = [(dy, dz) for dy in range(4) for dz in (0, 1, 7, 2 if dy < 2 else 6)][1:]
    g_peers = [device(x, (z + dz) % 8, (y + dy) % 4, core) for dy, dz in g_steps]

    greeted = x_peers + yc_peers + [z_peers[k] for k in (1, 5, 0, 6)]
    barrier = pltpu.get_barrier_semaphore()
    for peer in greeted:
        pl.semaphore_signal(barrier, inc=1, device_id=peer, device_id_type=MESH)
    told = x_peers + y_peers + [z_peers[1], z_peers[5]]

    small[0].wait()
    small[1].wait()
    levh, levl = split(lev_in[...])
    lev2 = jnp.concatenate(
        [jnp.concatenate([levh, levh], 1), jnp.concatenate([levl, jnp.zeros_like(levl)], 1)], 0
    )
    lats[...] = jnp.zeros_like(lats)
    lats[0:LATS, 0:RLAT] = lat_in[...]
    lat_pad = lats[...]
    lane = lax.broadcasted_iota(jnp.int32, (128, 128), 1)
    lat_hi, lat_lo = [], []
    for u in range(SLABS):
        tail = jnp.where(lane >= RLAT, pltpu.roll(lat_pad, 96 - 32 * u, 1), 0.0)
        hi, lo = split(jnp.concatenate([lat_pad, tail], 0))
        lat_hi.append(hi)
        lat_lo.append(lo)

    def levels(k):
        def one(i, carry):
            f = fv[pl.ds(pl.multiple_of(i * LATS, LATS), LATS), :]
            fh, fl = split(f)
            both = jnp.concatenate([fh, fl], 1)
            both = jnp.concatenate([both, jnp.zeros((128 - LATS, 256), BF16)], 0)
            r = lax.dot_general(lev2, both, (((1,), (1,)), ((), ())), preferred_element_type=F32)
            lvl[pl.ds(lax.rem(i, ROWS), RLEV, stride=ROWS), :] = r[:RLEV] + r[RLEV:]
            return carry

        loads[k].wait()
        at, rows = LOADS[k]
        lax.fori_loop(at, at + rows, one, 0, unroll=16)

    def latitudes(t, u):
        parts = [
            jnp.concatenate([lvl[pl.ds((4 * d + v) * ROWS, ROWS), :] for d in range(8)], 0) for v in (u, 3)
        ]
        hi, lo = split(jnp.concatenate(parts, 1))
        r = (
            jnp.dot(hi, lat_hi[u], preferred_element_type=F32)
            + jnp.dot(lo, lat_hi[u], preferred_element_type=F32)
            + jnp.dot(hi, lat_lo[u], preferred_element_type=F32)
        )
        for d in range(8):
            proj[2 * (t * SLABS + u) + d % 2, d // 2] = r[d * ROWS : (d + 1) * ROWS]

    for t in range(TIMES):
        for k in ((0, 1), (2,))[t]:
            levels(k)
        for u in range(SLABS):
            latitudes(t, u)
            if t + u == 0:
                pl.semaphore_wait(barrier, len(greeted))
                for peer in told:
                    pl.semaphore_signal(passed, inc=1, device_id=peer, device_id_type=MESH)
            for b in range(2 * (t * SLABS + u), 2 * (t * SLABS + u) + 2):
                for k in range(3):
                    send(proj.at[b, (x + k + 1) % 4], xr.at[b, k], sent, xsem.at[b], x_peers[k])

    pl.semaphore_wait(passed, len(told))
    small[2].wait()
    place_of = lambda r: 16 * (r // PART) + r % PART
    to_slots = (
        place_of(lax.broadcasted_iota(jnp.int32, (128, 128), 0)) == lax.broadcasted_iota(jnp.int32, (128, 128), 1)
    ).astype(F32)
    to_slots = jnp.where(lax.broadcasted_iota(jnp.int32, (128, 128), 0) < RLON, to_slots, 0.0)
    old_t = jnp.dot(old_in[...], to_slots[:RLON], precision=HIGHEST, preferred_element_type=F32).T
    wf[...] = jnp.zeros_like(wf)
    acc = jnp.zeros((ROWS, 128), F32)

    for at, kind, b in SCHEDULE:
        if kind == 0:
            arrived(xr.at[b], xsem.at[b])
            pz[b] = proj[b, x] + xr[b, 0] + xr[b, 1] + xr[b, 2]
            part = jnp.dot(old_t, pz[b], precision=HIGHEST, preferred_element_type=F32)
            for k in range(8):
                wt[b, k] = part[16 * k : 16 * k + PART]
            for k in range(7):
                send(wt.at[b, (me + k + 1) % 8], wr.at[b, k], sent, rsem.at[b], yc_peers[k])
        elif kind == 1:
            arrived(wr.at[b], rsem.at[b])
            part = wt[b, me]
            for k in range(7):
                part = part + wr[b, k]
            ws[b] = part
            for k in range(7):
                send(ws.at[b], wz.at[b, k], sent, zsem.at[b], z_peers[k])
        elif kind == 2:
            arrived(wz.at[b], zsem.at[b])
            part = ws[b]
            for k in range(7):
                part = part + wz[b, k]
            wf[b, me, 0:PART] = part
            mine = wf.at[b, me, pl.ds(0, PART)]
            for k in range(7):
                send(mine, mine, sent, asem.at[b], yc_peers[k])
        else:
            arrived(wr.at[b], asem.at[b])
            acc = acc + contract_lanes(pz[b], wf[b].reshape(128, 128))
    img[...] = pack_image(contract_lanes(acc, to_slots))
    for k in range(8):
        send(img, ir.at[k], sent, isem, i_peers[k])
    arrived(ir, isem)
    image = ir[0]
    for k in range(1, 8):
        image = image + ir[k]
    image = unpack_image(image)
    summed[...] = image
    send(summed, home, sent, hsem, z_peers[1])
    gp[...] = pack_gram(
        lax.dot_general(image, image, (((0,), (0,)), ((), ())), precision=HIGHEST, preferred_element_type=F32)
    )
    half = RLON // 4
    sibling = device(x, z, y, 1 - core)
    mine, other = (pl.ds(pl.multiple_of(half * c, 8), half) for c in (core, 1 - core))
    send(gp.at[other], gr, sent, gsem.at[0], sibling)
    arrived(gr, gsem.at[0])
    gh[...] = gp[mine] + gr[...]
    for k in range(15):
        send(gh, go.at[k], sent, gsem.at[1], g_peers[k])
    arrived(go, gsem.at[1])
    total = gh[...]
    for k in range(15):
        total = total + go[k]
    gf[mine] = total
    send(gf.at[mine], gf.at[mine], sent, gsem.at[2], sibling)
    arrived(gr, gsem.at[2])
    arrived(home, hsem)
    image_t = jnp.concatenate([home[...].T[0:RLON], jnp.zeros((RLON, 128 - ROWS), F32)], 1)
    solve(total_rows, unpack_gram(gf[...]), image_t, out, yt)

    refs = (xr, wr, wz, wr, ir, home, gr, go, gr)
    arrived(fv.at[pl.ds(0, sum(math.prod(ref.shape) // 128 for ref in refs))], sent)


def body(field, lat_factor, lev_factor, old_factor):
    vmem = pl.BlockSpec(memory_space=pltpu.VMEM)
    dma = pltpu.SemaphoreType.DMA
    field = field.reshape(TIMES * ROWS * LATS, LEVS)
    total_rows = ROWS * lax.axis_size("lon")
    return pl.pallas_call(
        functools.partial(hooi_kernel, total_rows),
        out_shape=pltpu.VMEM((ROWS, RLON), F32),
        in_specs=[pl.BlockSpec(memory_space=pltpu.HBM)] * 4,
        out_specs=vmem,
        scratch_shapes=[
            pltpu.VMEM((TIMES * ROWS * LATS, LEVS), F32),
            pltpu.VMEM((LATS, RLAT), F32),
            pltpu.VMEM((RLEV, LEVS), F32),
            pltpu.VMEM((ROWS, RLON), F32),
            pltpu.VMEM((128, 128), F32),
            pltpu.VMEM((RLEV * ROWS, 128), F32),
            pltpu.VMEM((BLOCKS, 4, ROWS, 128), F32),
            pltpu.VMEM((BLOCKS, 3, ROWS, 128), F32),
            pltpu.VMEM((BLOCKS, ROWS, 128), F32),
            pltpu.VMEM((BLOCKS, 8, PART, 128), F32),
            pltpu.VMEM((BLOCKS, 7, PART, 128), F32),
            pltpu.VMEM((BLOCKS, PART, 128), F32),
            pltpu.VMEM((BLOCKS, 7, PART, 128), F32),
            pltpu.VMEM((BLOCKS, 8, 16, 128), F32),
            pltpu.VMEM((IMAGE_ROWS, 128), F32),
            pltpu.VMEM((8, IMAGE_ROWS, 128), F32),
            pltpu.VMEM((ROWS, 128), F32),
            pltpu.VMEM((ROWS, 128), F32),
            pltpu.VMEM((RLON // 2, 128), F32),
            pltpu.VMEM((RLON // 4, 128), F32),
            pltpu.VMEM((RLON // 4, 128), F32),
            pltpu.VMEM((15, RLON // 4, 128), F32),
            pltpu.VMEM((RLON // 2, 128), F32),
            pltpu.VMEM((RLON, 128), F32),
            dma((3,)),
            dma((3,)),
            pltpu.SemaphoreType.REGULAR,
            dma,
            dma((BLOCKS,)),
            dma((BLOCKS,)),
            dma((BLOCKS,)),
            dma((BLOCKS,)),
            dma,
            dma,
            dma((3,)),
        ],
        compiler_params=pltpu.CompilerParams(
            collective_id=0, has_side_effects=True, vmem_limit_bytes=48 * 1024 * 1024
        ),
    )(*(pltpu.with_memory_space_constraint(v, pltpu.HBM) for v in (field, lat_factor, lev_factor.T, old_factor)))


def solution(mesh):
    placed = (P(None, "lon", "lat", None), P("lat", None), P(), P("lon", None))
    return jax.shard_map(
        body, mesh=mesh, in_specs=placed, out_specs=P("lon", None), check_vma=False
    )
```

```python
import functools
import math

import jax
import jax.numpy as jnp
from jax import lax
from jax.experimental import pallas as pl
from jax.experimental.pallas import tpu as pltpu
from jax.sharding import PartitionSpec as P

MESH = pl.DeviceIdType.MESH
HIGHEST = lax.Precision.HIGHEST
F32, BF16 = jnp.float32, jnp.bfloat16
TIMES, ROWS, LATS, LEVS = 2, 48, 96, 128
RLAT, RLEV, RLON = 96, 32, 96
SLABS = 3
BLOCKS = TIMES * SLABS * 2
LOADS = (0, 16), (16, 32), (48, 48)
PART = RLON // 8
GROUPS = tuple((b, 1) for b in range(BLOCKS))
SCHEDULE = sorted(
    (first + count + lag, kind, g) for g, (first, count) in enumerate(GROUPS) for kind, lag in enumerate((0, 4.6, 11, 16))
)


def split(v):
    hi = v.astype(BF16)
    return hi, (v - hi.astype(F32)).astype(BF16)


def dot3(a, b, dims):
    (ah, al), (bh, bl) = a, b
    dot = functools.partial(lax.dot_general, dimension_numbers=(dims, ((), ())), preferred_element_type=F32)
    return dot(ah, bh) + (dot(al, bh) + dot(ah, bl))


def place():
    lon, lat = lax.axis_index("lon"), lax.axis_index("lat")
    return lat // 2, (lat % 2) * 4 + lon // 8, (lon // 2) % 4, lon % 2


def device(x, z, y, core):
    return (z % 4) * 8 + y * 2 + core, x * 2 + z // 4


def from_slots(v, to_slots):
    total = jnp.zeros_like(v)
    for _ in range(3):
        piece = v.astype(BF16)
        v = v - piece.astype(F32)
        total = total + lax.dot_general(piece, to_slots, (((1,), (1,)), ((), ())), preferred_element_type=F32)
    return total


IMAGE_ROWS = 40


def lanes_of(v):
    return lax.broadcasted_iota(jnp.int32, v.shape, 1)


def pack_image(v):
    last = v[IMAGE_ROWS:]
    tail = [pltpu.roll(last, 96 - 32 * k, 1) for k in range(3)]
    tail = jnp.concatenate(tail + [jnp.zeros((IMAGE_ROWS - 24, 128), F32)], 0)
    return jnp.where(lanes_of(tail) < RLON, v[:IMAGE_ROWS], tail)


def unpack_image(v):
    last = jnp.zeros((8, 128), F32)
    for k in range(3):
        piece = pltpu.roll(v[8 * k : 8 * k + 8], 32 + 32 * k, 1)
        last = jnp.where(lanes_of(last) // 32 == k, piece, last)
    return jnp.concatenate([jnp.where(lanes_of(v) < RLON, v, 0.0), last], 0)


def pack_gram(g):
    half = RLON // 2
    top, low = g[:half], g[half:RLON]
    lane, row = lanes_of(top), lax.broadcasted_iota(jnp.int32, top.shape, 0)
    rest = jnp.where(lane <= half, pltpu.roll(top, 1, 1), pltpu.roll(top, 16, 1))
    return jnp.where(lane <= row, pltpu.roll(low, 128 - half, 1), rest)


def unpack_top(v):
    return jnp.where(lanes_of(v) < RLON // 2, pltpu.roll(v, 127, 1), pltpu.roll(v, 112, 1))


def unpack_low(v):
    half = RLON // 2
    square = jnp.concatenate([v, jnp.zeros((128 - half, 128), F32)], 0).T
    return pltpu.roll(square[:half], half, 1)


PANEL = 16


def solve(total_rows, head, rest, image_t, out, yt):
    tiles = RLON // 8
    left = [head[8 * r : 8 * r + 8] for r in range(PANEL // 8)]
    right = [image_t[8 * r : 8 * r + 8] for r in range(tiles)]
    sub = lax.broadcasted_iota(jnp.int32, (8, 128), 0)
    diagonal = lax.broadcasted_iota(jnp.int32, (8, 128), 1) - sub
    spread = lambda v: jnp.broadcast_to(v, (8, 128))
    for j in range(RLON // PANEL):
        at, first = PANEL * j, PANEL // 8 * j
        col = [
            [spread(left[first + s][:, at + q : at + q + 1]) if q >= 8 * s else None for q in range(PANEL)]
            for s in range(PANEL // 8)
        ]
        d = [[spread(col[p // 8][q][p % 8 : p % 8 + 1]) for p in range(q + 1)] for q in range(PANEL)]
        vl = [spread(left[first + p // 8][p % 8 : p % 8 + 1]) for p in range(PANEL)]
        vr = [spread(right[first + p // 8][p % 8 : p % 8 + 1]) for p in range(PANEL)]
        for p in range(PANEL):
            inv = lax.rsqrt(d[p][p])
            for q in range(p + 1, PANEL):
                d[q][p] = d[q][p] * inv
            for q in range(p + 1, PANEL):
                for r in range(p + 1, q + 1):
                    d[q][r] = d[q][r] - d[q][p] * d[r][p]
            vl[p], vr[p] = vl[p] * inv, vr[p] * inv
            for q in range(p + 1, PANEL):
                vl[q] = vl[q] - d[q][p] * vl[p]
                vr[q] = vr[q] - d[q][p] * vr[p]
        for s in range(PANEL // 8):
            rows = vr[8 * s]
            for p in range(1, 8):
                rows = jnp.where(sub == p, vr[8 * s + p], rows)
            yt[at + 8 * s : at + 8 * s + 8] = rows
        if j == 0:
            top = rest()
            left += [top[8 * r : 8 * r + 8] for r in range(tiles - PANEL // 8)]
        for r in range(first + PANEL // 8, tiles):
            ml, mr = [], []
            for p in range(PANEL):
                c = jnp.sum(jnp.where(diagonal == 8 * r, vl[p], 0.0), axis=1, keepdims=True)
                ml.append(c * vl[p])
                mr.append(c * vr[p])
            while len(ml) > 1:
                ml = [a + b for a, b in zip(ml[::2], ml[1::2])]
                mr = [a + b for a, b in zip(mr[::2], mr[1::2])]
            left[r], right[r] = left[r] - ml[0], right[r] - mr[0]
    out[...] = yt[...].T[0:ROWS] * jnp.sqrt(F32(total_rows))


def hooi_kernel(
    total_rows, field, lat, lev_t, old, out,
    fv, lat_in, lev_in, old_in, lats, lvl, proj, xr, pz, wt, wr, ws, wz, wf, img, ir, summed, home, gp, gr, gh, go, gf,
    yt, fsem, csem, passed, sent, xsem, rsem, zsem, isem, hsem, gsem,
):
    x, z, y, core = place()
    me = y * 2 + core

    def send(src, dst, sent, landed, to):
        copy = pltpu.make_async_remote_copy(
            src_ref=src, dst_ref=dst, send_sem=sent, recv_sem=landed, device_id=to, device_id_type=MESH
        )
        copy.start()
        return copy

    def arrived(ref, sem):
        pltpu.make_async_copy(ref, ref, sem).wait()

    loads = [
        pltpu.make_async_copy(
            field.at[pl.ds(at * LATS, rows * LATS)], fv.at[pl.ds(at * LATS, rows * LATS)], fsem.at[k]
        )
        for k, (at, rows) in enumerate(LOADS)
    ]
    small = [
        pltpu.make_async_copy(src, dst, csem.at[k])
        for k, (src, dst) in enumerate(((lev_t, lev_in), (lat, lat_in), (old, old_in)))
    ]
    for load in small + loads:
        load.start()

    x_peers = [device((x + dx) % 4, z, y, core) for dx in (1, 2, 3)]
    y_peers = [device(x, z, (y + dy) % 4, core) for dy in (1, 2, 3)]
    z_peers = [device(x, (z + dz) % 8, y, core) for dz in range(1, 8)]
    yc_peers = [device(x, z, ((me + j) % 8) // 2, (me + j) % 2) for j in range(1, 8)]
    i_peers = [device((x + dx) % 4, (z + dz) % 8, y, core) for dx in range(4) for dz in (2, 6)]
    g_steps = [(dy, dz) for dy in range(4) for dz in (0, 1, 7, 2 if dy < 2 else 6)][1:]
    g_peers = [device(x, (z + dz) % 8, (y + dy) % 4, core) for dy, dz in g_steps]

    greeted = x_peers + yc_peers + [z_peers[k] for k in (1, 5, 0, 6)]
    barrier = pltpu.get_barrier_semaphore()
    for peer in greeted:
        pl.semaphore_signal(barrier, inc=1, device_id=peer, device_id_type=MESH)
    told = x_peers + y_peers + [z_peers[1], z_peers[5]]

    small[0].wait()
    small[1].wait()
    levh, levl = split(lev_in[...])
    lev2 = jnp.concatenate(
        [jnp.concatenate([levh, levh], 1), jnp.concatenate([levl, jnp.zeros_like(levl)], 1)], 0
    )
    lats[...] = jnp.zeros_like(lats)
    lats[0:LATS, 0:RLAT] = lat_in[...]
    lat_pad = lats[...]
    lane = lax.broadcasted_iota(jnp.int32, (128, 128), 1)
    lat_hi, lat_lo = [], []
    for u in range(SLABS):
        tail = jnp.where(lane >= RLAT, pltpu.roll(lat_pad, 96 - 32 * u, 1), 0.0)
        hi, lo = split(jnp.concatenate([lat_pad, tail], 0))
        lat_hi.append(hi)
        lat_lo.append(lo)

    def levels(k):
        def one(i, carry):
            f = fv[pl.ds(pl.multiple_of(i * LATS, LATS), LATS), :]
            fh, fl = split(f)
            both = jnp.concatenate([fh, fl], 1)
            both = jnp.concatenate([both, jnp.zeros((128 - LATS, 256), BF16)], 0)
            r = lax.dot_general(lev2, both, (((1,), (1,)), ((), ())), preferred_element_type=F32)
            lvl[pl.ds(lax.rem(i, ROWS), RLEV, stride=ROWS), :] = r[:RLEV] + r[RLEV:]
            return carry

        loads[k].wait()
        at, rows = LOADS[k]
        lax.fori_loop(at, at + rows, one, 0, unroll=16)

    def latitudes(t, u):
        parts = [
            jnp.concatenate([lvl[pl.ds((4 * d + v) * ROWS, ROWS), :] for d in range(8)], 0) for v in (u, 3)
        ]
        hi, lo = split(jnp.concatenate(parts, 1))
        r = (
            jnp.dot(hi, lat_hi[u], preferred_element_type=F32)
            + jnp.dot(lo, lat_hi[u], preferred_element_type=F32)
            + jnp.dot(hi, lat_lo[u], preferred_element_type=F32)
        )
        for d in range(8):
            proj[2 * (t * SLABS + u) + d % 2, d // 2] = r[d * ROWS : (d + 1) * ROWS]

    for t in range(TIMES):
        for k in ((0, 1), (2,))[t]:
            levels(k)
        for u in range(SLABS):
            latitudes(t, u)
            if t + u == 0:
                pl.semaphore_wait(barrier, len(greeted))
                for peer in told:
                    pl.semaphore_signal(passed, inc=1, device_id=peer, device_id_type=MESH)
            for g, (first, count) in enumerate(GROUPS):
                if first // 2 == t * SLABS + u:
                    blocks = pl.ds(first, count)
                    for k in range(3):
                        send(proj.at[blocks, (x + k + 1) % 4], xr.at[blocks, k], sent, xsem.at[g], x_peers[k])

    pl.semaphore_wait(passed, len(told))
    small[2].wait()
    place_of = lambda r: 16 * (r // PART) + r % PART
    to_slots = (
        place_of(lax.broadcasted_iota(jnp.int32, (128, 128), 0)) == lax.broadcasted_iota(jnp.int32, (128, 128), 1)
    ).astype(F32)
    to_slots = jnp.where(lax.broadcasted_iota(jnp.int32, (128, 128), 0) < RLON, to_slots, 0.0)
    old_t = jnp.dot(old_in[...], to_slots[:RLON], precision=HIGHEST, preferred_element_type=F32)
    old_t = split(old_t.T)
    to_slots = to_slots.astype(BF16)
    wf[...] = jnp.zeros_like(wf)
    acc = jnp.zeros((ROWS, 128), F32)

    for at, kind, g in SCHEDULE:
        first, count = GROUPS[g]
        blocks = pl.ds(first, count)
        if kind == 0:
            arrived(xr.at[blocks], xsem.at[g])
            for b in range(first, first + count):
                pz[b] = proj[b, x] + xr[b, 0] + xr[b, 1] + xr[b, 2]
                part = dot3(old_t, split(pz[b]), ((1,), (0,)))
                for k in range(8):
                    wt[b, k] = part[16 * k : 16 * k + PART]
            for k in range(7):
                send(wt.at[blocks, (me + k + 1) % 8], wr.at[blocks, k], sent, rsem.at[g], yc_peers[k])
        elif kind == 1:
            arrived(wr.at[blocks], rsem.at[g])
            for b in range(first, first + count):
                part = wt[b, me]
                for k in range(7):
                    part = part + wr[b, k]
                ws[b] = part
            for k in range(7):
                send(ws.at[blocks], wz.at[blocks, k], sent, zsem.at[g], z_peers[k])
        elif kind == 2:
            arrived(wz.at[blocks], zsem.at[g])
            for b in range(first, first + count):
                part = ws[b]
                for k in range(7):
                    part = part + wz[b, k]
                wf[b, me, 0:PART] = part
            mine = wf.at[blocks, me, pl.ds(0, PART)]
            for k in range(7):
                send(mine, mine, sent, xsem.at[g], yc_peers[k])
        else:
            arrived(wr.at[blocks], xsem.at[g])
            for b in range(first, first + count):
                acc = acc + dot3(split(pz[b]), split(wf[b].reshape(128, 128)), ((1,), (1,)))
    img[...] = pack_image(from_slots(acc, to_slots))
    for k in range(8):
        send(img, ir.at[k], sent, isem, i_peers[k])
    arrived(ir, isem)
    image = ir[0]
    for k in range(1, 8):
        image = image + ir[k]
    image = unpack_image(image)
    summed[...] = image
    send(summed, home, sent, hsem, z_peers[1])
    gp[...] = pack_gram(
        lax.dot_general(image, image, (((0,), (0,)), ((), ())), precision=HIGHEST, preferred_element_type=F32)
    )
    half = RLON // 4
    sibling = device(x, z, y, 1 - core)
    mine, other = (pl.ds(pl.multiple_of(half * c, 8), half) for c in (1 - core, core))
    send(gp.at[other], gr, sent, gsem.at[0], sibling)
    arrived(gr, gsem.at[0])
    gh[...] = gp[mine] + gr[...]
    for k in range(15):
        send(gh, go.at[k], sent, gsem.at[1], g_peers[k])
    arrived(home, hsem)
    image_t = jnp.concatenate([home[...].T[0:RLON], jnp.zeros((RLON, 128 - ROWS), F32)], 1)
    arrived(go, gsem.at[1])
    total = gh[...]
    for k in range(15):
        total = total + go[k]
    gf[mine] = total
    send(gf.at[mine], gf.at[mine], sent, gsem.at[2], sibling)

    @pl.when(core == 0)
    def _():
        arrived(gr, gsem.at[2])

    def rest():
        @pl.when(core == 1)
        def _():
            arrived(gr, gsem.at[2])

        return jnp.concatenate([unpack_top(gf[PANEL:]), unpack_low(gf[...])], 0)

    solve(total_rows, unpack_top(gf[0:PANEL]), rest, image_t, out, yt)

    refs = (xr, wr, wz, wr, ir, home, gr, go, gr)
    arrived(fv.at[pl.ds(0, sum(math.prod(ref.shape) // 128 for ref in refs))], sent)


def body(field, lat_factor, lev_factor, old_factor):
    vmem = pl.BlockSpec(memory_space=pltpu.VMEM)
    dma = pltpu.SemaphoreType.DMA
    field = field.reshape(TIMES * ROWS * LATS, LEVS)
    total_rows = ROWS * lax.axis_size("lon")
    return pl.pallas_call(
        functools.partial(hooi_kernel, total_rows),
        out_shape=pltpu.VMEM((ROWS, RLON), F32),
        in_specs=[pl.BlockSpec(memory_space=pltpu.HBM)] * 4,
        out_specs=vmem,
        scratch_shapes=[
            pltpu.VMEM((TIMES * ROWS * LATS, LEVS), F32),
            pltpu.VMEM((LATS, RLAT), F32),
            pltpu.VMEM((RLEV, LEVS), F32),
            pltpu.VMEM((ROWS, RLON), F32),
            pltpu.VMEM((128, 128), F32),
            pltpu.VMEM((RLEV * ROWS, 128), F32),
            pltpu.VMEM((BLOCKS, 4, ROWS, 128), F32),
            pltpu.VMEM((BLOCKS, 3, ROWS, 128), F32),
            pltpu.VMEM((BLOCKS, ROWS, 128), F32),
            pltpu.VMEM((BLOCKS, 8, PART, 128), F32),
            pltpu.VMEM((BLOCKS, 7, PART, 128), F32),
            pltpu.VMEM((BLOCKS, PART, 128), F32),
            pltpu.VMEM((BLOCKS, 7, PART, 128), F32),
            pltpu.VMEM((BLOCKS, 8, 16, 128), F32),
            pltpu.VMEM((IMAGE_ROWS, 128), F32),
            pltpu.VMEM((8, IMAGE_ROWS, 128), F32),
            pltpu.VMEM((ROWS, 128), F32),
            pltpu.VMEM((ROWS, 128), F32),
            pltpu.VMEM((RLON // 2, 128), F32),
            pltpu.VMEM((RLON // 4, 128), F32),
            pltpu.VMEM((RLON // 4, 128), F32),
            pltpu.VMEM((15, RLON // 4, 128), F32),
            pltpu.VMEM((RLON // 2, 128), F32),
            pltpu.VMEM((RLON, 128), F32),
            dma((3,)),
            dma((3,)),
            pltpu.SemaphoreType.REGULAR,
            dma,
            dma((len(GROUPS),)),
            dma((len(GROUPS),)),
            dma((len(GROUPS),)),
            dma,
            dma,
            dma((3,)),
        ],
        compiler_params=pltpu.CompilerParams(
            collective_id=0, has_side_effects=True, vmem_limit_bytes=48 * 1024 * 1024
        ),
    )(*(pltpu.with_memory_space_constraint(v, pltpu.HBM) for v in (field, lat_factor, lev_factor.T, old_factor)))


def solution(mesh):
    placed = (P(None, "lon", "lat", None), P("lat", None), P(), P("lon", None))
    return jax.shard_map(
        body, mesh=mesh, in_specs=placed, out_specs=P("lon", None), check_vma=False
    )
```

```python
import functools
import math

import jax
import jax.numpy as jnp
from jax import lax
from jax.experimental import pallas as pl
from jax.experimental.pallas import tpu as pltpu
from jax.sharding import PartitionSpec as P

MESH = pl.DeviceIdType.MESH
HIGHEST = lax.Precision.HIGHEST
F32, BF16 = jnp.float32, jnp.bfloat16
TIMES, ROWS, LATS, LEVS = 2, 48, 96, 128
RLAT, RLEV, RLON = 96, 32, 96
SLABS = 3
BLOCKS = TIMES * SLABS * 2
LOADS = (0, 16), (16, 32), (48, 48)
FAR_FIRST = (3, 2, 4, 1, 5, 0, 6)
PART = RLON // 8
GROUPS = tuple((b, 1) for b in range(BLOCKS))
SCHEDULE = sorted(
    (first + count + lag, kind, g) for g, (first, count) in enumerate(GROUPS) for kind, lag in enumerate((0, 4.6, 11, 16))
)


def split(v):
    hi = v.astype(BF16)
    return hi, (v - hi.astype(F32)).astype(BF16)


def dot3(a, b, dims):
    (ah, al), (bh, bl) = a, b
    dot = functools.partial(lax.dot_general, dimension_numbers=(dims, ((), ())), preferred_element_type=F32)
    return dot(ah, bh) + (dot(al, bh) + dot(ah, bl))


def place():
    lon, lat = lax.axis_index("lon"), lax.axis_index("lat")
    return lat // 2, (lat % 2) * 4 + lon // 8, (lon // 2) % 4, lon % 2


def device(x, z, y, core):
    return (z % 4) * 8 + y * 2 + core, x * 2 + z // 4


IMAGE_ROWS = 40


def lanes_of(v):
    return lax.broadcasted_iota(jnp.int32, v.shape, 1)


def pack_image(v):
    last = v[IMAGE_ROWS:]
    tail = [pltpu.roll(last, 96 - 32 * k, 1) for k in range(3)]
    tail = jnp.concatenate(tail + [jnp.zeros((IMAGE_ROWS - 24, 128), F32)], 0)
    return jnp.where(lanes_of(tail) < RLON, v[:IMAGE_ROWS], tail)


def unpack_image(v):
    last = jnp.zeros((8, 128), F32)
    for k in range(3):
        piece = pltpu.roll(v[8 * k : 8 * k + 8], 32 + 32 * k, 1)
        last = jnp.where(lanes_of(last) // 32 == k, piece, last)
    return jnp.concatenate([jnp.where(lanes_of(v) < RLON, v, 0.0), last], 0)


def pack_gram(g):
    half = RLON // 2
    top, low = g[:half], g[half:RLON]
    lane, row = lanes_of(top), lax.broadcasted_iota(jnp.int32, top.shape, 0)
    rest = jnp.where(lane <= half, pltpu.roll(top, 1, 1), pltpu.roll(top, 16, 1))
    return jnp.where(lane <= row, pltpu.roll(low, 128 - half, 1), rest)


def unpack_top(v):
    return jnp.where(lanes_of(v) < RLON // 2, pltpu.roll(v, 127, 1), pltpu.roll(v, 112, 1))


def unpack_low(v):
    half = RLON // 2
    square = jnp.concatenate([v, jnp.zeros((128 - half, 128), F32)], 0).T
    return pltpu.roll(square[:half], half, 1)


PANEL = 16


def solve(total_rows, head, rest, image_t, out, yt):
    tiles = RLON // 8
    left = [head[8 * r : 8 * r + 8] for r in range(PANEL // 8)]
    right = [image_t[8 * r : 8 * r + 8] for r in range(tiles)]
    sub = lax.broadcasted_iota(jnp.int32, (8, 128), 0)
    diagonal = lax.broadcasted_iota(jnp.int32, (8, 128), 1) - sub
    spread = lambda v: jnp.broadcast_to(v, (8, 128))
    for j in range(RLON // PANEL):
        at, first = PANEL * j, PANEL // 8 * j
        col = [
            [spread(left[first + s][:, at + q : at + q + 1]) if q >= 8 * s else None for q in range(PANEL)]
            for s in range(PANEL // 8)
        ]
        d = [[spread(col[p // 8][q][p % 8 : p % 8 + 1]) for p in range(q + 1)] for q in range(PANEL)]
        vl = [spread(left[first + p // 8][p % 8 : p % 8 + 1]) for p in range(PANEL)]
        vr = [spread(right[first + p // 8][p % 8 : p % 8 + 1]) for p in range(PANEL)]
        for p in range(PANEL):
            inv = lax.rsqrt(d[p][p])
            for q in range(p + 1, PANEL):
                d[q][p] = d[q][p] * inv
            for q in range(p + 1, PANEL):
                for r in range(p + 1, q + 1):
                    d[q][r] = d[q][r] - d[q][p] * d[r][p]
            vl[p], vr[p] = vl[p] * inv, vr[p] * inv
            for q in range(p + 1, PANEL):
                vl[q] = vl[q] - d[q][p] * vl[p]
                vr[q] = vr[q] - d[q][p] * vr[p]
        for s in range(PANEL // 8):
            rows = vr[8 * s]
            for p in range(1, 8):
                rows = jnp.where(sub == p, vr[8 * s + p], rows)
            yt[at + 8 * s : at + 8 * s + 8] = rows
        if j == 0:
            top = rest()
            left += [top[8 * r : 8 * r + 8] for r in range(tiles - PANEL // 8)]
        for r in range(first + PANEL // 8, tiles):
            ml, mr = [], []
            for p in range(PANEL):
                c = jnp.sum(jnp.where(diagonal == 8 * r, vl[p], 0.0), axis=1, keepdims=True)
                ml.append(c * vl[p])
                mr.append(c * vr[p])
            while len(ml) > 1:
                ml = [a + b for a, b in zip(ml[::2], ml[1::2])]
                mr = [a + b for a, b in zip(mr[::2], mr[1::2])]
            left[r], right[r] = left[r] - ml[0], right[r] - mr[0]
    out[...] = yt[...].T[0:ROWS] * jnp.sqrt(F32(total_rows))


def hooi_kernel(
    total_rows, field, lat, lev_t, old, out,
    fv, lat_in, lev_in, old_in, lats, lvl, proj, xr, pz, wt, wr, ws, wz, wf, img, ir, summed, home, gp, gr, gh, go, gf,
    yt, fsem, csem, passed, sent, xsem, rsem, zsem, isem, hsem, gsem,
):
    x, z, y, core = place()
    me = y * 2 + core

    def send(src, dst, sent, landed, to):
        copy = pltpu.make_async_remote_copy(
            src_ref=src, dst_ref=dst, send_sem=sent, recv_sem=landed, device_id=to, device_id_type=MESH
        )
        copy.start()
        return copy

    def arrived(ref, sem):
        pltpu.make_async_copy(ref, ref, sem).wait()

    loads = [
        pltpu.make_async_copy(
            field.at[pl.ds(at * LATS, rows * LATS)], fv.at[pl.ds(at * LATS, rows * LATS)], fsem.at[k]
        )
        for k, (at, rows) in enumerate(LOADS)
    ]
    small = [
        pltpu.make_async_copy(src, dst, csem.at[k])
        for k, (src, dst) in enumerate(((lev_t, lev_in), (lat, lat_in), (old, old_in)))
    ]
    for load in small + loads:
        load.start()

    x_peers = [device((x + dx) % 4, z, y, core) for dx in (1, 2, 3)]
    y_peers = [device(x, z, (y + dy) % 4, core) for dy in (1, 2, 3)]
    z_peers = [device(x, (z + dz) % 8, y, core) for dz in range(1, 8)]
    yc_peers = [device(x, z, ((me + j) % 8) // 2, (me + j) % 2) for j in range(1, 8)]
    i_peers = [device((x + dx) % 4, (z + dz) % 8, y, core) for dx in (2, 1, 3, 0) for dz in (2, 6)]
    g_steps = [(dy, dz) for dy in range(4) for dz in (0, 1, 7, 2 if dy < 2 else 6)][1:]
    g_steps.sort(key=lambda step: -min(step[0], 4 - step[0]) - min(step[1], 8 - step[1]))
    g_peers = [device(x, (z + dz) % 8, (y + dy) % 4, core) for dy, dz in g_steps]

    greeted = x_peers + yc_peers + [z_peers[k] for k in (1, 5, 0, 6)]
    barrier = pltpu.get_barrier_semaphore()
    for peer in greeted:
        pl.semaphore_signal(barrier, inc=1, device_id=peer, device_id_type=MESH)
    told = x_peers + y_peers + [z_peers[1], z_peers[5]]

    small[0].wait()
    small[1].wait()
    levh, levl = split(lev_in[...])
    lev2 = jnp.concatenate(
        [jnp.concatenate([levh, levh], 1), jnp.concatenate([levl, jnp.zeros_like(levl)], 1)], 0
    )
    lats[...] = jnp.zeros_like(lats)
    lats[0:LATS, 0:RLAT] = lat_in[...]
    lat_pad = lats[...]
    lane = lax.broadcasted_iota(jnp.int32, (128, 128), 1)
    lat_hi, lat_lo = [], []
    for u in range(SLABS):
        tail = jnp.where(lane >= RLAT, pltpu.roll(lat_pad, 96 - 32 * u, 1), 0.0)
        hi, lo = split(jnp.concatenate([lat_pad, tail], 0))
        lat_hi.append(hi)
        lat_lo.append(lo)

    def levels(k):
        def one(i, carry):
            f = fv[pl.ds(pl.multiple_of(i * LATS, LATS), LATS), :]
            fh, fl = split(f)
            both = jnp.concatenate([fh, fl], 1)
            both = jnp.concatenate([both, jnp.zeros((128 - LATS, 256), BF16)], 0)
            r = lax.dot_general(lev2, both, (((1,), (1,)), ((), ())), preferred_element_type=F32)
            lvl[pl.ds(lax.rem(i, ROWS), RLEV, stride=ROWS), :] = r[:RLEV] + r[RLEV:]
            return carry

        loads[k].wait()
        at, rows = LOADS[k]
        lax.fori_loop(at, at + rows, one, 0, unroll=16)

    def latitudes(t, u):
        parts = [
            jnp.concatenate([lvl[pl.ds((4 * d + v) * ROWS, ROWS), :] for d in range(8)], 0) for v in (u, 3)
        ]
        hi, lo = split(jnp.concatenate(parts, 1))
        r = (
            jnp.dot(hi, lat_hi[u], preferred_element_type=F32)
            + jnp.dot(lo, lat_hi[u], preferred_element_type=F32)
            + jnp.dot(hi, lat_lo[u], preferred_element_type=F32)
        )
        for d in range(8):
            proj[2 * (t * SLABS + u) + d % 2, d // 2] = r[d * ROWS : (d + 1) * ROWS]

    for t in range(TIMES):
        for k in ((0, 1), (2,))[t]:
            levels(k)
        for u in range(SLABS):
            latitudes(t, u)
            if t + u == 0:
                pl.semaphore_wait(barrier, len(greeted))
                for peer in told:
                    pl.semaphore_signal(passed, inc=1, device_id=peer, device_id_type=MESH)
            for g, (first, count) in enumerate(GROUPS):
                if first // 2 == t * SLABS + u:
                    blocks = pl.ds(first, count)
                    for k in (1, 0, 2):
                        send(proj.at[blocks, (x + k + 1) % 4], xr.at[blocks, k], sent, xsem.at[g], x_peers[k])

    pl.semaphore_wait(passed, len(told))
    small[2].wait()
    old_t = split(old_in[...].T)
    acc = jnp.zeros((ROWS, RLON), F32)

    for at, kind, g in SCHEDULE:
        first, count = GROUPS[g]
        blocks = pl.ds(first, count)
        if kind == 0:
            arrived(xr.at[blocks], xsem.at[g])
            for b in range(first, first + count):
                pz[b] = proj[b, x] + xr[b, 0] + xr[b, 1] + xr[b, 2]
                wt[b] = dot3(old_t, split(pz[b]), ((1,), (0,)))
            for k in FAR_FIRST:
                part = pl.ds(PART * ((me + k + 1) % 8), PART)
                send(wt.at[blocks, part], wr.at[blocks, k], sent, rsem.at[g], yc_peers[k])
        elif kind == 1:
            arrived(wr.at[blocks], rsem.at[g])
            for b in range(first, first + count):
                part = wt[b, pl.ds(PART * me, PART)]
                for k in range(7):
                    part = part + wr[b, k]
                ws[b] = part
            for k in FAR_FIRST:
                send(ws.at[blocks], wz.at[blocks, k], sent, zsem.at[g], z_peers[k])
        elif kind == 2:
            arrived(wz.at[blocks], zsem.at[g])
            for b in range(first, first + count):
                part = ws[b]
                for k in range(7):
                    part = part + wz[b, k]
                wf[b, pl.ds(PART * me, PART)] = part
            mine = wf.at[blocks, pl.ds(PART * me, PART)]
            for k in FAR_FIRST:
                send(mine, mine, sent, xsem.at[g], yc_peers[k])
        else:
            arrived(wr.at[blocks], xsem.at[g])
            for b in range(first, first + count):
                acc = acc + dot3(split(pz[b]), split(wf[b]), ((1,), (1,)))
    img[...] = pack_image(jnp.concatenate([acc, jnp.zeros((ROWS, 128 - RLON), F32)], 1))
    for k in range(8):
        send(img, ir.at[k], sent, isem, i_peers[k])
    arrived(ir, isem)
    image = ir[0]
    for k in range(1, 8):
        image = image + ir[k]
    image = unpack_image(image)
    summed[...] = image
    send(summed, home, sent, hsem, z_peers[1])
    gp[...] = pack_gram(
        lax.dot_general(image, image, (((0,), (0,)), ((), ())), precision=HIGHEST, preferred_element_type=F32)
    )
    half = RLON // 4
    sibling = device(x, z, y, 1 - core)
    mine, other = (pl.ds(pl.multiple_of(half * c, 8), half) for c in (1 - core, core))
    send(gp.at[other], gr, sent, gsem.at[0], sibling)
    arrived(gr, gsem.at[0])
    gh[...] = gp[mine] + gr[...]
    for k in range(15):
        send(gh, go.at[k], sent, gsem.at[1], g_peers[k])
    arrived(home, hsem)
    image_t = jnp.concatenate([home[...].T[0:RLON], jnp.zeros((RLON, 128 - ROWS), F32)], 1)
    arrived(go, gsem.at[1])
    total = gh[...]
    for k in range(15):
        total = total + go[k]
    gf[mine] = total
    send(gf.at[mine], gf.at[mine], sent, gsem.at[2], sibling)

    @pl.when(core == 0)
    def _():
        arrived(gr, gsem.at[2])

    def rest():
        @pl.when(core == 1)
        def _():
            arrived(gr, gsem.at[2])

        return jnp.concatenate([unpack_top(gf[PANEL:]), unpack_low(gf[...])], 0)

    solve(total_rows, unpack_top(gf[0:PANEL]), rest, image_t, out, yt)

    refs = (xr, wr, wz, wr, ir, home, gr, go, gr)
    arrived(fv.at[pl.ds(0, sum(math.prod(ref.shape) // 128 for ref in refs))], sent)


def body(field, lat_factor, lev_factor, old_factor):
    vmem = pl.BlockSpec(memory_space=pltpu.VMEM)
    dma = pltpu.SemaphoreType.DMA
    field = field.reshape(TIMES * ROWS * LATS, LEVS)
    total_rows = ROWS * lax.axis_size("lon")
    return pl.pallas_call(
        functools.partial(hooi_kernel, total_rows),
        out_shape=pltpu.VMEM((ROWS, RLON), F32),
        in_specs=[pl.BlockSpec(memory_space=pltpu.HBM)] * 4,
        out_specs=vmem,
        scratch_shapes=[
            pltpu.VMEM((TIMES * ROWS * LATS, LEVS), F32),
            pltpu.VMEM((LATS, RLAT), F32),
            pltpu.VMEM((RLEV, LEVS), F32),
            pltpu.VMEM((ROWS, RLON), F32),
            pltpu.VMEM((128, 128), F32),
            pltpu.VMEM((RLEV * ROWS, 128), F32),
            pltpu.VMEM((BLOCKS, 4, ROWS, 128), F32),
            pltpu.VMEM((BLOCKS, 3, ROWS, 128), F32),
            pltpu.VMEM((BLOCKS, ROWS, 128), F32),
            pltpu.VMEM((BLOCKS, RLON, 128), F32),
            pltpu.VMEM((BLOCKS, 7, PART, 128), F32),
            pltpu.VMEM((BLOCKS, PART, 128), F32),
            pltpu.VMEM((BLOCKS, 7, PART, 128), F32),
            pltpu.VMEM((BLOCKS, RLON, 128), F32),
            pltpu.VMEM((IMAGE_ROWS, 128), F32),
            pltpu.VMEM((8, IMAGE_ROWS, 128), F32),
            pltpu.VMEM((ROWS, 128), F32),
            pltpu.VMEM((ROWS, 128), F32),
            pltpu.VMEM((RLON // 2, 128), F32),
            pltpu.VMEM((RLON // 4, 128), F32),
            pltpu.VMEM((RLON // 4, 128), F32),
            pltpu.VMEM((15, RLON // 4, 128), F32),
            pltpu.VMEM((RLON // 2, 128), F32),
            pltpu.VMEM((RLON, 128), F32),
            dma((3,)),
            dma((3,)),
            pltpu.SemaphoreType.REGULAR,
            dma,
            dma((len(GROUPS),)),
            dma((len(GROUPS),)),
            dma((len(GROUPS),)),
            dma,
            dma,
            dma((3,)),
        ],
        compiler_params=pltpu.CompilerParams(
            collective_id=0, has_side_effects=True, vmem_limit_bytes=48 * 1024 * 1024
        ),
    )(*(pltpu.with_memory_space_constraint(v, pltpu.HBM) for v in (field, lat_factor, lev_factor.T, old_factor)))


def solution(mesh):
    placed = (P(None, "lon", "lat", None), P("lat", None), P(), P("lon", None))
    return jax.shard_map(
        body, mesh=mesh, in_specs=placed, out_specs=P("lon", None), check_vma=False
    )
```

```python
import functools
import math

import jax
import jax.numpy as jnp
from jax import lax
from jax.experimental import pallas as pl
from jax.experimental.pallas import tpu as pltpu
from jax.sharding import PartitionSpec as P

MESH = pl.DeviceIdType.MESH
HIGHEST = lax.Precision.HIGHEST
F32, BF16 = jnp.float32, jnp.bfloat16
TIMES, ROWS, LATS, LEVS = 2, 48, 96, 128
RLAT, RLEV, RLON = 96, 32, 96
SLABS = 3
BLOCKS = TIMES * SLABS * 2
LOADS = (0, 16), (16, 32), (48, 48)
FAR_FIRST = (3, 2, 4, 1, 5, 0, 6)
PART = RLON // 8
GROUPS = tuple((b, 1) for b in range(BLOCKS))
SCHEDULE = sorted(
    (first + count + lag, kind, g) for g, (first, count) in enumerate(GROUPS) for kind, lag in enumerate((0, 4.6, 11, 16))
)


def split(v):
    hi = v.astype(BF16)
    return hi, (v - hi.astype(F32)).astype(BF16)


def dot3(a, b, dims):
    (ah, al), (bh, bl) = a, b
    dot = functools.partial(lax.dot_general, dimension_numbers=(dims, ((), ())), preferred_element_type=F32)
    return dot(ah, bh) + (dot(al, bh) + dot(ah, bl))


def place():
    lon, lat = lax.axis_index("lon"), lax.axis_index("lat")
    return lat // 2, (lat % 2) * 4 + lon // 8, (lon // 2) % 4, lon % 2


def device(x, z, y, core):
    return (z % 4) * 8 + y * 2 + core, x * 2 + z // 4


IMAGE_ROWS = 40


def lanes_of(v):
    return lax.broadcasted_iota(jnp.int32, v.shape, 1)


def pack_image(v):
    last = v[IMAGE_ROWS:]
    tail = [pltpu.roll(last, 96 - 32 * k, 1) for k in range(3)]
    tail = jnp.concatenate(tail + [jnp.zeros((IMAGE_ROWS - 24, 128), F32)], 0)
    return jnp.where(lanes_of(tail) < RLON, v[:IMAGE_ROWS], tail)


def unpack_image(v):
    last = jnp.zeros((8, 128), F32)
    for k in range(3):
        piece = pltpu.roll(v[8 * k : 8 * k + 8], 32 + 32 * k, 1)
        last = jnp.where(lanes_of(last) // 32 == k, piece, last)
    return jnp.concatenate([jnp.where(lanes_of(v) < RLON, v, 0.0), last], 0)


def pack_gram(g):
    half = RLON // 2
    top, low = g[:half], g[half:RLON]
    lane, row = lanes_of(top), lax.broadcasted_iota(jnp.int32, top.shape, 0)
    rest = jnp.where(lane <= half, pltpu.roll(top, 1, 1), pltpu.roll(top, 16, 1))
    return jnp.where(lane <= row, pltpu.roll(low, 128 - half, 1), rest)


def unpack_top(v):
    return jnp.where(lanes_of(v) < RLON // 2, pltpu.roll(v, 127, 1), pltpu.roll(v, 112, 1))


def unpack_low(v):
    half = RLON // 2
    square = jnp.concatenate([v, jnp.zeros((128 - half, 128), F32)], 0).T
    return pltpu.roll(square[:half], half, 1)


HEAD = 16


def tree_sum(terms):
    while len(terms) > 1:
        terms = [a + b for a, b in zip(terms[::2], terms[1::2])]
    return terms[0]


def solve(total_rows, head, rest, image_t, out, yt):
    tiles = RLON // 8
    left = [head[8 * r : 8 * r + 8] for r in range(HEAD // 8)]
    right = [image_t[8 * r : 8 * r + 8] for r in range(tiles)]
    sub = lax.broadcasted_iota(jnp.int32, (8, 128), 0)
    diagonal = lax.broadcasted_iota(jnp.int32, (8, 128), 1) - sub
    spread = lambda v: jnp.broadcast_to(v, (8, 128))

    def down(row, r):
        return spread(jnp.sum(jnp.where(diagonal == 8 * r, row, 0.0), axis=1, keepdims=True))

    col = [spread(left[0][:, q : q + 1]) for q in range(8)]
    for j in range(tiles):
        at = 8 * j
        d = [[spread(col[q][p : p + 1]) for p in range(q + 1)] for q in range(8)]
        vl = [spread(left[j][p : p + 1]) for p in range(8)]
        vr = [spread(right[j][p : p + 1]) for p in range(8)]
        if j + 1 < tiles:
            col = [spread(left[j + 1][:, at + 8 + q : at + 9 + q]) for q in range(8)]
            m = [down(vl[p], j + 1) for p in range(8)]
        else:
            m = [jnp.zeros((8, 128), F32)] * 8
        for p in range(8):
            inv = lax.rsqrt(d[p][p])
            for q in range(p + 1, 8):
                d[q][p] = d[q][p] * inv
            for q in range(p + 1, 8):
                for r in range(p + 1, q + 1):
                    d[q][r] = d[q][r] - d[q][p] * d[r][p]
            vl[p], vr[p], m[p] = vl[p] * inv, vr[p] * inv, m[p] * inv
            for q in range(p + 1, 8):
                vl[q] = vl[q] - d[q][p] * vl[p]
                vr[q] = vr[q] - d[q][p] * vr[p]
                m[q] = m[q] - d[q][p] * m[p]
        rows = vr[0]
        for p in range(1, 8):
            rows = jnp.where(sub == p, vr[p], rows)
        yt[at : at + 8] = rows
        if j == 0:
            more = rest()
            left += [more[8 * r : 8 * r + 8] for r in range(tiles - HEAD // 8)]
        for r in range(j + 1, tiles):
            if r == j + 1:
                col = [col[q] - tree_sum([m[p] * spread(m[p][q : q + 1]) for p in range(8)]) for q in range(8)]
            else:
                m = [down(vl[p], r) for p in range(8)]
            left[r] = left[r] - tree_sum([m[p] * vl[p] for p in range(8)])
            right[r] = right[r] - tree_sum([m[p] * vr[p] for p in range(8)])
    out[...] = yt[...].T[0:ROWS] * jnp.sqrt(F32(total_rows))


def hooi_kernel(
    total_rows, field, lat, lev_t, old, out,
    fv, lat_in, lev_in, old_in, lats, lvl, proj, xr, pz, wt, wr, ws, wz, wf, img, ir, summed, home, gp, gr, gh, go, gf,
    yt, fsem, csem, passed, sent, xsem, rsem, zsem, isem, hsem, gsem,
):
    x, z, y, core = place()
    me = y * 2 + core

    def send(src, dst, sent, landed, to):
        copy = pltpu.make_async_remote_copy(
            src_ref=src, dst_ref=dst, send_sem=sent, recv_sem=landed, device_id=to, device_id_type=MESH
        )
        copy.start()
        return copy

    def arrived(ref, sem):
        pltpu.make_async_copy(ref, ref, sem).wait()

    loads = [
        pltpu.make_async_copy(
            field.at[pl.ds(at * LATS, rows * LATS)], fv.at[pl.ds(at * LATS, rows * LATS)], fsem.at[k]
        )
        for k, (at, rows) in enumerate(LOADS)
    ]
    small = [
        pltpu.make_async_copy(src, dst, csem.at[k])
        for k, (src, dst) in enumerate(((lev_t, lev_in), (lat, lat_in), (old, old_in)))
    ]
    for load in small + loads:
        load.start()

    x_peers = [device((x + dx) % 4, z, y, core) for dx in (1, 2, 3)]
    z_peers = [device(x, (z + dz) % 8, y, core) for dz in range(1, 8)]
    yc_peers = [device(x, z, ((me + j) % 8) // 2, (me + j) % 2) for j in range(1, 8)]
    i_peers = [device((x + dx) % 4, (z + dz) % 8, y, core) for dx in (2, 1, 3, 0) for dz in (2, 6)]
    g_steps = [(dy, dz) for dy in range(4) for dz in (0, 1, 7, 2 if dy < 2 else 6)][1:]
    g_steps.sort(key=lambda step: -min(step[0], 4 - step[0]) - min(step[1], 8 - step[1]))
    g_peers = [device(x, (z + dz) % 8, (y + dy) % 4, core) for dy, dz in g_steps]

    greeted = x_peers + yc_peers + [z_peers[k] for k in (1, 5, 0, 6)]
    barrier = pltpu.get_barrier_semaphore()
    for peer in greeted:
        pl.semaphore_signal(barrier, inc=1, device_id=peer, device_id_type=MESH)
    told = [z_peers[1], z_peers[5]]

    small[0].wait()
    small[1].wait()
    levh, levl = split(lev_in[...])
    lev2 = jnp.concatenate(
        [jnp.concatenate([levh, levh], 1), jnp.concatenate([levl, jnp.zeros_like(levl)], 1)], 0
    )
    lats[...] = jnp.zeros_like(lats)
    lats[0:LATS, 0:RLAT] = lat_in[...]
    lat_pad = lats[...]
    lane = lax.broadcasted_iota(jnp.int32, (128, 128), 1)
    lat_hi, lat_lo = [], []
    for u in range(SLABS):
        tail = jnp.where(lane >= RLAT, pltpu.roll(lat_pad, 96 - 32 * u, 1), 0.0)
        hi, lo = split(jnp.concatenate([lat_pad, tail], 0))
        lat_hi.append(hi)
        lat_lo.append(lo)

    def levels(k):
        def one(i, carry):
            f = fv[pl.ds(pl.multiple_of(i * LATS, LATS), LATS), :]
            fh, fl = split(f)
            both = jnp.concatenate([fh, fl], 1)
            both = jnp.concatenate([both, jnp.zeros((128 - LATS, 256), BF16)], 0)
            r = lax.dot_general(lev2, both, (((1,), (1,)), ((), ())), preferred_element_type=F32)
            lvl[pl.ds(lax.rem(i, ROWS), RLEV, stride=ROWS), :] = r[:RLEV] + r[RLEV:]
            return carry

        loads[k].wait()
        at, rows = LOADS[k]
        lax.fori_loop(at, at + rows, one, 0, unroll=16)

    def latitudes(t, u):
        parts = [
            jnp.concatenate([lvl[pl.ds((4 * d + v) * ROWS, ROWS), :] for d in range(8)], 0) for v in (u, 3)
        ]
        hi, lo = split(jnp.concatenate(parts, 1))
        r = (
            jnp.dot(hi, lat_hi[u], preferred_element_type=F32)
            + jnp.dot(lo, lat_hi[u], preferred_element_type=F32)
            + jnp.dot(hi, lat_lo[u], preferred_element_type=F32)
        )
        for d in range(8):
            proj[2 * (t * SLABS + u) + d % 2, d // 2] = r[d * ROWS : (d + 1) * ROWS]

    for t in range(TIMES):
        for k in ((0, 1), (2,))[t]:
            levels(k)
        for u in range(SLABS):
            latitudes(t, u)
            if t + u == 0:
                pl.semaphore_wait(barrier, len(greeted))
                for peer in told:
                    pl.semaphore_signal(passed, inc=1, device_id=peer, device_id_type=MESH)
            for g, (first, count) in enumerate(GROUPS):
                if first // 2 == t * SLABS + u:
                    blocks = pl.ds(first, count)
                    for k in (1, 0, 2):
                        send(proj.at[blocks, (x + k + 1) % 4], xr.at[blocks, k], sent, xsem.at[g], x_peers[k])

    pl.semaphore_wait(passed, len(told))
    small[2].wait()
    old_t = split(old_in[...].T)
    acc = jnp.zeros((ROWS, RLON), F32)

    for at, kind, g in SCHEDULE:
        first, count = GROUPS[g]
        blocks = pl.ds(first, count)
        if kind == 0:
            arrived(xr.at[blocks], xsem.at[g])
            for b in range(first, first + count):
                pz[b] = proj[b, x] + xr[b, 0] + xr[b, 1] + xr[b, 2]
                wt[b] = dot3(old_t, split(pz[b]), ((1,), (0,)))
            for k in FAR_FIRST:
                part = pl.ds(PART * ((me + k + 1) % 8), PART)
                send(wt.at[blocks, part], wr.at[blocks, k], sent, rsem.at[g], yc_peers[k])
        elif kind == 1:
            arrived(wr.at[blocks], rsem.at[g])
            for b in range(first, first + count):
                part = wt[b, pl.ds(PART * me, PART)]
                for k in range(7):
                    part = part + wr[b, k]
                ws[b] = part
            for k in FAR_FIRST:
                send(ws.at[blocks], wz.at[blocks, k], sent, zsem.at[g], z_peers[k])
        elif kind == 2:
            arrived(wz.at[blocks], zsem.at[g])
            for b in range(first, first + count):
                part = ws[b]
                for k in range(7):
                    part = part + wz[b, k]
                wf[b, pl.ds(PART * me, PART)] = part
            mine = wf.at[blocks, pl.ds(PART * me, PART)]
            for k in FAR_FIRST:
                send(mine, mine, sent, xsem.at[g], yc_peers[k])
        else:
            arrived(wr.at[blocks], xsem.at[g])
            for b in range(first, first + count):
                acc = acc + dot3(split(pz[b]), split(wf[b]), ((1,), (1,)))
    img[...] = pack_image(jnp.concatenate([acc, jnp.zeros((ROWS, 128 - RLON), F32)], 1))
    for k in range(8):
        send(img, ir.at[k], sent, isem, i_peers[k])
    arrived(ir, isem)
    image = ir[0]
    for k in range(1, 8):
        image = image + ir[k]
    image = unpack_image(image)
    summed[...] = image
    send(summed, home, sent, hsem, z_peers[1])
    gp[...] = pack_gram(
        lax.dot_general(image, image, (((0,), (0,)), ((), ())), precision=HIGHEST, preferred_element_type=F32)
    )
    half = RLON // 4
    sibling = device(x, z, y, 1 - core)
    mine, other = (pl.ds(pl.multiple_of(half * c, 8), half) for c in (1 - core, core))
    send(gp.at[other], gr, sent, gsem.at[0], sibling)
    arrived(gr, gsem.at[0])
    gh[...] = gp[mine] + gr[...]
    for k in range(15):
        send(gh, go.at[k], sent, gsem.at[1], g_peers[k])
    arrived(home, hsem)
    image_t = jnp.concatenate([home[...].T[0:RLON], jnp.zeros((RLON, 128 - ROWS), F32)], 1)
    arrived(go, gsem.at[1])
    total = gh[...]
    for k in range(15):
        total = total + go[k]
    gf[mine] = total
    send(gf.at[mine], gf.at[mine], sent, gsem.at[2], sibling)

    @pl.when(core == 0)
    def _():
        arrived(gr, gsem.at[2])

    def rest():
        @pl.when(core == 1)
        def _():
            arrived(gr, gsem.at[2])

        return jnp.concatenate([unpack_top(gf[HEAD:]), unpack_low(gf[...])], 0)

    solve(total_rows, unpack_top(gf[0:HEAD]), rest, image_t, out, yt)

    refs = (xr, wr, wz, wr, ir, home, gr, go, gr)
    arrived(fv.at[pl.ds(0, sum(math.prod(ref.shape) // 128 for ref in refs))], sent)


def body(field, lat_factor, lev_factor, old_factor):
    vmem = pl.BlockSpec(memory_space=pltpu.VMEM)
    dma = pltpu.SemaphoreType.DMA
    field = field.reshape(TIMES * ROWS * LATS, LEVS)
    total_rows = ROWS * lax.axis_size("lon")
    return pl.pallas_call(
        functools.partial(hooi_kernel, total_rows),
        out_shape=pltpu.VMEM((ROWS, RLON), F32),
        in_specs=[pl.BlockSpec(memory_space=pltpu.HBM)] * 4,
        out_specs=vmem,
        scratch_shapes=[
            pltpu.VMEM((TIMES * ROWS * LATS, LEVS), F32),
            pltpu.VMEM((LATS, RLAT), F32),
            pltpu.VMEM((RLEV, LEVS), F32),
            pltpu.VMEM((ROWS, RLON), F32),
            pltpu.VMEM((128, 128), F32),
            pltpu.VMEM((RLEV * ROWS, 128), F32),
            pltpu.VMEM((BLOCKS, 4, ROWS, 128), F32),
            pltpu.VMEM((BLOCKS, 3, ROWS, 128), F32),
            pltpu.VMEM((BLOCKS, ROWS, 128), F32),
            pltpu.VMEM((BLOCKS, RLON, 128), F32),
            pltpu.VMEM((BLOCKS, 7, PART, 128), F32),
            pltpu.VMEM((BLOCKS, PART, 128), F32),
            pltpu.VMEM((BLOCKS, 7, PART, 128), F32),
            pltpu.VMEM((BLOCKS, RLON, 128), F32),
            pltpu.VMEM((IMAGE_ROWS, 128), F32),
            pltpu.VMEM((8, IMAGE_ROWS, 128), F32),
            pltpu.VMEM((ROWS, 128), F32),
            pltpu.VMEM((ROWS, 128), F32),
            pltpu.VMEM((RLON // 2, 128), F32),
            pltpu.VMEM((RLON // 4, 128), F32),
            pltpu.VMEM((RLON // 4, 128), F32),
            pltpu.VMEM((15, RLON // 4, 128), F32),
            pltpu.VMEM((RLON // 2, 128), F32),
            pltpu.VMEM((RLON, 128), F32),
            dma((3,)),
            dma((3,)),
            pltpu.SemaphoreType.REGULAR,
            dma,
            dma((len(GROUPS),)),
            dma((len(GROUPS),)),
            dma((len(GROUPS),)),
            dma,
            dma,
            dma((3,)),
        ],
        compiler_params=pltpu.CompilerParams(
            collective_id=0, has_side_effects=True, vmem_limit_bytes=48 * 1024 * 1024
        ),
    )(*(pltpu.with_memory_space_constraint(v, pltpu.HBM) for v in (field, lat_factor, lev_factor.T, old_factor)))


def solution(mesh):
    placed = (P(None, "lon", "lat", None), P("lat", None), P(), P("lon", None))
    return jax.shard_map(
        body, mesh=mesh, in_specs=placed, out_specs=P("lon", None), check_vma=False
    )
```

```python
import functools
import math

import jax
import jax.numpy as jnp
from jax import lax
from jax.experimental import pallas as pl
from jax.experimental.pallas import tpu as pltpu
from jax.sharding import PartitionSpec as P

MESH = pl.DeviceIdType.MESH
HIGHEST = lax.Precision.HIGHEST
F32, BF16 = jnp.float32, jnp.bfloat16
TIMES, ROWS, LATS, LEVS = 2, 48, 96, 128
RLAT, RLEV, RLON = 96, 32, 96
SLABS = 3
BLOCKS = TIMES * SLABS * 2
LOADS = (0, 24), (24, 24), (48, 48)
FAR_FIRST = (3, 2, 4, 1, 5, 0, 6)
PART = RLON // 8
GROUPS = tuple((b, 1) for b in range(BLOCKS))
SCHEDULE = sorted(
    (first + count + lag, kind, g) for g, (first, count) in enumerate(GROUPS) for kind, lag in enumerate((0, 4.6, 11, 16))
)


def split(v):
    hi = v.astype(BF16)
    return hi, (v - hi.astype(F32)).astype(BF16)


def dot3(a, b, dims):
    (ah, al), (bh, bl) = a, b
    dot = functools.partial(lax.dot_general, dimension_numbers=(dims, ((), ())), preferred_element_type=F32)
    return dot(ah, bh) + (dot(al, bh) + dot(ah, bl))


def place():
    lon, lat = lax.axis_index("lon"), lax.axis_index("lat")
    return lat // 2, (lat % 2) * 4 + lon // 8, (lon // 2) % 4, lon % 2


def device(x, z, y, core):
    return (z % 4) * 8 + y * 2 + core, x * 2 + z // 4


IMAGE_ROWS = 36


def lanes_of(v):
    return lax.broadcasted_iota(jnp.int32, v.shape, 1)


def pack_image(v):
    last = v[IMAGE_ROWS:]
    tail = jnp.concatenate([pltpu.roll(last, 96 - 32 * k, 1) for k in range(3)], 0)
    return jnp.where(lanes_of(tail) < RLON, v[:IMAGE_ROWS], tail)


def unpack_image(v):
    last = jnp.zeros((12, 128), F32)
    for k in range(3):
        piece = pltpu.roll(v[12 * k : 12 * k + 12], 32 + 32 * k, 1)
        last = jnp.where(lanes_of(last) // 32 == k, piece, last)
    return jnp.concatenate([jnp.where(lanes_of(v) < RLON, v, 0.0), last], 0)


def pack_gram(g):
    half = RLON // 2
    top, low = g[:half], g[half:RLON]
    lane, row = lanes_of(top), lax.broadcasted_iota(jnp.int32, top.shape, 0)
    rest = jnp.where(lane <= half, pltpu.roll(top, 1, 1), pltpu.roll(top, 16, 1))
    return jnp.where(lane <= row, pltpu.roll(low, 128 - half, 1), rest)


def unpack_top(v):
    return jnp.where(lanes_of(v) < RLON // 2, pltpu.roll(v, 127, 1), pltpu.roll(v, 112, 1))


def unpack_low(v):
    half = RLON // 2
    square = jnp.concatenate([v, jnp.zeros((128 - half, 128), F32)], 0).T
    return pltpu.roll(square[:half], half, 1)


HEAD = 16


def tree_sum(terms):
    while len(terms) > 1:
        terms = [a + b for a, b in zip(terms[::2], terms[1::2])]
    return terms[0]


def solve(total_rows, head, rest, image_t, out, yt):
    tiles = RLON // 8
    left = [head[8 * r : 8 * r + 8] for r in range(HEAD // 8)]
    right = [image_t[8 * r : 8 * r + 8] for r in range(tiles)]
    sub = lax.broadcasted_iota(jnp.int32, (8, 128), 0)
    diagonal = lax.broadcasted_iota(jnp.int32, (8, 128), 1) - sub
    spread = lambda v: jnp.broadcast_to(v, (8, 128))

    def down(row, r):
        return spread(jnp.sum(jnp.where(diagonal == 8 * r, row, 0.0), axis=1, keepdims=True))

    col = [spread(left[0][:, q : q + 1]) for q in range(8)]
    for j in range(tiles):
        at = 8 * j
        d = [[spread(col[q][p : p + 1]) for p in range(q + 1)] for q in range(8)]
        vl = [spread(left[j][p : p + 1]) for p in range(8)]
        vr = [spread(right[j][p : p + 1]) for p in range(8)]
        if j + 1 < tiles:
            col = [spread(left[j + 1][:, at + 8 + q : at + 9 + q]) for q in range(8)]
            m = [down(vl[p], j + 1) for p in range(8)]
        else:
            m = [jnp.zeros((8, 128), F32)] * 8
        for p in range(8):
            inv = lax.rsqrt(d[p][p])
            for q in range(p + 1, 8):
                d[q][p] = d[q][p] * inv
            for q in range(p + 1, 8):
                for r in range(p + 1, q + 1):
                    d[q][r] = d[q][r] - d[q][p] * d[r][p]
            vl[p], vr[p], m[p] = vl[p] * inv, vr[p] * inv, m[p] * inv
            for q in range(p + 1, 8):
                vl[q] = vl[q] - d[q][p] * vl[p]
                vr[q] = vr[q] - d[q][p] * vr[p]
                m[q] = m[q] - d[q][p] * m[p]
        rows = vr[0]
        for p in range(1, 8):
            rows = jnp.where(sub == p, vr[p], rows)
        yt[at : at + 8] = rows
        if j == 0:
            more = rest()
            left += [more[8 * r : 8 * r + 8] for r in range(tiles - HEAD // 8)]
        for r in range(j + 1, tiles):
            if r == j + 1:
                col = [col[q] - tree_sum([m[p] * spread(m[p][q : q + 1]) for p in range(8)]) for q in range(8)]
            else:
                m = [down(vl[p], r) for p in range(8)]
            left[r] = left[r] - tree_sum([m[p] * vl[p] for p in range(8)])
            right[r] = right[r] - tree_sum([m[p] * vr[p] for p in range(8)])
    out[...] = yt[...].T[0:ROWS] * jnp.sqrt(F32(total_rows))


def hooi_kernel(
    total_rows, field, lat, lev_t, old, out,
    fv, lat_in, lev_in, old_in, lats, lvl, proj, xr, pz, wt, wr, ws, wz, wf, img, ir, summed, home, gp, gr, gh, go, gf,
    yt, fsem, csem, passed, sent, xsem, rsem, zsem, isem, hsem, gsem,
):
    x, z, y, core = place()
    me = y * 2 + core

    def send(src, dst, sent, landed, to):
        copy = pltpu.make_async_remote_copy(
            src_ref=src, dst_ref=dst, send_sem=sent, recv_sem=landed, device_id=to, device_id_type=MESH
        )
        copy.start()
        return copy

    def arrived(ref, sem):
        pltpu.make_async_copy(ref, ref, sem).wait()

    loads = [
        pltpu.make_async_copy(
            field.at[pl.ds(at * LATS, rows * LATS)], fv.at[pl.ds(at * LATS, rows * LATS)], fsem.at[k]
        )
        for k, (at, rows) in enumerate(LOADS)
    ]
    small = [
        pltpu.make_async_copy(src, dst, csem.at[k])
        for k, (src, dst) in enumerate(((lev_t, lev_in), (lat, lat_in), (old, old_in)))
    ]
    for load in small + loads:
        load.start()

    x_peers = [device((x + dx) % 4, z, y, core) for dx in (1, 2, 3)]
    z_peers = [device(x, (z + dz) % 8, y, core) for dz in range(1, 8)]
    yc_peers = [device(x, z, ((me + j) % 8) // 2, (me + j) % 2) for j in range(1, 8)]
    i_peers = [device((x + dx) % 4, (z + dz) % 8, y, core) for dx in (2, 1, 3, 0) for dz in (2, 6)]
    g_steps = [(dy, dz) for dy in range(4) for dz in (0, 1, 7, 2 if dy < 2 else 6)][1:]
    g_steps.sort(key=lambda step: -min(step[0], 4 - step[0]) - min(step[1], 8 - step[1]))
    g_peers = [device(x, (z + dz) % 8, (y + dy) % 4, core) for dy, dz in g_steps]

    greeted = [x_peers[1], z_peers[1], z_peers[5]] + [yc_peers[k] for k in FAR_FIRST]
    greeted += [x_peers[0], x_peers[2], z_peers[0], z_peers[6]]
    barrier = pltpu.get_barrier_semaphore()
    for peer in greeted:
        pl.semaphore_signal(barrier, inc=1, device_id=peer, device_id_type=MESH)
    told = [z_peers[1], z_peers[5]]

    small[0].wait()
    small[1].wait()
    levh, levl = split(lev_in[...])
    lev2 = jnp.concatenate(
        [jnp.concatenate([levh, levh], 1), jnp.concatenate([levl, jnp.zeros_like(levl)], 1)], 0
    )
    lats[...] = jnp.zeros_like(lats)
    lats[0:LATS, 0:RLAT] = lat_in[...]
    lat_pad = lats[...]
    lane = lax.broadcasted_iota(jnp.int32, (128, 128), 1)
    lat_hi, lat_lo = [], []
    for u in range(SLABS):
        tail = jnp.where(lane >= RLAT, pltpu.roll(lat_pad, 96 - 32 * u, 1), 0.0)
        hi, lo = split(jnp.concatenate([lat_pad, tail], 0))
        lat_hi.append(hi)
        lat_lo.append(lo)

    def levels(k):
        def one(i, carry):
            f = fv[pl.ds(pl.multiple_of(i * LATS, LATS), LATS), :]
            fh, fl = split(f)
            both = jnp.concatenate([fh, fl], 1)
            both = jnp.concatenate([both, jnp.zeros((128 - LATS, 256), BF16)], 0)
            r = lax.dot_general(lev2, both, (((1,), (1,)), ((), ())), preferred_element_type=F32)
            lvl[pl.ds(lax.rem(i, ROWS), RLEV, stride=ROWS), :] = r[:RLEV] + r[RLEV:]
            return carry

        loads[k].wait()
        at, rows = LOADS[k]
        lax.fori_loop(at, at + rows, one, 0, unroll=24)

    def latitudes(t, u):
        parts = [
            jnp.concatenate([lvl[pl.ds((4 * d + v) * ROWS, ROWS), :] for d in range(8)], 0) for v in (u, 3)
        ]
        hi, lo = split(jnp.concatenate(parts, 1))
        r = (
            jnp.dot(hi, lat_hi[u], preferred_element_type=F32)
            + jnp.dot(lo, lat_hi[u], preferred_element_type=F32)
            + jnp.dot(hi, lat_lo[u], preferred_element_type=F32)
        )
        for d in range(8):
            proj[2 * (t * SLABS + u) + d % 2, d // 2] = r[d * ROWS : (d + 1) * ROWS]

    for t in range(TIMES):
        for k in ((0, 1), (2,))[t]:
            levels(k)
        for u in range(SLABS):
            latitudes(t, u)
            if t + u == 0:
                pl.semaphore_wait(barrier, len(greeted))
                for peer in told:
                    pl.semaphore_signal(passed, inc=1, device_id=peer, device_id_type=MESH)
            for g, (first, count) in enumerate(GROUPS):
                if first // 2 == t * SLABS + u:
                    blocks = pl.ds(first, count)
                    for k in (1, 0, 2):
                        send(proj.at[blocks, (x + k + 1) % 4], xr.at[blocks, k], sent, xsem.at[g], x_peers[k])

    pl.semaphore_wait(passed, len(told))
    small[2].wait()
    old_t = split(old_in[...].T)
    acc = jnp.zeros((ROWS, RLON), F32)

    for at, kind, g in SCHEDULE:
        first, count = GROUPS[g]
        blocks = pl.ds(first, count)
        if kind == 0:
            arrived(xr.at[blocks], xsem.at[g])
            for b in range(first, first + count):
                pz[b] = proj[b, x] + xr[b, 0] + xr[b, 1] + xr[b, 2]
                wt[b] = dot3(old_t, split(pz[b]), ((1,), (0,)))
            for k in FAR_FIRST:
                part = pl.ds(PART * ((me + k + 1) % 8), PART)
                send(wt.at[blocks, part], wr.at[blocks, k], sent, rsem.at[g], yc_peers[k])
        elif kind == 1:
            arrived(wr.at[blocks], rsem.at[g])
            for b in range(first, first + count):
                part = wt[b, pl.ds(PART * me, PART)]
                for k in range(7):
                    part = part + wr[b, k]
                ws[b] = part
            for k in FAR_FIRST:
                send(ws.at[blocks], wz.at[blocks, k], sent, zsem.at[g], z_peers[k])
        elif kind == 2:
            arrived(wz.at[blocks], zsem.at[g])
            for b in range(first, first + count):
                part = ws[b]
                for k in range(7):
                    part = part + wz[b, k]
                wf[b, pl.ds(PART * me, PART)] = part
            mine = wf.at[blocks, pl.ds(PART * me, PART)]
            for k in FAR_FIRST:
                send(mine, mine, sent, xsem.at[g], yc_peers[k])
        else:
            arrived(wr.at[blocks], xsem.at[g])
            for b in range(first, first + count):
                acc = acc + dot3(split(pz[b]), split(wf[b]), ((1,), (1,)))
    img[...] = pack_image(jnp.concatenate([acc, jnp.zeros((ROWS, 128 - RLON), F32)], 1))
    for k in range(8):
        send(img, ir.at[k], sent, isem, i_peers[k])
    arrived(ir, isem)
    image = ir[0]
    for k in range(1, 8):
        image = image + ir[k]
    image = unpack_image(image)
    summed[...] = image
    send(summed, home, sent, hsem, z_peers[1])
    gp[...] = pack_gram(
        lax.dot_general(image, image, (((0,), (0,)), ((), ())), precision=HIGHEST, preferred_element_type=F32)
    )
    half = RLON // 4
    sibling = device(x, z, y, 1 - core)
    mine, other = (pl.ds(pl.multiple_of(half * c, 8), half) for c in (1 - core, core))
    send(gp.at[other], gr, sent, gsem.at[0], sibling)
    arrived(gr, gsem.at[0])
    gh[...] = gp[mine] + gr[...]
    for k in range(15):
        send(gh, go.at[k], sent, gsem.at[1], g_peers[k])
    arrived(home, hsem)
    image_t = jnp.concatenate([home[...].T[0:RLON], jnp.zeros((RLON, 128 - ROWS), F32)], 1)
    arrived(go, gsem.at[1])
    total = gh[...]
    for k in range(15):
        total = total + go[k]
    gf[mine] = total
    send(gf.at[mine], gf.at[mine], sent, gsem.at[2], sibling)

    @pl.when(core == 0)
    def _():
        arrived(gr, gsem.at[2])

    def rest():
        @pl.when(core == 1)
        def _():
            arrived(gr, gsem.at[2])

        return jnp.concatenate([unpack_top(gf[HEAD:]), unpack_low(gf[...])], 0)

    solve(total_rows, unpack_top(gf[0:HEAD]), rest, image_t, out, yt)

    refs = (xr, wr, wz, wr, ir, home, gr, go, gr)
    arrived(fv.at[pl.ds(0, sum(math.prod(ref.shape) // 128 for ref in refs))], sent)


def body(field, lat_factor, lev_factor, old_factor):
    vmem = pl.BlockSpec(memory_space=pltpu.VMEM)
    dma = pltpu.SemaphoreType.DMA
    field = field.reshape(TIMES * ROWS * LATS, LEVS)
    total_rows = ROWS * lax.axis_size("lon")
    return pl.pallas_call(
        functools.partial(hooi_kernel, total_rows),
        out_shape=pltpu.VMEM((ROWS, RLON), F32),
        in_specs=[pl.BlockSpec(memory_space=pltpu.HBM)] * 4,
        out_specs=vmem,
        scratch_shapes=[
            pltpu.VMEM((TIMES * ROWS * LATS, LEVS), F32),
            pltpu.VMEM((LATS, RLAT), F32),
            pltpu.VMEM((RLEV, LEVS), F32),
            pltpu.VMEM((ROWS, RLON), F32),
            pltpu.VMEM((128, 128), F32),
            pltpu.VMEM((RLEV * ROWS, 128), F32),
            pltpu.VMEM((BLOCKS, 4, ROWS, 128), F32),
            pltpu.VMEM((BLOCKS, 3, ROWS, 128), F32),
            pltpu.VMEM((BLOCKS, ROWS, 128), F32),
            pltpu.VMEM((BLOCKS, RLON, 128), F32),
            pltpu.VMEM((BLOCKS, 7, PART, 128), F32),
            pltpu.VMEM((BLOCKS, PART, 128), F32),
            pltpu.VMEM((BLOCKS, 7, PART, 128), F32),
            pltpu.VMEM((BLOCKS, RLON, 128), F32),
            pltpu.VMEM((IMAGE_ROWS, 128), F32),
            pltpu.VMEM((8, IMAGE_ROWS, 128), F32),
            pltpu.VMEM((ROWS, 128), F32),
            pltpu.VMEM((ROWS, 128), F32),
            pltpu.VMEM((RLON // 2, 128), F32),
            pltpu.VMEM((RLON // 4, 128), F32),
            pltpu.VMEM((RLON // 4, 128), F32),
            pltpu.VMEM((15, RLON // 4, 128), F32),
            pltpu.VMEM((RLON // 2, 128), F32),
            pltpu.VMEM((RLON, 128), F32),
            dma((3,)),
            dma((3,)),
            pltpu.SemaphoreType.REGULAR,
            dma,
            dma((len(GROUPS),)),
            dma((len(GROUPS),)),
            dma((len(GROUPS),)),
            dma,
            dma,
            dma((3,)),
        ],
        compiler_params=pltpu.CompilerParams(
            collective_id=0, has_side_effects=True, vmem_limit_bytes=48 * 1024 * 1024
        ),
    )(*(pltpu.with_memory_space_constraint(v, pltpu.HBM) for v in (field, lat_factor, lev_factor.T, old_factor)))


def solution(mesh):
    placed = (P(None, "lon", "lat", None), P("lat", None), P(), P("lon", None))
    return jax.shard_map(
        body, mesh=mesh, in_specs=placed, out_specs=P("lon", None), check_vma=False
    )
```

```python
import functools
import math

import jax
import jax.numpy as jnp
from jax import lax
from jax.experimental import pallas as pl
from jax.experimental.pallas import tpu as pltpu
from jax.sharding import PartitionSpec as P

MESH = pl.DeviceIdType.MESH
HIGHEST = lax.Precision.HIGHEST
F32, BF16 = jnp.float32, jnp.bfloat16
TIMES, ROWS, LATS, LEVS = 2, 48, 96, 128
RLAT, RLEV, RLON = 96, 32, 96
SLABS = 3
BLOCKS = TIMES * SLABS * 2
LOADS = (0, 24), (24, 24), (48, 48)
FAR_FIRST = (3, 2, 4, 1, 5, 0, 6)
PART = RLON // 8
GROUPS = tuple((b, 1) for b in range(BLOCKS))
SCHEDULE = sorted(
    (first + count + lag, kind, g) for g, (first, count) in enumerate(GROUPS) for kind, lag in enumerate((0, 4.6, 11, 16))
)


def split(v):
    hi = v.astype(BF16)
    return hi, (v - hi.astype(F32)).astype(BF16)


def dot3(a, b, dims):
    (ah, al), (bh, bl) = a, b
    dot = functools.partial(lax.dot_general, dimension_numbers=(dims, ((), ())), preferred_element_type=F32)
    return dot(ah, bh) + (dot(al, bh) + dot(ah, bl))


def place():
    lon, lat = lax.axis_index("lon"), lax.axis_index("lat")
    return lat // 2, (lat % 2) * 4 + lon // 8, (lon // 2) % 4, lon % 2


def device(x, z, y, core):
    return (z % 4) * 8 + y * 2 + core, x * 2 + z // 4


IMAGE_ROWS = 36


def lanes_of(v):
    return lax.broadcasted_iota(jnp.int32, v.shape, 1)


def pack_image(v):
    last = v[IMAGE_ROWS:]
    tail = jnp.concatenate([pltpu.roll(last, 96 - 32 * k, 1) for k in range(3)], 0)
    return jnp.where(lanes_of(tail) < RLON, v[:IMAGE_ROWS], tail)


def unpack_image(v):
    last = jnp.zeros((12, 128), F32)
    for k in range(3):
        piece = pltpu.roll(v[12 * k : 12 * k + 12], 32 + 32 * k, 1)
        last = jnp.where(lanes_of(last) // 32 == k, piece, last)
    return jnp.concatenate([jnp.where(lanes_of(v) < RLON, v, 0.0), last], 0)


def pack_gram(g):
    half = RLON // 2
    top, low = g[:half], g[half:RLON]
    lane, row = lanes_of(top), lax.broadcasted_iota(jnp.int32, top.shape, 0)
    rest = jnp.where(lane <= half, pltpu.roll(top, 1, 1), pltpu.roll(top, 16, 1))
    return jnp.where(lane <= row, pltpu.roll(low, 128 - half, 1), rest)


def unpack_top(v):
    return jnp.where(lanes_of(v) < RLON // 2, pltpu.roll(v, 127, 1), pltpu.roll(v, 112, 1))


def unpack_low(v):
    half = RLON // 2
    square = jnp.concatenate([v, jnp.zeros((128 - half, 128), F32)], 0).T
    return pltpu.roll(square[:half], half, 1)


HEAD = 24


def tree_sum(terms):
    while len(terms) > 1:
        terms = [a + b for a, b in zip(terms[::2], terms[1::2])] + terms[len(terms) // 2 * 2 :]
    return terms[0]


def solve(total_rows, head, rest, image_t, out, yt):
    tiles = RLON // 8
    known = HEAD // 8
    left = [head[8 * r : 8 * r + 8] for r in range(known)]
    right = [image_t[8 * r : 8 * r + 8] for r in range(tiles)]
    sub = lax.broadcasted_iota(jnp.int32, (8, 128), 0)
    diagonal = lax.broadcasted_iota(jnp.int32, (8, 128), 1) - sub
    spread = lambda v: jnp.broadcast_to(v, (8, 128))

    def down(row, r):
        return spread(jnp.sum(jnp.where(diagonal == 8 * r, row, 0.0), axis=1, keepdims=True))

    done = []
    col = [spread(left[0][:, q : q + 1]) for q in range(8)]
    for j in range(tiles):
        at = 8 * j
        d = [[spread(col[q][p : p + 1]) for p in range(q + 1)] for q in range(8)]
        vl = [spread(left[j][p : p + 1]) for p in range(8)]
        vr = [spread(right[j][p : p + 1]) for p in range(8)]
        if j + 1 < len(left):
            col = [spread(left[j + 1][:, at + 8 + q : at + 9 + q]) for q in range(8)]
            m = [down(vl[p], j + 1) for p in range(8)]
        else:
            m = [jnp.zeros((8, 128), F32)] * 8
        for p in range(8):
            inv = lax.rsqrt(d[p][p])
            for q in range(p + 1, 8):
                d[q][p] = d[q][p] * inv
            for q in range(p + 1, 8):
                for r in range(p + 1, q + 1):
                    d[q][r] = d[q][r] - d[q][p] * d[r][p]
            vl[p], vr[p], m[p] = vl[p] * inv, vr[p] * inv, m[p] * inv
            for q in range(p + 1, 8):
                vl[q] = vl[q] - d[q][p] * vl[p]
                vr[q] = vr[q] - d[q][p] * vr[p]
                m[q] = m[q] - d[q][p] * m[p]
        rows = vr[0]
        for p in range(1, 8):
            rows = jnp.where(sub == p, vr[p], rows)
        yt[at : at + 8] = rows
        done.append((vl, vr))
        if j == known - 1:
            late = []
            for r in range(known, tiles):
                terms = [(down(row, r), row, y) for rows in done for row, y in zip(*rows)]
                late.append([tree_sum([t[0] * t[k] for t in terms]) for k in (1, 2)])
            more = rest()
            for r in range(known, tiles):
                left.append(more[8 * (r - known) : 8 * (r - known) + 8] - late[r - known][0])
                right[r] = right[r] - late[r - known][1]
            col = [spread(left[known][:, HEAD + q : HEAD + q + 1]) for q in range(8)]
            continue
        for r in range(j + 1, len(left)):
            if r == j + 1:
                col = [col[q] - tree_sum([m[p] * spread(m[p][q : q + 1]) for p in range(8)]) for q in range(8)]
            else:
                m = [down(vl[p], r) for p in range(8)]
            left[r] = left[r] - tree_sum([m[p] * vl[p] for p in range(8)])
            right[r] = right[r] - tree_sum([m[p] * vr[p] for p in range(8)])
    out[...] = yt[...].T[0:ROWS] * jnp.sqrt(F32(total_rows))


def hooi_kernel(
    total_rows, field, lat, lev_t, old, out,
    fv, lat_in, lev_in, old_in, lats, lvl, proj, xr, pz, wt, wr, ws, wz, wf, img, ir, summed, home, gp, gr, gh, go, gf,
    yt, fsem, csem, passed, sent, xsem, rsem, zsem, isem, hsem, gsem,
):
    x, z, y, core = place()
    me = y * 2 + core

    def send(src, dst, sent, landed, to):
        copy = pltpu.make_async_remote_copy(
            src_ref=src, dst_ref=dst, send_sem=sent, recv_sem=landed, device_id=to, device_id_type=MESH
        )
        copy.start()
        return copy

    def arrived(ref, sem):
        pltpu.make_async_copy(ref, ref, sem).wait()

    loads = [
        pltpu.make_async_copy(
            field.at[pl.ds(at * LATS, rows * LATS)], fv.at[pl.ds(at * LATS, rows * LATS)], fsem.at[k]
        )
        for k, (at, rows) in enumerate(LOADS)
    ]
    small = [
        pltpu.make_async_copy(src, dst, csem.at[k])
        for k, (src, dst) in enumerate(((lev_t, lev_in), (lat, lat_in), (old, old_in)))
    ]
    for load in small + loads:
        load.start()

    x_peers = [device((x + dx) % 4, z, y, core) for dx in (1, 2, 3)]
    z_peers = [device(x, (z + dz) % 8, y, core) for dz in range(1, 8)]
    yc_peers = [device(x, z, ((me + j) % 8) // 2, (me + j) % 2) for j in range(1, 8)]
    i_peers = [device((x + dx) % 4, (z + dz) % 8, y, core) for dx in (2, 1, 3, 0) for dz in (2, 6)]
    g_steps = [(dy, dz) for dy in range(4) for dz in (0, 1, 7, 2 if dy < 2 else 6)][1:]
    g_steps.sort(key=lambda step: -min(step[0], 4 - step[0]) - min(step[1], 8 - step[1]))
    g_peers = [device(x, (z + dz) % 8, (y + dy) % 4, core) for dy, dz in g_steps]

    greeted = [x_peers[1], z_peers[1], z_peers[5]] + [yc_peers[k] for k in FAR_FIRST]
    greeted += [x_peers[0], x_peers[2], z_peers[0], z_peers[6]]
    barrier = pltpu.get_barrier_semaphore()
    for peer in greeted:
        pl.semaphore_signal(barrier, inc=1, device_id=peer, device_id_type=MESH)
    told = [z_peers[1], z_peers[5]]

    small[0].wait()
    small[1].wait()
    levh, levl = split(lev_in[...])
    lev2 = jnp.concatenate(
        [jnp.concatenate([levh, levh], 1), jnp.concatenate([levl, jnp.zeros_like(levl)], 1)], 0
    )
    lats[...] = jnp.zeros_like(lats)
    lats[0:LATS, 0:RLAT] = lat_in[...]
    lat_pad = lats[...]
    lane = lax.broadcasted_iota(jnp.int32, (128, 128), 1)
    lat_hi, lat_lo = [], []
    for u in range(SLABS):
        tail = jnp.where(lane >= RLAT, pltpu.roll(lat_pad, 96 - 32 * u, 1), 0.0)
        hi, lo = split(jnp.concatenate([lat_pad, tail], 0))
        lat_hi.append(hi)
        lat_lo.append(lo)

    def levels(k):
        def one(i, carry):
            f = fv[pl.ds(pl.multiple_of(i * LATS, LATS), LATS), :]
            fh, fl = split(f)
            both = jnp.concatenate([fh, fl], 1)
            both = jnp.concatenate([both, jnp.zeros((128 - LATS, 256), BF16)], 0)
            r = lax.dot_general(lev2, both, (((1,), (1,)), ((), ())), preferred_element_type=F32)
            lvl[pl.ds(lax.rem(i, ROWS), RLEV, stride=ROWS), :] = r[:RLEV] + r[RLEV:]
            return carry

        loads[k].wait()
        at, rows = LOADS[k]
        lax.fori_loop(at, at + rows, one, 0, unroll=24)

    def latitudes(t, u):
        parts = [
            jnp.concatenate([lvl[pl.ds((4 * d + v) * ROWS, ROWS), :] for d in range(8)], 0) for v in (u, 3)
        ]
        hi, lo = split(jnp.concatenate(parts, 1))
        r = (
            jnp.dot(hi, lat_hi[u], preferred_element_type=F32)
            + jnp.dot(lo, lat_hi[u], preferred_element_type=F32)
            + jnp.dot(hi, lat_lo[u], preferred_element_type=F32)
        )
        for d in range(8):
            proj[2 * (t * SLABS + u) + d % 2, d // 2] = r[d * ROWS : (d + 1) * ROWS]

    for t in range(TIMES):
        for k in ((0, 1), (2,))[t]:
            levels(k)
        for u in range(SLABS):
            latitudes(t, u)
            if t + u == 0:
                pl.semaphore_wait(barrier, len(greeted))
                for peer in told:
                    pl.semaphore_signal(passed, inc=1, device_id=peer, device_id_type=MESH)
            for g, (first, count) in enumerate(GROUPS):
                if first // 2 == t * SLABS + u:
                    blocks = pl.ds(first, count)
                    for k in (1, 0, 2):
                        send(proj.at[blocks, (x + k + 1) % 4], xr.at[blocks, k], sent, xsem.at[g], x_peers[k])

    pl.semaphore_wait(passed, len(told))
    small[2].wait()
    old_t = split(old_in[...].T)
    acc = jnp.zeros((ROWS, RLON), F32)

    for at, kind, g in SCHEDULE:
        first, count = GROUPS[g]
        blocks = pl.ds(first, count)
        if kind == 0:
            arrived(xr.at[blocks], xsem.at[g])
            for b in range(first, first + count):
                pz[b] = proj[b, x] + xr[b, 0] + xr[b, 1] + xr[b, 2]
                wt[b] = dot3(old_t, split(pz[b]), ((1,), (0,)))
            for k in FAR_FIRST:
                part = pl.ds(PART * ((me + k + 1) % 8), PART)
                send(wt.at[blocks, part], wr.at[blocks, k], sent, rsem.at[g], yc_peers[k])
        elif kind == 1:
            arrived(wr.at[blocks], rsem.at[g])
            for b in range(first, first + count):
                part = wt[b, pl.ds(PART * me, PART)]
                for k in range(7):
                    part = part + wr[b, k]
                ws[b] = part
            for k in FAR_FIRST:
                send(ws.at[blocks], wz.at[blocks, k], sent, zsem.at[g], z_peers[k])
        elif kind == 2:
            arrived(wz.at[blocks], zsem.at[g])
            for b in range(first, first + count):
                part = ws[b]
                for k in range(7):
                    part = part + wz[b, k]
                wf[b, pl.ds(PART * me, PART)] = part
            mine = wf.at[blocks, pl.ds(PART * me, PART)]
            for k in FAR_FIRST:
                send(mine, mine, sent, xsem.at[g], yc_peers[k])
        else:
            arrived(wr.at[blocks], xsem.at[g])
            for b in range(first, first + count):
                acc = acc + dot3(split(pz[b]), split(wf[b]), ((1,), (1,)))
    img[...] = pack_image(jnp.concatenate([acc, jnp.zeros((ROWS, 128 - RLON), F32)], 1))
    for k in range(8):
        send(img, ir.at[k], sent, isem, i_peers[k])
    arrived(ir, isem)
    image = ir[0]
    for k in range(1, 8):
        image = image + ir[k]
    image = unpack_image(image)
    summed[...] = image
    send(summed, home, sent, hsem, z_peers[1])
    gp[...] = pack_gram(
        lax.dot_general(image, image, (((0,), (0,)), ((), ())), precision=HIGHEST, preferred_element_type=F32)
    )
    half = RLON // 4
    sibling = device(x, z, y, 1 - core)
    mine, other = (pl.ds(pl.multiple_of(half * c, 8), half) for c in (1 - core, core))
    send(gp.at[other], gr, sent, gsem.at[0], sibling)
    arrived(gr, gsem.at[0])
    gh[...] = gp[mine] + gr[...]
    for k in range(15):
        send(gh, go.at[k], sent, gsem.at[1], g_peers[k])
    arrived(home, hsem)
    image_t = jnp.concatenate([home[...].T[0:RLON], jnp.zeros((RLON, 128 - ROWS), F32)], 1)
    arrived(go, gsem.at[1])
    total = gh[...]
    for k in range(15):
        total = total + go[k]
    gf[mine] = total
    send(gf.at[mine], gf.at[mine], sent, gsem.at[2], sibling)

    @pl.when(core == 0)
    def _():
        arrived(gr, gsem.at[2])

    def rest():
        @pl.when(core == 1)
        def _():
            arrived(gr, gsem.at[2])

        return jnp.concatenate([unpack_top(gf[HEAD:]), unpack_low(gf[...])], 0)

    solve(total_rows, unpack_top(gf[0:HEAD]), rest, image_t, out, yt)

    refs = (xr, wr, wz, wr, ir, home, gr, go, gr)
    arrived(fv.at[pl.ds(0, sum(math.prod(ref.shape) // 128 for ref in refs))], sent)


def body(field, lat_factor, lev_factor, old_factor):
    vmem = pl.BlockSpec(memory_space=pltpu.VMEM)
    dma = pltpu.SemaphoreType.DMA
    field = field.reshape(TIMES * ROWS * LATS, LEVS)
    total_rows = ROWS * lax.axis_size("lon")
    return pl.pallas_call(
        functools.partial(hooi_kernel, total_rows),
        out_shape=pltpu.VMEM((ROWS, RLON), F32),
        in_specs=[pl.BlockSpec(memory_space=pltpu.HBM)] * 4,
        out_specs=vmem,
        scratch_shapes=[
            pltpu.VMEM((TIMES * ROWS * LATS, LEVS), F32),
            pltpu.VMEM((LATS, RLAT), F32),
            pltpu.VMEM((RLEV, LEVS), F32),
            pltpu.VMEM((ROWS, RLON), F32),
            pltpu.VMEM((128, 128), F32),
            pltpu.VMEM((RLEV * ROWS, 128), F32),
            pltpu.VMEM((BLOCKS, 4, ROWS, 128), F32),
            pltpu.VMEM((BLOCKS, 3, ROWS, 128), F32),
            pltpu.VMEM((BLOCKS, ROWS, 128), F32),
            pltpu.VMEM((BLOCKS, RLON, 128), F32),
            pltpu.VMEM((BLOCKS, 7, PART, 128), F32),
            pltpu.VMEM((BLOCKS, PART, 128), F32),
            pltpu.VMEM((BLOCKS, 7, PART, 128), F32),
            pltpu.VMEM((BLOCKS, RLON, 128), F32),
            pltpu.VMEM((IMAGE_ROWS, 128), F32),
            pltpu.VMEM((8, IMAGE_ROWS, 128), F32),
            pltpu.VMEM((ROWS, 128), F32),
            pltpu.VMEM((ROWS, 128), F32),
            pltpu.VMEM((RLON // 2, 128), F32),
            pltpu.VMEM((RLON // 4, 128), F32),
            pltpu.VMEM((RLON // 4, 128), F32),
            pltpu.VMEM((15, RLON // 4, 128), F32),
            pltpu.VMEM((RLON // 2, 128), F32),
            pltpu.VMEM((RLON, 128), F32),
            dma((3,)),
            dma((3,)),
            pltpu.SemaphoreType.REGULAR,
            dma,
            dma((len(GROUPS),)),
            dma((len(GROUPS),)),
            dma((len(GROUPS),)),
            dma,
            dma,
            dma((3,)),
        ],
        compiler_params=pltpu.CompilerParams(
            collective_id=0, has_side_effects=True, vmem_limit_bytes=48 * 1024 * 1024
        ),
    )(*(pltpu.with_memory_space_constraint(v, pltpu.HBM) for v in (field, lat_factor, lev_factor.T, old_factor)))


def solution(mesh):
    placed = (P(None, "lon", "lat", None), P("lat", None), P(), P("lon", None))
    return jax.shard_map(
        body, mesh=mesh, in_specs=placed, out_specs=P("lon", None), check_vma=False
    )
```

```python
import functools
import math

import jax
import jax.numpy as jnp
from jax import lax
from jax.experimental import pallas as pl
from jax.experimental.pallas import tpu as pltpu
from jax.sharding import PartitionSpec as P

MESH = pl.DeviceIdType.MESH
HIGHEST = lax.Precision.HIGHEST
F32, BF16 = jnp.float32, jnp.bfloat16
TIMES, ROWS, LATS, LEVS = 2, 48, 96, 128
RLAT, RLEV, RLON = 96, 32, 96
SLABS = 3
BLOCKS = TIMES * SLABS * 2
LOADS = (0, 24), (24, 24), (48, 48)
FAR_FIRST = (3, 2, 4, 1, 5, 0, 6)
PART = RLON // 8
GROUPS = tuple((b, 1) for b in range(BLOCKS))
SCHEDULE = sorted(
    (first + count + lag, kind, g) for g, (first, count) in enumerate(GROUPS) for kind, lag in enumerate((0, 4.6, 11, 16))
)


def split(v):
    hi = v.astype(BF16)
    return hi, (v - hi.astype(F32)).astype(BF16)


def dot3(a, b, dims):
    (ah, al), (bh, bl) = a, b
    dot = functools.partial(lax.dot_general, dimension_numbers=(dims, ((), ())), preferred_element_type=F32)
    return dot(ah, bh) + (dot(al, bh) + dot(ah, bl))


def place():
    lon, lat = lax.axis_index("lon"), lax.axis_index("lat")
    return lat // 2, (lat % 2) * 4 + lon // 8, (lon // 2) % 4, lon % 2


def device(x, z, y, core):
    return (z % 4) * 8 + y * 2 + core, x * 2 + z // 4


IMAGE_ROWS = 36


def lanes_of(v):
    return lax.broadcasted_iota(jnp.int32, v.shape, 1)


def pack_image(v):
    last = v[IMAGE_ROWS:]
    tail = jnp.concatenate([pltpu.roll(last, 96 - 32 * k, 1) for k in range(3)], 0)
    return jnp.where(lanes_of(tail) < RLON, v[:IMAGE_ROWS], tail)


def unpack_image(v):
    last = jnp.zeros((12, 128), F32)
    for k in range(3):
        piece = pltpu.roll(v[12 * k : 12 * k + 12], 32 + 32 * k, 1)
        last = jnp.where(lanes_of(last) // 32 == k, piece, last)
    return jnp.concatenate([jnp.where(lanes_of(v) < RLON, v, 0.0), last], 0)


def pack_gram(g):
    half = RLON // 2
    top, low = g[:half], g[half:RLON]
    lane, row = lanes_of(top), lax.broadcasted_iota(jnp.int32, top.shape, 0)
    rest = jnp.where(lane <= half, pltpu.roll(top, 1, 1), pltpu.roll(top, 16, 1))
    return jnp.where(lane <= row, pltpu.roll(low, 128 - half, 1), rest)


def unpack_top(v):
    return jnp.where(lanes_of(v) < RLON // 2, pltpu.roll(v, 127, 1), pltpu.roll(v, 112, 1))


def unpack_low(v):
    half = RLON // 2
    square = jnp.concatenate([v, jnp.zeros((128 - half, 128), F32)], 0).T
    return pltpu.roll(square[:half], half, 1)


HEAD = 24


def tree_sum(terms):
    while len(terms) > 1:
        terms = [a + b for a, b in zip(terms[::2], terms[1::2])] + terms[len(terms) // 2 * 2 :]
    return terms[0]


def solve(total_rows, head, rest, image_t, out, yt):
    tiles = RLON // 8
    known = HEAD // 8
    left = [head[8 * r : 8 * r + 8] for r in range(known)]
    right = [image_t[8 * r : 8 * r + 8] for r in range(tiles)]
    sub = lax.broadcasted_iota(jnp.int32, (8, 128), 0)
    diagonal = lax.broadcasted_iota(jnp.int32, (8, 128), 1) - sub
    spread = lambda v: jnp.broadcast_to(v, (8, 128))

    def down(row, r):
        return spread(jnp.sum(jnp.where(diagonal == 8 * r, row, 0.0), axis=1, keepdims=True))

    done = []
    col = [spread(left[0][:, q : q + 1]) for q in range(8)]
    for j in range(tiles):
        at = 8 * j
        d = [[spread(col[q][p : p + 1]) for p in range(q + 1)] for q in range(8)]
        vl = [spread(left[j][p : p + 1]) for p in range(8)]
        vr = [spread(right[j][p : p + 1]) for p in range(8)]
        if j + 1 < len(left):
            col = [spread(left[j + 1][:, at + 8 + q : at + 9 + q]) for q in range(8)]
            m = [down(vl[p], j + 1) for p in range(8)]
        else:
            m = [jnp.zeros((8, 128), F32)] * 8
        for p in range(8):
            inv = lax.rsqrt(d[p][p])
            for q in range(p + 1, 8):
                d[q][p] = d[q][p] * inv
            for q in range(p + 1, 8):
                for r in range(p + 1, q + 1):
                    d[q][r] = d[q][r] - d[q][p] * d[r][p]
            vl[p], vr[p], m[p] = vl[p] * inv, vr[p] * inv, m[p] * inv
            for q in range(p + 1, 8):
                vl[q] = vl[q] - d[q][p] * vl[p]
                vr[q] = vr[q] - d[q][p] * vr[p]
                m[q] = m[q] - d[q][p] * m[p]
        rows = vr[0]
        for p in range(1, 8):
            rows = jnp.where(sub == p, vr[p], rows)
        yt[at : at + 8] = rows
        done.append((vl, vr))
        if j == known - 1:
            late = []
            for r in range(known, tiles):
                terms = [(down(row, r), row, y) for rows in done for row, y in zip(*rows)]
                late.append([tree_sum([t[0] * t[k] for t in terms]) for k in (1, 2)])
            more = rest()
            for r in range(known, tiles):
                left.append(more[8 * (r - known) : 8 * (r - known) + 8] - late[r - known][0])
                right[r] = right[r] - late[r - known][1]
            col = [spread(left[known][:, HEAD + q : HEAD + q + 1]) for q in range(8)]
            continue
        for r in range(j + 1, len(left)):
            if r == j + 1:
                col = [col[q] - tree_sum([m[p] * spread(m[p][q : q + 1]) for p in range(8)]) for q in range(8)]
            else:
                m = [down(vl[p], r) for p in range(8)]
            left[r] = left[r] - tree_sum([m[p] * vl[p] for p in range(8)])
            right[r] = right[r] - tree_sum([m[p] * vr[p] for p in range(8)])
    out[...] = yt[...].T[0:ROWS] * jnp.sqrt(F32(total_rows))


def hooi_kernel(
    total_rows, field, lat, lev_t, old, out,
    fv, lat_in, lev_in, old_in, lats, lvl, proj, xr, pz, wt, wr, ws, wz, wf, img, ir, summed, home, gp, gr, gh, go, gf,
    yt, fsem, csem, passed, sent, xsem, rsem, zsem, isem, hsem, gsem,
):
    x, z, y, core = place()
    me = y * 2 + core

    def send(src, dst, sent, landed, to):
        copy = pltpu.make_async_remote_copy(
            src_ref=src, dst_ref=dst, send_sem=sent, recv_sem=landed, device_id=to, device_id_type=MESH
        )
        copy.start()
        return copy

    def arrived(ref, sem):
        pltpu.make_async_copy(ref, ref, sem).wait()

    loads = [
        pltpu.make_async_copy(
            field.at[pl.ds(at * LATS, rows * LATS)], fv.at[pl.ds(at * LATS, rows * LATS)], fsem.at[k]
        )
        for k, (at, rows) in enumerate(LOADS)
    ]
    small = [
        pltpu.make_async_copy(src, dst, csem.at[k])
        for k, (src, dst) in enumerate(((lev_t, lev_in), (lat, lat_in), (old, old_in)))
    ]
    for load in small + loads:
        load.start()

    way = 1 + 6 * core
    x_peers = [device((x + way * dx) % 4, z, y, core) for dx in (1, 2, 3)]
    z_peers = [device(x, (z + way * dz) % 8, y, core) for dz in range(1, 8)]
    yc_peers = [device(x, z, ((me + j) % 8) // 2, (me + j) % 2) for j in range(1, 8)]
    i_peers = [device((x + way * dx) % 4, (z + way * dz) % 8, y, core) for dx in (2, 1, 3, 0) for dz in (2, 6)]
    g_steps = [(dy, dz) for dy in range(4) for dz in (0, 1, 7, 2 if dy < 2 else 6)][1:]
    g_steps.sort(key=lambda step: -min(step[0], 4 - step[0]) - min(step[1], 8 - step[1]))
    g_peers = [device(x, (z + way * dz) % 8, (y + way * dy) % 4, core) for dy, dz in g_steps]

    greeted = [x_peers[1], z_peers[1], z_peers[5]] + [yc_peers[k] for k in FAR_FIRST]
    greeted += [x_peers[0], x_peers[2], z_peers[0], z_peers[6]]
    barrier = pltpu.get_barrier_semaphore()
    for peer in greeted:
        pl.semaphore_signal(barrier, inc=1, device_id=peer, device_id_type=MESH)
    told = [z_peers[1], z_peers[5]]

    small[0].wait()
    small[1].wait()
    levh, levl = split(lev_in[...])
    lev2 = jnp.concatenate(
        [jnp.concatenate([levh, levh], 1), jnp.concatenate([levl, jnp.zeros_like(levl)], 1)], 0
    )
    lats[...] = jnp.zeros_like(lats)
    lats[0:LATS, 0:RLAT] = lat_in[...]
    lat_pad = lats[...]
    lane = lax.broadcasted_iota(jnp.int32, (128, 128), 1)
    lat_hi, lat_lo = [], []
    for u in range(SLABS):
        tail = jnp.where(lane >= RLAT, pltpu.roll(lat_pad, 96 - 32 * u, 1), 0.0)
        hi, lo = split(jnp.concatenate([lat_pad, tail], 0))
        lat_hi.append(hi)
        lat_lo.append(lo)

    def levels(k):
        def one(i, carry):
            f = fv[pl.ds(pl.multiple_of(i * LATS, LATS), LATS), :]
            fh, fl = split(f)
            both = jnp.concatenate([fh, fl], 1)
            both = jnp.concatenate([both, jnp.zeros((128 - LATS, 256), BF16)], 0)
            r = lax.dot_general(lev2, both, (((1,), (1,)), ((), ())), preferred_element_type=F32)
            lvl[pl.ds(lax.rem(i, ROWS), RLEV, stride=ROWS), :] = r[:RLEV] + r[RLEV:]
            return carry

        loads[k].wait()
        at, rows = LOADS[k]
        lax.fori_loop(at, at + rows, one, 0, unroll=24)

    def latitudes(t, u):
        parts = [
            jnp.concatenate([lvl[pl.ds((4 * d + v) * ROWS, ROWS), :] for d in range(8)], 0) for v in (u, 3)
        ]
        hi, lo = split(jnp.concatenate(parts, 1))
        r = (
            jnp.dot(hi, lat_hi[u], preferred_element_type=F32)
            + jnp.dot(lo, lat_hi[u], preferred_element_type=F32)
            + jnp.dot(hi, lat_lo[u], preferred_element_type=F32)
        )
        for d in range(8):
            proj[2 * (t * SLABS + u) + d % 2, d // 2] = r[d * ROWS : (d + 1) * ROWS]

    for t in range(TIMES):
        for k in ((0, 1), (2,))[t]:
            levels(k)
        for u in range(SLABS):
            latitudes(t, u)
            if t + u == 0:
                pl.semaphore_wait(barrier, len(greeted))
                for peer in told:
                    pl.semaphore_signal(passed, inc=1, device_id=peer, device_id_type=MESH)
            for g, (first, count) in enumerate(GROUPS):
                if first // 2 == t * SLABS + u:
                    blocks = pl.ds(first, count)
                    for k in (1, 0, 2):
                        send(proj.at[blocks, (x + way * (k + 1)) % 4], xr.at[blocks, k], sent, xsem.at[g], x_peers[k])

    pl.semaphore_wait(passed, len(told))
    small[2].wait()
    old_t = split(old_in[...].T)
    acc = jnp.zeros((ROWS, RLON), F32)

    for at, kind, g in SCHEDULE:
        first, count = GROUPS[g]
        blocks = pl.ds(first, count)
        if kind == 0:
            arrived(xr.at[blocks], xsem.at[g])
            for b in range(first, first + count):
                pz[b] = proj[b, x] + xr[b, 0] + xr[b, 1] + xr[b, 2]
                wt[b] = dot3(old_t, split(pz[b]), ((1,), (0,)))
            for k in FAR_FIRST:
                part = pl.ds(PART * ((me + k + 1) % 8), PART)
                send(wt.at[blocks, part], wr.at[blocks, k], sent, rsem.at[g], yc_peers[k])
        elif kind == 1:
            arrived(wr.at[blocks], rsem.at[g])
            for b in range(first, first + count):
                part = wt[b, pl.ds(PART * me, PART)]
                for k in range(7):
                    part = part + wr[b, k]
                ws[b] = part
            for k in FAR_FIRST:
                send(ws.at[blocks], wz.at[blocks, k], sent, zsem.at[g], z_peers[k])
        elif kind == 2:
            arrived(wz.at[blocks], zsem.at[g])
            for b in range(first, first + count):
                part = ws[b]
                for k in range(7):
                    part = part + wz[b, k]
                wf[b, pl.ds(PART * me, PART)] = part
            mine = wf.at[blocks, pl.ds(PART * me, PART)]
            for k in FAR_FIRST:
                send(mine, mine, sent, xsem.at[g], yc_peers[k])
        else:
            arrived(wr.at[blocks], xsem.at[g])
            for b in range(first, first + count):
                acc = acc + dot3(split(pz[b]), split(wf[b]), ((1,), (1,)))
    img[...] = pack_image(jnp.concatenate([acc, jnp.zeros((ROWS, 128 - RLON), F32)], 1))
    for k in range(8):
        send(img, ir.at[k], sent, isem, i_peers[k])
    arrived(ir, isem)
    image = ir[0]
    for k in range(1, 8):
        image = image + ir[k]
    image = unpack_image(image)
    summed[...] = image
    send(summed, home, sent, hsem, z_peers[1])
    gp[...] = pack_gram(
        lax.dot_general(image, image, (((0,), (0,)), ((), ())), precision=HIGHEST, preferred_element_type=F32)
    )
    half = RLON // 4
    sibling = device(x, z, y, 1 - core)
    mine, other = (pl.ds(pl.multiple_of(half * c, 8), half) for c in (1 - core, core))
    send(gp.at[other], gr, sent, gsem.at[0], sibling)
    arrived(gr, gsem.at[0])
    gh[...] = gp[mine] + gr[...]
    for k in range(15):
        send(gh, go.at[k], sent, gsem.at[1], g_peers[k])
    arrived(home, hsem)
    image_t = jnp.concatenate([home[...].T[0:RLON], jnp.zeros((RLON, 128 - ROWS), F32)], 1)
    arrived(go, gsem.at[1])
    total = gh[...]
    for k in range(15):
        total = total + go[k]
    gf[mine] = total
    send(gf.at[mine], gf.at[mine], sent, gsem.at[2], sibling)

    @pl.when(core == 0)
    def _():
        arrived(gr, gsem.at[2])

    def rest():
        @pl.when(core == 1)
        def _():
            arrived(gr, gsem.at[2])

        return jnp.concatenate([unpack_top(gf[HEAD:]), unpack_low(gf[...])], 0)

    solve(total_rows, unpack_top(gf[0:HEAD]), rest, image_t, out, yt)

    refs = (xr, wr, wz, wr, ir, home, gr, go, gr)
    arrived(fv.at[pl.ds(0, sum(math.prod(ref.shape) // 128 for ref in refs))], sent)


def body(field, lat_factor, lev_factor, old_factor):
    vmem = pl.BlockSpec(memory_space=pltpu.VMEM)
    dma = pltpu.SemaphoreType.DMA
    field = field.reshape(TIMES * ROWS * LATS, LEVS)
    total_rows = ROWS * lax.axis_size("lon")
    return pl.pallas_call(
        functools.partial(hooi_kernel, total_rows),
        out_shape=pltpu.VMEM((ROWS, RLON), F32),
        in_specs=[pl.BlockSpec(memory_space=pltpu.HBM)] * 4,
        out_specs=vmem,
        scratch_shapes=[
            pltpu.VMEM((TIMES * ROWS * LATS, LEVS), F32),
            pltpu.VMEM((LATS, RLAT), F32),
            pltpu.VMEM((RLEV, LEVS), F32),
            pltpu.VMEM((ROWS, RLON), F32),
            pltpu.VMEM((128, 128), F32),
            pltpu.VMEM((RLEV * ROWS, 128), F32),
            pltpu.VMEM((BLOCKS, 4, ROWS, 128), F32),
            pltpu.VMEM((BLOCKS, 3, ROWS, 128), F32),
            pltpu.VMEM((BLOCKS, ROWS, 128), F32),
            pltpu.VMEM((BLOCKS, RLON, 128), F32),
            pltpu.VMEM((BLOCKS, 7, PART, 128), F32),
            pltpu.VMEM((BLOCKS, PART, 128), F32),
            pltpu.VMEM((BLOCKS, 7, PART, 128), F32),
            pltpu.VMEM((BLOCKS, RLON, 128), F32),
            pltpu.VMEM((IMAGE_ROWS, 128), F32),
            pltpu.VMEM((8, IMAGE_ROWS, 128), F32),
            pltpu.VMEM((ROWS, 128), F32),
            pltpu.VMEM((ROWS, 128), F32),
            pltpu.VMEM((RLON // 2, 128), F32),
            pltpu.VMEM((RLON // 4, 128), F32),
            pltpu.VMEM((RLON // 4, 128), F32),
            pltpu.VMEM((15, RLON // 4, 128), F32),
            pltpu.VMEM((RLON // 2, 128), F32),
            pltpu.VMEM((RLON, 128), F32),
            dma((3,)),
            dma((3,)),
            pltpu.SemaphoreType.REGULAR,
            dma,
            dma((len(GROUPS),)),
            dma((len(GROUPS),)),
            dma((len(GROUPS),)),
            dma,
            dma,
            dma((3,)),
        ],
        compiler_params=pltpu.CompilerParams(
            collective_id=0, has_side_effects=True, vmem_limit_bytes=48 * 1024 * 1024
        ),
    )(*(pltpu.with_memory_space_constraint(v, pltpu.HBM) for v in (field, lat_factor, lev_factor.T, old_factor)))


def solution(mesh):
    placed = (P(None, "lon", "lat", None), P("lat", None), P(), P("lon", None))
    return jax.shard_map(
        body, mesh=mesh, in_specs=placed, out_specs=P("lon", None), check_vma=False
    )
```

```python
import functools
import math

import jax
import jax.numpy as jnp
from jax import lax
from jax.experimental import pallas as pl
from jax.experimental.pallas import tpu as pltpu
from jax.sharding import PartitionSpec as P

MESH = pl.DeviceIdType.MESH
HIGHEST = lax.Precision.HIGHEST
F32, BF16 = jnp.float32, jnp.bfloat16
TIMES, ROWS, LATS, LEVS = 2, 48, 96, 128
RLAT, RLEV, RLON = 96, 32, 96
SLABS = 3
BLOCKS = TIMES * SLABS * 2
LOADS = (0, 24), (24, 24), (48, 48)
FAR_FIRST = (3, 2, 4, 1, 5, 0, 6)
PART = RLON // 8
GROUPS = tuple((b, 1) for b in range(BLOCKS))
SCHEDULE = sorted(
    (first + count + lag, kind, g) for g, (first, count) in enumerate(GROUPS) for kind, lag in enumerate((0, 4.6, 11, 16))
)


def split(v):
    hi = v.astype(BF16)
    return hi, (v - hi.astype(F32)).astype(BF16)


def dot3(a, b, dims):
    (ah, al), (bh, bl) = a, b
    dot = functools.partial(lax.dot_general, dimension_numbers=(dims, ((), ())), preferred_element_type=F32)
    return dot(ah, bh) + (dot(al, bh) + dot(ah, bl))


def place():
    lon, lat = lax.axis_index("lon"), lax.axis_index("lat")
    return lat // 2, (lat % 2) * 4 + lon // 8, (lon // 2) % 4, lon % 2


def device(x, z, y, core):
    return (z % 4) * 8 + y * 2 + core, x * 2 + z // 4


IMAGE_ROWS = 36


def lanes_of(v):
    return lax.broadcasted_iota(jnp.int32, v.shape, 1)


def pack_image(v):
    last = v[IMAGE_ROWS:]
    tail = jnp.concatenate([pltpu.roll(last, 96 - 32 * k, 1) for k in range(3)], 0)
    return jnp.where(lanes_of(tail) < RLON, v[:IMAGE_ROWS], tail)


def unpack_image(v):
    last = jnp.zeros((12, 128), F32)
    for k in range(3):
        piece = pltpu.roll(v[12 * k : 12 * k + 12], 32 + 32 * k, 1)
        last = jnp.where(lanes_of(last) // 32 == k, piece, last)
    return jnp.concatenate([jnp.where(lanes_of(v) < RLON, v, 0.0), last], 0)


def pack_gram(g):
    half = RLON // 2
    top, low = g[:half], g[half:RLON]
    lane, row = lanes_of(top), lax.broadcasted_iota(jnp.int32, top.shape, 0)
    rest = jnp.where(lane <= half, pltpu.roll(top, 1, 1), pltpu.roll(top, 16, 1))
    return jnp.where(lane <= row, pltpu.roll(low, 128 - half, 1), rest)


def unpack_top(v):
    return jnp.where(lanes_of(v) < RLON // 2, pltpu.roll(v, 127, 1), pltpu.roll(v, 112, 1))


def unpack_low(v):
    half = RLON // 2
    square = jnp.concatenate([v, jnp.zeros((128 - half, 128), F32)], 0).T
    return pltpu.roll(square[:half], half, 1)


HEAD = 24


def tree_sum(terms):
    while len(terms) > 1:
        terms = [a + b for a, b in zip(terms[::2], terms[1::2])] + terms[len(terms) // 2 * 2 :]
    return terms[0]


def solve(total_rows, head, rest, image_t, out, yt):
    tiles = RLON // 8
    known = HEAD // 8
    left = [head[8 * r : 8 * r + 8] for r in range(known)]
    right = [image_t[8 * r : 8 * r + 8] for r in range(tiles)]
    sub = lax.broadcasted_iota(jnp.int32, (8, 128), 0)
    diagonal = lax.broadcasted_iota(jnp.int32, (8, 128), 1) - sub
    spread = lambda v: jnp.broadcast_to(v, (8, 128))

    def down(row, r):
        return spread(jnp.sum(jnp.where(diagonal == 8 * r, row, 0.0), axis=1, keepdims=True))

    done = []
    col = [spread(left[0][:, q : q + 1]) for q in range(8)]
    for j in range(tiles):
        at = 8 * j
        d = [[spread(col[q][p : p + 1]) for p in range(q + 1)] for q in range(8)]
        vl = [spread(left[j][p : p + 1]) for p in range(8)]
        vr = [spread(right[j][p : p + 1]) for p in range(8)]
        if j + 1 < len(left):
            col = [spread(left[j + 1][:, at + 8 + q : at + 9 + q]) for q in range(8)]
            m = [down(vl[p], j + 1) for p in range(8)]
        else:
            m = [jnp.zeros((8, 128), F32)] * 8
        for p in range(8):
            inv = lax.rsqrt(d[p][p])
            for q in range(p + 1, 8):
                d[q][p] = d[q][p] * inv
            for q in range(p + 1, 8):
                for r in range(p + 1, q + 1):
                    d[q][r] = d[q][r] - d[q][p] * d[r][p]
            vl[p], vr[p], m[p] = vl[p] * inv, vr[p] * inv, m[p] * inv
            for q in range(p + 1, 8):
                vl[q] = vl[q] - d[q][p] * vl[p]
                vr[q] = vr[q] - d[q][p] * vr[p]
                m[q] = m[q] - d[q][p] * m[p]
        rows = vr[0]
        for p in range(1, 8):
            rows = jnp.where(sub == p, vr[p], rows)
        yt[at : at + 8] = rows
        done.append((vl, vr))
        if j == known - 1:
            late = []
            for r in range(known, tiles):
                terms = [(down(row, r), row, y) for rows in done for row, y in zip(*rows)]
                late.append([tree_sum([t[0] * t[k] for t in terms]) for k in (1, 2)])
            more = rest()
            for r in range(known, tiles):
                left.append(more[8 * (r - known) : 8 * (r - known) + 8] - late[r - known][0])
                right[r] = right[r] - late[r - known][1]
            col = [spread(left[known][:, HEAD + q : HEAD + q + 1]) for q in range(8)]
            continue
        for r in range(j + 1, len(left)):
            if r == j + 1:
                col = [col[q] - tree_sum([m[p] * spread(m[p][q : q + 1]) for p in range(8)]) for q in range(8)]
            else:
                m = [down(vl[p], r) for p in range(8)]
            left[r] = left[r] - tree_sum([m[p] * vl[p] for p in range(8)])
            right[r] = right[r] - tree_sum([m[p] * vr[p] for p in range(8)])
    out[...] = yt[...].T[0:ROWS] * jnp.sqrt(F32(total_rows))


def hooi_kernel(
    total_rows, field, lat, lev_t, old, out,
    fv, lat_in, lev_in, old_in, lats, lvl, proj, xr, pz, wt, wr, ws, wz, wf, img, ir, summed, home, gp, gr, gh, go, gf,
    yt, fsem, csem, passed, sent, xsem, rsem, zsem, isem, hsem, gsem,
):
    x, z, y, core = place()
    me = y * 2 + core

    def send(src, dst, sent, landed, to):
        copy = pltpu.make_async_remote_copy(
            src_ref=src, dst_ref=dst, send_sem=sent, recv_sem=landed, device_id=to, device_id_type=MESH
        )
        copy.start()
        return copy

    def arrived(ref, sem):
        pltpu.make_async_copy(ref, ref, sem).wait()

    loads = [
        pltpu.make_async_copy(
            field.at[pl.ds(at * LATS, rows * LATS)], fv.at[pl.ds(at * LATS, rows * LATS)], fsem.at[k]
        )
        for k, (at, rows) in enumerate(LOADS)
    ]
    small = [
        pltpu.make_async_copy(src, dst, csem.at[k])
        for k, (src, dst) in enumerate(((lev_t, lev_in), (lat, lat_in), (old, old_in)))
    ]
    for load in small + loads:
        load.start()

    x_peers = [device((x + dx) % 4, z, y, core) for dx in (1, 2, 3)]
    z_peers = [device(x, (z + dz) % 8, y, core) for dz in range(1, 8)]
    yc_steps = [(2, 0), (2, 1), (1, 0), (1, 1), (3, 0), (3, 1), (0, 1)]
    yc_peers = [device(x, z, (y + dy) % 4, (core + dc) % 2) for dy, dc in yc_steps]
    yc_parts = [PART * ((y + dy) % 4 * 2 + (core + dc) % 2) for dy, dc in yc_steps]
    i_peers = [device((x + dx) % 4, (z + dz) % 8, y, core) for dx in (2, 1, 3, 0) for dz in (2, 6)]
    g_steps = [(dy, dz) for dy in range(4) for dz in (0, 1, 7, 2 if dy < 2 else 6)][1:]
    g_steps.sort(key=lambda step: -min(step[0], 4 - step[0]) - min(step[1], 8 - step[1]))
    g_peers = [device(x, (z + dz) % 8, (y + dy) % 4, core) for dy, dz in g_steps]

    greeted = [x_peers[1], z_peers[1], z_peers[5]] + yc_peers
    greeted += [x_peers[0], x_peers[2], z_peers[0], z_peers[6]]
    barrier = pltpu.get_barrier_semaphore()
    for peer in greeted:
        pl.semaphore_signal(barrier, inc=1, device_id=peer, device_id_type=MESH)
    told = [z_peers[1], z_peers[5]]

    small[0].wait()
    small[1].wait()
    levh, levl = split(lev_in[...])
    lev2 = jnp.concatenate(
        [jnp.concatenate([levh, levh], 1), jnp.concatenate([levl, jnp.zeros_like(levl)], 1)], 0
    )
    lats[...] = jnp.zeros_like(lats)
    lats[0:LATS, 0:RLAT] = lat_in[...]
    lat_pad = lats[...]
    lane = lax.broadcasted_iota(jnp.int32, (128, 128), 1)
    lat_hi, lat_lo = [], []
    for u in range(SLABS):
        tail = jnp.where(lane >= RLAT, pltpu.roll(lat_pad, 96 - 32 * u, 1), 0.0)
        hi, lo = split(jnp.concatenate([lat_pad, tail], 0))
        lat_hi.append(hi)
        lat_lo.append(lo)

    def levels(k):
        def one(i, carry):
            f = fv[pl.ds(pl.multiple_of(i * LATS, LATS), LATS), :]
            fh, fl = split(f)
            both = jnp.concatenate([fh, fl], 1)
            both = jnp.concatenate([both, jnp.zeros((128 - LATS, 256), BF16)], 0)
            r = lax.dot_general(lev2, both, (((1,), (1,)), ((), ())), preferred_element_type=F32)
            lvl[pl.ds(lax.rem(i, ROWS), RLEV, stride=ROWS), :] = r[:RLEV] + r[RLEV:]
            return carry

        loads[k].wait()
        at, rows = LOADS[k]
        lax.fori_loop(at, at + rows, one, 0, unroll=24)

    def latitudes(t, u):
        parts = [
            jnp.concatenate([lvl[pl.ds((4 * d + v) * ROWS, ROWS), :] for d in range(8)], 0) for v in (u, 3)
        ]
        hi, lo = split(jnp.concatenate(parts, 1))
        r = (
            jnp.dot(hi, lat_hi[u], preferred_element_type=F32)
            + jnp.dot(lo, lat_hi[u], preferred_element_type=F32)
            + jnp.dot(hi, lat_lo[u], preferred_element_type=F32)
        )
        for d in range(8):
            proj[2 * (t * SLABS + u) + d % 2, d // 2] = r[d * ROWS : (d + 1) * ROWS]

    for t in range(TIMES):
        for k in ((0, 1), (2,))[t]:
            levels(k)
        for u in range(SLABS):
            latitudes(t, u)
            if t + u == 0:
                pl.semaphore_wait(barrier, len(greeted))
                for peer in told:
                    pl.semaphore_signal(passed, inc=1, device_id=peer, device_id_type=MESH)
            for g, (first, count) in enumerate(GROUPS):
                if first // 2 == t * SLABS + u:
                    blocks = pl.ds(first, count)
                    for k in (1, 0, 2):
                        send(proj.at[blocks, (x + k + 1) % 4], xr.at[blocks, k], sent, xsem.at[g], x_peers[k])

    pl.semaphore_wait(passed, len(told))
    small[2].wait()
    old_t = split(old_in[...].T)
    acc = jnp.zeros((ROWS, RLON), F32)

    for at, kind, g in SCHEDULE:
        first, count = GROUPS[g]
        blocks = pl.ds(first, count)
        if kind == 0:
            arrived(xr.at[blocks], xsem.at[g])
            for b in range(first, first + count):
                pz[b] = proj[b, x] + xr[b, 0] + xr[b, 1] + xr[b, 2]
                wt[b] = dot3(old_t, split(pz[b]), ((1,), (0,)))
            for k in range(7):
                part = pl.ds(yc_parts[k], PART)
                send(wt.at[blocks, part], wr.at[blocks, k], sent, rsem.at[g], yc_peers[k])
        elif kind == 1:
            arrived(wr.at[blocks], rsem.at[g])
            for b in range(first, first + count):
                part = wt[b, pl.ds(PART * me, PART)]
                for k in range(7):
                    part = part + wr[b, k]
                ws[b] = part
            for k in FAR_FIRST:
                send(ws.at[blocks], wz.at[blocks, k], sent, zsem.at[g], z_peers[k])
        elif kind == 2:
            arrived(wz.at[blocks], zsem.at[g])
            for b in range(first, first + count):
                part = ws[b]
                for k in range(7):
                    part = part + wz[b, k]
                wf[b, pl.ds(PART * me, PART)] = part
            mine = wf.at[blocks, pl.ds(PART * me, PART)]
            for k in range(7):
                send(mine, mine, sent, xsem.at[g], yc_peers[k])
        else:
            arrived(wr.at[blocks], xsem.at[g])
            for b in range(first, first + count):
                acc = acc + dot3(split(pz[b]), split(wf[b]), ((1,), (1,)))
    img[...] = pack_image(jnp.concatenate([acc, jnp.zeros((ROWS, 128 - RLON), F32)], 1))
    for k in range(8):
        send(img, ir.at[k], sent, isem, i_peers[k])
    arrived(ir, isem)
    image = ir[0]
    for k in range(1, 8):
        image = image + ir[k]
    image = unpack_image(image)
    summed[...] = image
    send(summed, home, sent, hsem, z_peers[1])
    gp[...] = pack_gram(
        lax.dot_general(image, image, (((0,), (0,)), ((), ())), precision=HIGHEST, preferred_element_type=F32)
    )
    half = RLON // 4
    sibling = device(x, z, y, 1 - core)
    mine, other = (pl.ds(pl.multiple_of(half * c, 8), half) for c in (1 - core, core))
    send(gp.at[other], gr, sent, gsem.at[0], sibling)
    arrived(gr, gsem.at[0])
    gh[...] = gp[mine] + gr[...]
    for k in range(15):
        send(gh, go.at[k], sent, gsem.at[1], g_peers[k])
    arrived(home, hsem)
    image_t = jnp.concatenate([home[...].T[0:RLON], jnp.zeros((RLON, 128 - ROWS), F32)], 1)
    arrived(go, gsem.at[1])
    total = gh[...]
    for k in range(15):
        total = total + go[k]
    gf[mine] = total
    send(gf.at[mine], gf.at[mine], sent, gsem.at[2], sibling)

    @pl.when(core == 0)
    def _():
        arrived(gr, gsem.at[2])

    def rest():
        @pl.when(core == 1)
        def _():
            arrived(gr, gsem.at[2])

        return jnp.concatenate([unpack_top(gf[HEAD:]), unpack_low(gf[...])], 0)

    solve(total_rows, unpack_top(gf[0:HEAD]), rest, image_t, out, yt)

    refs = (xr, wr, wz, wr, ir, home, gr, go, gr)
    arrived(fv.at[pl.ds(0, sum(math.prod(ref.shape) // 128 for ref in refs))], sent)


def body(field, lat_factor, lev_factor, old_factor):
    vmem = pl.BlockSpec(memory_space=pltpu.VMEM)
    dma = pltpu.SemaphoreType.DMA
    field = field.reshape(TIMES * ROWS * LATS, LEVS)
    total_rows = ROWS * lax.axis_size("lon")
    return pl.pallas_call(
        functools.partial(hooi_kernel, total_rows),
        out_shape=pltpu.VMEM((ROWS, RLON), F32),
        in_specs=[pl.BlockSpec(memory_space=pltpu.HBM)] * 4,
        out_specs=vmem,
        scratch_shapes=[
            pltpu.VMEM((TIMES * ROWS * LATS, LEVS), F32),
            pltpu.VMEM((LATS, RLAT), F32),
            pltpu.VMEM((RLEV, LEVS), F32),
            pltpu.VMEM((ROWS, RLON), F32),
            pltpu.VMEM((128, 128), F32),
            pltpu.VMEM((RLEV * ROWS, 128), F32),
            pltpu.VMEM((BLOCKS, 4, ROWS, 128), F32),
            pltpu.VMEM((BLOCKS, 3, ROWS, 128), F32),
            pltpu.VMEM((BLOCKS, ROWS, 128), F32),
            pltpu.VMEM((BLOCKS, RLON, 128), F32),
            pltpu.VMEM((BLOCKS, 7, PART, 128), F32),
            pltpu.VMEM((BLOCKS, PART, 128), F32),
            pltpu.VMEM((BLOCKS, 7, PART, 128), F32),
            pltpu.VMEM((BLOCKS, RLON, 128), F32),
            pltpu.VMEM((IMAGE_ROWS, 128), F32),
            pltpu.VMEM((8, IMAGE_ROWS, 128), F32),
            pltpu.VMEM((ROWS, 128), F32),
            pltpu.VMEM((ROWS, 128), F32),
            pltpu.VMEM((RLON // 2, 128), F32),
            pltpu.VMEM((RLON // 4, 128), F32),
            pltpu.VMEM((RLON // 4, 128), F32),
            pltpu.VMEM((15, RLON // 4, 128), F32),
            pltpu.VMEM((RLON // 2, 128), F32),
            pltpu.VMEM((RLON, 128), F32),
            dma((3,)),
            dma((3,)),
            pltpu.SemaphoreType.REGULAR,
            dma,
            dma((len(GROUPS),)),
            dma((len(GROUPS),)),
            dma((len(GROUPS),)),
            dma,
            dma,
            dma((3,)),
        ],
        compiler_params=pltpu.CompilerParams(
            collective_id=0, has_side_effects=True, vmem_limit_bytes=48 * 1024 * 1024
        ),
    )(*(pltpu.with_memory_space_constraint(v, pltpu.HBM) for v in (field, lat_factor, lev_factor.T, old_factor)))


def solution(mesh):
    placed = (P(None, "lon", "lat", None), P("lat", None), P(), P("lon", None))
    return jax.shard_map(
        body, mesh=mesh, in_specs=placed, out_specs=P("lon", None), check_vma=False
    )
```

```python
import functools
import math

import jax
import jax.numpy as jnp
from jax import lax
from jax.experimental import pallas as pl
from jax.experimental.pallas import tpu as pltpu
from jax.sharding import PartitionSpec as P

MESH = pl.DeviceIdType.MESH
HIGHEST = lax.Precision.HIGHEST
F32, BF16 = jnp.float32, jnp.bfloat16
TIMES, ROWS, LATS, LEVS = 2, 48, 96, 128
RLAT, RLEV, RLON = 96, 32, 96
SLABS = 3
BLOCKS = TIMES * SLABS * 2
LOADS = (0, 24), (24, 24), (48, 48)
FAR_FIRST = (3, 2, 4, 1, 5, 0, 6)
PART = RLON // 8
GROUPS = tuple((b, 1) for b in range(BLOCKS))
SCHEDULE = sorted(
    (first + count + lag, kind, g) for g, (first, count) in enumerate(GROUPS) for kind, lag in enumerate((0, 4.6, 11, 16))
)


def split(v):
    hi = v.astype(BF16)
    return hi, (v - hi.astype(F32)).astype(BF16)


def dot3(a, b, dims):
    (ah, al), (bh, bl) = a, b
    dot = functools.partial(lax.dot_general, dimension_numbers=(dims, ((), ())), preferred_element_type=F32)
    return dot(ah, bh) + (dot(al, bh) + dot(ah, bl))


def place():
    lon, lat = lax.axis_index("lon"), lax.axis_index("lat")
    return lat // 2, (lat % 2) * 4 + lon // 8, (lon // 2) % 4, lon % 2


def device(x, z, y, core):
    return (z % 4) * 8 + y * 2 + core, x * 2 + z // 4


IMAGE_ROWS = 36


def lanes_of(v):
    return lax.broadcasted_iota(jnp.int32, v.shape, 1)


def pack_image(v):
    last = v[IMAGE_ROWS:]
    tail = jnp.concatenate([pltpu.roll(last, 96 - 32 * k, 1) for k in range(3)], 0)
    return jnp.where(lanes_of(tail) < RLON, v[:IMAGE_ROWS], tail)


def unpack_image(v):
    last = jnp.zeros((12, 128), F32)
    for k in range(3):
        piece = pltpu.roll(v[12 * k : 12 * k + 12], 32 + 32 * k, 1)
        last = jnp.where(lanes_of(last) // 32 == k, piece, last)
    return jnp.concatenate([jnp.where(lanes_of(v) < RLON, v, 0.0), last], 0)


def pack_gram(g):
    half = RLON // 2
    top, low = g[:half], g[half:RLON]
    lane, row = lanes_of(top), lax.broadcasted_iota(jnp.int32, top.shape, 0)
    rest = jnp.where(lane <= half, pltpu.roll(top, 1, 1), pltpu.roll(top, 16, 1))
    return jnp.where(lane <= row, pltpu.roll(low, 128 - half, 1), rest)


def unpack_top(v):
    return jnp.where(lanes_of(v) < RLON // 2, pltpu.roll(v, 127, 1), pltpu.roll(v, 112, 1))


def unpack_low(v):
    half = RLON // 2
    square = jnp.concatenate([v, jnp.zeros((128 - half, 128), F32)], 0).T
    return pltpu.roll(square[:half], half, 1)


HEAD = 24


def tree_sum(terms):
    while len(terms) > 1:
        terms = [a + b for a, b in zip(terms[::2], terms[1::2])] + terms[len(terms) // 2 * 2 :]
    return terms[0]


def solve(total_rows, head, rest, image_t, out, yt):
    tiles = RLON // 8
    known = HEAD // 8
    left = [head[8 * r : 8 * r + 8] for r in range(known)]
    right = [image_t[8 * r : 8 * r + 8] for r in range(tiles)]
    sub = lax.broadcasted_iota(jnp.int32, (8, 128), 0)
    diagonal = lax.broadcasted_iota(jnp.int32, (8, 128), 1) - sub
    spread = lambda v: jnp.broadcast_to(v, (8, 128))

    def down(row, r):
        return spread(jnp.sum(jnp.where(diagonal == 8 * r, row, 0.0), axis=1, keepdims=True))

    done = []
    col = [spread(left[0][:, q : q + 1]) for q in range(8)]
    for j in range(tiles):
        at = 8 * j
        d = [[spread(col[q][p : p + 1]) for p in range(q + 1)] for q in range(8)]
        vl = [spread(left[j][p : p + 1]) for p in range(8)]
        vr = [spread(right[j][p : p + 1]) for p in range(8)]
        if j + 1 < len(left):
            col = [spread(left[j + 1][:, at + 8 + q : at + 9 + q]) for q in range(8)]
            m = [down(vl[p], j + 1) for p in range(8)]
        else:
            m = [jnp.zeros((8, 128), F32)] * 8
        for p in range(8):
            inv = lax.rsqrt(d[p][p])
            for q in range(p + 1, 8):
                d[q][p] = d[q][p] * inv
            for q in range(p + 1, 8):
                for r in range(p + 1, q + 1):
                    d[q][r] = d[q][r] - d[q][p] * d[r][p]
            vl[p], vr[p], m[p] = vl[p] * inv, vr[p] * inv, m[p] * inv
            for q in range(p + 1, 8):
                vl[q] = vl[q] - d[q][p] * vl[p]
                vr[q] = vr[q] - d[q][p] * vr[p]
                m[q] = m[q] - d[q][p] * m[p]
        rows = vr[0]
        for p in range(1, 8):
            rows = jnp.where(sub == p, vr[p], rows)
        yt[at : at + 8] = rows
        done.append((vl, vr))
        if j == known - 1:
            late = []
            for r in range(known, tiles):
                terms = [(down(row, r), row, y) for rows in done for row, y in zip(*rows)]
                late.append([tree_sum([t[0] * t[k] for t in terms]) for k in (1, 2)])
            more = rest()
            for r in range(known, tiles):
                left.append(more[8 * (r - known) : 8 * (r - known) + 8] - late[r - known][0])
                right[r] = right[r] - late[r - known][1]
            col = [spread(left[known][:, HEAD + q : HEAD + q + 1]) for q in range(8)]
            continue
        for r in range(j + 1, len(left)):
            if r == j + 1:
                col = [col[q] - tree_sum([m[p] * spread(m[p][q : q + 1]) for p in range(8)]) for q in range(8)]
            else:
                m = [down(vl[p], r) for p in range(8)]
            left[r] = left[r] - tree_sum([m[p] * vl[p] for p in range(8)])
            right[r] = right[r] - tree_sum([m[p] * vr[p] for p in range(8)])
    out[...] = yt[...].T[0:ROWS] * jnp.sqrt(F32(total_rows))


def hooi_kernel(
    total_rows, field, lat, lev_t, old, out,
    fv, lat_in, lev_in, old_in, lats, lvl, proj, xr, pz, wt, wr, ws, wz, wf, img, ir, summed, home, gp, gr, gh, go, gf,
    yt, fsem, csem, passed, sent, xsem, rsem, zsem, isem, hsem, gsem,
):
    x, z, y, core = place()
    me = y * 2 + core

    def send(src, dst, sent, landed, to):
        copy = pltpu.make_async_remote_copy(
            src_ref=src, dst_ref=dst, send_sem=sent, recv_sem=landed, device_id=to, device_id_type=MESH
        )
        copy.start()
        return copy

    def arrived(ref, sem):
        pltpu.make_async_copy(ref, ref, sem).wait()

    loads = [
        pltpu.make_async_copy(
            field.at[pl.ds(at * LATS, rows * LATS)], fv.at[pl.ds(at * LATS, rows * LATS)], fsem.at[k]
        )
        for k, (at, rows) in enumerate(LOADS)
    ]
    small = [
        pltpu.make_async_copy(src, dst, csem.at[k])
        for k, (src, dst) in enumerate(((lev_t, lev_in), (lat, lat_in), (old, old_in)))
    ]
    for load in small + loads:
        load.start()

    x_peers = [device((x + dx) % 4, z, y, core) for dx in (1, 2, 3)]
    z_peers = [device(x, (z + dz) % 8, y, core) for dz in range(1, 8)]
    yc_steps = [(2, 0), (2, 1), (1, 0), (1, 1), (3, 0), (3, 1), (0, 1)]
    yc_peers = [device(x, z, (y + dy) % 4, (core + dc) % 2) for dy, dc in yc_steps]
    yc_parts = [PART * ((y + dy) % 4 * 2 + (core + dc) % 2) for dy, dc in yc_steps]
    i_peers = [device((x + dx) % 4, (z + dz) % 8, y, core) for dx in (2, 1, 3, 0) for dz in (2, 6)]
    g_steps = [(dy, dz) for dy in range(4) for dz in (0, 1, 7, 2 if dy < 2 else 6)][1:]
    g_steps.sort(key=lambda step: -min(step[0], 4 - step[0]) - min(step[1], 8 - step[1]))
    g_peers = [device(x, (z + dz) % 8, (y + dy) % 4, core) for dy, dz in g_steps]

    greeted = [x_peers[1], z_peers[1], z_peers[5]] + yc_peers
    greeted += [x_peers[0], x_peers[2], z_peers[0], z_peers[6]]
    barrier = pltpu.get_barrier_semaphore()
    for peer in greeted:
        pl.semaphore_signal(barrier, inc=1, device_id=peer, device_id_type=MESH)
    told = [z_peers[1], z_peers[5]]

    small[0].wait()
    small[1].wait()
    levh, levl = split(lev_in[...])
    lev2 = jnp.concatenate(
        [jnp.concatenate([levh, levh], 1), jnp.concatenate([levl, jnp.zeros_like(levl)], 1)], 0
    )
    lats[...] = jnp.zeros_like(lats)
    lats[0:LATS, 0:RLAT] = lat_in[...]
    lat_pad = lats[...]
    lane = lax.broadcasted_iota(jnp.int32, (128, 128), 1)
    lat_hi, lat_lo = [], []
    for u in range(SLABS):
        tail = jnp.where(lane >= RLAT, pltpu.roll(lat_pad, 96 - 32 * u, 1), 0.0)
        hi, lo = split(jnp.concatenate([lat_pad, tail], 0))
        lat_hi.append(hi)
        lat_lo.append(lo)

    def levels(k):
        def one(i, carry):
            f = fv[pl.ds(pl.multiple_of(i * LATS, LATS), LATS), :]
            fh, fl = split(f)
            both = jnp.concatenate([fh, fl], 1)
            both = jnp.concatenate([both, jnp.zeros((128 - LATS, 256), BF16)], 0)
            r = lax.dot_general(lev2, both, (((1,), (1,)), ((), ())), preferred_element_type=F32)
            lvl[pl.ds(lax.rem(i, ROWS), RLEV, stride=ROWS), :] = r[:RLEV] + r[RLEV:]
            return carry

        loads[k].wait()
        at, rows = LOADS[k]
        lax.fori_loop(at, at + rows, one, 0, unroll=24)

    def latitudes(t, u):
        parts = [
            jnp.concatenate([lvl[pl.ds((4 * d + v) * ROWS, ROWS), :] for d in range(8)], 0) for v in (u, 3)
        ]
        hi, lo = split(jnp.concatenate(parts, 1))
        r = (
            jnp.dot(hi, lat_hi[u], preferred_element_type=F32)
            + jnp.dot(lo, lat_hi[u], preferred_element_type=F32)
            + jnp.dot(hi, lat_lo[u], preferred_element_type=F32)
        )
        for d in range(8):
            proj[2 * (t * SLABS + u) + d % 2, d // 2] = r[d * ROWS : (d + 1) * ROWS]

    for t in range(TIMES):
        for k in ((0, 1), (2,))[t]:
            levels(k)
        for u in range(SLABS):
            latitudes(t, u)
            if t + u == 0:
                pl.semaphore_wait(barrier, len(greeted))
                for peer in told:
                    pl.semaphore_signal(passed, inc=1, device_id=peer, device_id_type=MESH)
            for g, (first, count) in enumerate(GROUPS):
                if first // 2 == t * SLABS + u:
                    blocks = pl.ds(first, count)
                    for k in (1, 0, 2):
                        send(proj.at[blocks, (x + k + 1) % 4], xr.at[blocks, k], sent, xsem.at[g], x_peers[k])

    pl.semaphore_wait(passed, len(told))
    small[2].wait()
    old_t = split(old_in[...].T)
    acc = jnp.zeros((ROWS, RLON), F32)

    for at, kind, g in SCHEDULE:
        first, count = GROUPS[g]
        blocks = pl.ds(first, count)
        if kind == 0:
            arrived(xr.at[blocks], xsem.at[g])
            for b in range(first, first + count):
                pz[b] = proj[b, x] + xr[b, 0] + xr[b, 1] + xr[b, 2]
                wt[b] = dot3(old_t, split(pz[b]), ((1,), (0,)))
            for k in range(7):
                part = pl.ds(yc_parts[k], PART)
                send(wt.at[blocks, part], wr.at[blocks, k], sent, rsem.at[g], yc_peers[k])
        elif kind == 1:
            arrived(wr.at[blocks], rsem.at[g])
            for b in range(first, first + count):
                ws[b] = tree_sum([wr[b, k] for k in range(7)] + [wt[b, pl.ds(PART * me, PART)]])
            for k in FAR_FIRST:
                send(ws.at[blocks], wz.at[blocks, k], sent, zsem.at[g], z_peers[k])
        elif kind == 2:
            arrived(wz.at[blocks], zsem.at[g])
            for b in range(first, first + count):
                wf[b, pl.ds(PART * me, PART)] = tree_sum([wz[b, k] for k in range(7)] + [ws[b]])
            mine = wf.at[blocks, pl.ds(PART * me, PART)]
            for k in range(7):
                send(mine, mine, sent, xsem.at[g], yc_peers[k])
        else:
            arrived(wr.at[blocks], xsem.at[g])
            for b in range(first, first + count):
                acc = acc + dot3(split(pz[b]), split(wf[b]), ((1,), (1,)))
    img[...] = pack_image(jnp.concatenate([acc, jnp.zeros((ROWS, 128 - RLON), F32)], 1))
    for k in range(8):
        send(img, ir.at[k], sent, isem, i_peers[k])
    arrived(ir, isem)
    image = tree_sum([ir[k] for k in range(8)])
    image = unpack_image(image)
    summed[...] = image
    send(summed, home, sent, hsem, z_peers[1])
    gp[...] = pack_gram(
        lax.dot_general(image, image, (((0,), (0,)), ((), ())), precision=HIGHEST, preferred_element_type=F32)
    )
    half = RLON // 4
    sibling = device(x, z, y, 1 - core)
    mine, other = (pl.ds(pl.multiple_of(half * c, 8), half) for c in (1 - core, core))
    send(gp.at[other], gr, sent, gsem.at[0], sibling)
    arrived(gr, gsem.at[0])
    gh[...] = gp[mine] + gr[...]
    for k in range(15):
        send(gh, go.at[k], sent, gsem.at[1], g_peers[k])
    arrived(home, hsem)
    image_t = jnp.concatenate([home[...].T[0:RLON], jnp.zeros((RLON, 128 - ROWS), F32)], 1)
    arrived(go, gsem.at[1])
    gf[mine] = tree_sum([go[k] for k in range(15)] + [gh[...]])
    send(gf.at[mine], gf.at[mine], sent, gsem.at[2], sibling)

    @pl.when(core == 0)
    def _():
        arrived(gr, gsem.at[2])

    def rest():
        @pl.when(core == 1)
        def _():
            arrived(gr, gsem.at[2])

        return jnp.concatenate([unpack_top(gf[HEAD:]), unpack_low(gf[...])], 0)

    solve(total_rows, unpack_top(gf[0:HEAD]), rest, image_t, out, yt)

    refs = (xr, wr, wz, wr, ir, home, gr, go, gr)
    arrived(fv.at[pl.ds(0, sum(math.prod(ref.shape) // 128 for ref in refs))], sent)


def body(field, lat_factor, lev_factor, old_factor):
    vmem = pl.BlockSpec(memory_space=pltpu.VMEM)
    dma = pltpu.SemaphoreType.DMA
    field = field.reshape(TIMES * ROWS * LATS, LEVS)
    total_rows = ROWS * lax.axis_size("lon")
    return pl.pallas_call(
        functools.partial(hooi_kernel, total_rows),
        out_shape=pltpu.VMEM((ROWS, RLON), F32),
        in_specs=[pl.BlockSpec(memory_space=pltpu.HBM)] * 4,
        out_specs=vmem,
        scratch_shapes=[
            pltpu.VMEM((TIMES * ROWS * LATS, LEVS), F32),
            pltpu.VMEM((LATS, RLAT), F32),
            pltpu.VMEM((RLEV, LEVS), F32),
            pltpu.VMEM((ROWS, RLON), F32),
            pltpu.VMEM((128, 128), F32),
            pltpu.VMEM((RLEV * ROWS, 128), F32),
            pltpu.VMEM((BLOCKS, 4, ROWS, 128), F32),
            pltpu.VMEM((BLOCKS, 3, ROWS, 128), F32),
            pltpu.VMEM((BLOCKS, ROWS, 128), F32),
            pltpu.VMEM((BLOCKS, RLON, 128), F32),
            pltpu.VMEM((BLOCKS, 7, PART, 128), F32),
            pltpu.VMEM((BLOCKS, PART, 128), F32),
            pltpu.VMEM((BLOCKS, 7, PART, 128), F32),
            pltpu.VMEM((BLOCKS, RLON, 128), F32),
            pltpu.VMEM((IMAGE_ROWS, 128), F32),
            pltpu.VMEM((8, IMAGE_ROWS, 128), F32),
            pltpu.VMEM((ROWS, 128), F32),
            pltpu.VMEM((ROWS, 128), F32),
            pltpu.VMEM((RLON // 2, 128), F32),
            pltpu.VMEM((RLON // 4, 128), F32),
            pltpu.VMEM((RLON // 4, 128), F32),
            pltpu.VMEM((15, RLON // 4, 128), F32),
            pltpu.VMEM((RLON // 2, 128), F32),
            pltpu.VMEM((RLON, 128), F32),
            dma((3,)),
            dma((3,)),
            pltpu.SemaphoreType.REGULAR,
            dma,
            dma((len(GROUPS),)),
            dma((len(GROUPS),)),
            dma((len(GROUPS),)),
            dma,
            dma,
            dma((3,)),
        ],
        compiler_params=pltpu.CompilerParams(
            collective_id=0, has_side_effects=True, vmem_limit_bytes=48 * 1024 * 1024
        ),
    )(*(pltpu.with_memory_space_constraint(v, pltpu.HBM) for v in (field, lat_factor, lev_factor.T, old_factor)))


def solution(mesh):
    placed = (P(None, "lon", "lat", None), P("lat", None), P(), P("lon", None))
    return jax.shard_map(
        body, mesh=mesh, in_specs=placed, out_specs=P("lon", None), check_vma=False
    )
```
